32 devices in a mesh: batch: 8 (over z, x), seq: 4 (over y, core).
Axes of the slice: x: 2, y: 2, z: 4, core: 2. Of those that a mesh axis runs over, the one named last changes fastest.
Arguments:
- tokens: bfloat16 [24576, 768], P(('batch', 'seq')), may hold values from -6 to 6
- group_bucket: int32 [8], P('batch'), may hold values from 0 to 1, as said below
- lengths: int32 [8, 3], P('batch'), may hold values from 0 to 3072, as said below
- random_blocks: int32 [8, 48, 3], P('batch'), may hold values from 1 to 46, as said below
- w_qkv: bfloat16 [768, 2304], replicated, may hold values from -0.21875 to 0.21875
- w_out: bfloat16 [768, 768], replicated, may hold values from -1.25 to 1.25
- b_out: float32 [768], replicated, may hold values from -3 to 3
- norm1_gain: float32 [768], replicated, may hold values from 0.5 to 1.5
- norm1_shift: float32 [768], replicated, may hold values from -3 to 3
- w_in: bfloat16 [768, 3072], replicated, may hold values from -0.21875 to 0.21875
- b_in: float32 [3072], replicated, may hold values from -3 to 3
- w_back: bfloat16 [3072, 768], replicated, may hold values from -0.109375 to 0.109375
- b_back: float32 [768], replicated, may hold values from -3 to 3
- norm2_gain: float32 [768], replicated, may hold values from 0.5 to 1.5
- norm2_shift: float32 [768], replicated, may hold values from -3 to 3
- cotangent: bfloat16 [24576, 768], P(('batch', 'seq')), may hold values from -6 to 6
Outputs:
- layer_out: bfloat16 [24576, 768], P(('batch', 'seq'))
- grad_tokens: bfloat16 [24576, 768], P(('batch', 'seq'))
- grad_w_qkv: float32 [768, 2304], replicated
- grad_w_out: float32 [768, 768], replicated
- grad_b_out: float32 [768], replicated
- grad_norm1_gain: float32 [768], replicated
- grad_norm1_shift: float32 [768], replicated
- grad_w_in: float32 [768, 3072], replicated
- grad_b_in: float32 [3072], replicated
- grad_w_back: float32 [3072, 768], replicated
- grad_b_back: float32 [768], replicated
- grad_norm2_gain: float32 [768], replicated
- grad_norm2_shift: float32 [768], replicated
The draws below stay inside these ranges and needn't reach their ends.
Inputs may be any that keep to these rules, and one draw needn't show every extreme that they name: `group_bucket`: both buckets occur among the groups. `lengths`: in a group of bucket 0 every entry exceeds 3 * 256 and is at most 1024, and some such sequence has exactly 1024; in a group of bucket 1 entry 0 exceeds 3 * 768, the other entries are 0, and some such group has exactly 3072. `random_blocks`: each entry is a block of the query block's own sequence that starts below that sequence's length, is neither the query block nor next to it nor the sequence's first or last block; the three entries of a query block differ.
All inputs are finite; a program needn't handle non-finite values.
Results may differ from the reference program's by a relative error of at most 0.014.
Values may be sent and summed in bfloat16 or wider, within the bound.
A program may use at most 192 MiB of HBM per device.

```python
import jax
import jax.numpy as jnp
from jax import lax

D = 768
HEADS = 12
HEAD = 64
FF = 3072
BLOCK = 64
SHORT = 1024
GROUPS = 8
SEQ_LEN = 3072
TOKENS = 24576


def draw_layout(key):
    key = jax.random.fold_in(key, 5)
    flag_key, pick_key, other_key, short_key, long_key = jax.random.split(key, 5)
    seq_count = SEQ_LEN // SHORT
    group_ids = jnp.arange(GROUPS, dtype=jnp.int32)
    seq_slots = jnp.arange(seq_count, dtype=jnp.int32)
    long_group = jax.random.randint(pick_key, (), 0, GROUPS)
    short_group = (long_group + 1 + jax.random.randint(other_key, (), 0, GROUPS - 1)) % GROUPS
    drawn_flags = (jax.random.randint(flag_key, (GROUPS,), 0, 10) < 3).astype(jnp.int32)
    flags = jnp.where(group_ids == long_group, 1, jnp.where(group_ids == short_group, 0, drawn_flags)).astype(jnp.int32)
    short_lengths = jax.random.randint(short_key, (GROUPS, seq_count), 3 * SHORT // 4 + 1, SHORT + 1)
    short_lengths = jnp.where((group_ids[:, None] == short_group) & (seq_slots[None, :] == 0), SHORT, short_lengths)
    long_lengths = jax.random.randint(long_key, (GROUPS,), 3 * SEQ_LEN // 4 + 1, SEQ_LEN + 1)
    long_lengths = jnp.where(group_ids == long_group, SEQ_LEN, long_lengths)
    long_rows = jnp.where(seq_slots[None, :] == 0, long_lengths[:, None], 0)
    seq_lengths = jnp.where(flags[:, None] > 0, long_rows, short_lengths).astype(jnp.int32)
    return (flags, seq_lengths, long_group)


def draw_group_bucket(key, part):
    flags, seq_lengths, long_group = draw_layout(key)
    return flags.astype(jnp.int32)


def draw_lengths(key, part):
    flags, seq_lengths, long_group = draw_layout(key)
    return seq_lengths.astype(jnp.int32)


def draw_random_blocks(key, part):
    flags, seq_lengths, long_group = draw_layout(key)
    key = jax.random.fold_in(key, 31)
    nblocks = SEQ_LEN // BLOCK
    short_blocks = SHORT // BLOCK
    own_block = jnp.arange(nblocks, dtype=jnp.int32)
    is_long = flags[:, None] > 0
    member = jnp.where(is_long, 0, own_block[None, :] // short_blocks).astype(jnp.int32)
    start_block = jnp.where(is_long, 0, member * short_blocks).astype(jnp.int32)
    last_block = jnp.where(is_long, nblocks - 1, start_block + short_blocks - 1).astype(jnp.int32)
    seq_valid = jnp.take_along_axis(seq_lengths, member, axis=1)
    usable = (seq_valid + BLOCK - 1) // BLOCK
    candidate = own_block[None, None, :]
    usable_mask = (candidate >= start_block[:, :, None]) & (candidate < (start_block + usable)[:, :, None]) & (jnp.abs(candidate - own_block[None, :, None]) > 1) & (candidate != start_block[:, :, None]) & (candidate != last_block[:, :, None])
    noise = jax.random.randint(key, (GROUPS, nblocks, nblocks), 0, 1 << 20)
    scores = jnp.where(usable_mask, noise * nblocks + candidate + 1, 0)
    group_ids = jnp.arange(GROUPS, dtype=jnp.int32)[:, None, None]
    query_ids = own_block[None, :, None]
    forced = (group_ids == long_group) & ((query_ids == 1) & (candidate == nblocks - 2) | (query_ids == nblocks - 2) & (candidate == 1))
    scores = jnp.where(forced, (1 << 20) * nblocks + nblocks + 1, scores)
    chosen = lax.top_k(scores, 3)[1]
    return chosen.astype(jnp.int32)


def steps_of(rng, dims, cuts, least, high):
    def one(dim, parts):
        draws = jax.random.uniform(jax.random.fold_in(jax.random.fold_in(rng, 6), dim), (parts,), jnp.float32, least / len(cuts), high / len(cuts))
        return jnp.repeat(jnp.exp(draws), dims[dim] // parts).reshape((-1,) + (1,) * (len(dims) - dim - 1))

    factor_of = one(*cuts[0])
    for cut in cuts[1:]:
        factor_of = factor_of * one(*cut)
    return factor_of


def scatter_about(stream_key, shape, scale, most, cuts=(), kind=jnp.bfloat16):
    values = jax.random.normal(stream_key, shape, jnp.float32) * scale
    if len(cuts) > 0:
        values = steps_of(stream_key, shape, cuts, -0.22, 0.18) * values
    return jnp.clip(values, min=-most, max=most).astype(kind)


def setup_inputs(seed: int = 0) -> dict:
    key_list = jax.random.split(jax.random.key(seed), 17)
    tokens = scatter_about(key_list[0], (TOKENS, D), 1.0, 6.0, ((0, 32),))
    group_bucket = draw_group_bucket(jax.random.fold_in(key_list[16], 71), 0)
    lengths = draw_lengths(jax.random.fold_in(key_list[16], 71), 0)
    random_blocks = draw_random_blocks(jax.random.fold_in(key_list[16], 71), 0)
    w_qkv = scatter_about(key_list[4], (D, 3 * D), D ** -0.5, 0.21875)
    w_out = scatter_about(key_list[5], (D, D), (D // 32) ** -0.5, 1.25)
    b_out = scatter_about(key_list[6], (D,), 0.5, 3.0, (), jnp.float32)
    norm1_gain = jnp.clip(1.0 + 0.1 * jax.random.normal(key_list[7], (D,), jnp.float32), 0.5, 1.5)
    norm1_shift = scatter_about(key_list[8], (D,), 0.5, 3.0, (), jnp.float32)
    w_in = scatter_about(key_list[9], (D, FF), D ** -0.5, 0.21875)
    b_in = scatter_about(key_list[10], (FF,), 0.5, 3.0, (), jnp.float32)
    w_back = scatter_about(key_list[11], (FF, D), FF ** -0.5, 0.109375)
    b_back = scatter_about(key_list[12], (D,), 0.5, 3.0, (), jnp.float32)
    norm2_gain = jnp.clip(1.0 + 0.1 * jax.random.normal(key_list[13], (D,), jnp.float32), 0.5, 1.5)
    norm2_shift = scatter_about(key_list[14], (D,), 0.5, 3.0, (), jnp.float32)
    cotangent = scatter_about(key_list[15], (TOKENS, D), 1.0, 6.0, ((0, 32),))
    return dict(tokens=tokens, group_bucket=group_bucket, lengths=lengths, random_blocks=random_blocks, w_qkv=w_qkv, w_out=w_out, b_out=b_out, norm1_gain=norm1_gain, norm1_shift=norm1_shift, w_in=w_in, b_in=b_in, w_back=w_back, b_back=b_back, norm2_gain=norm2_gain, norm2_shift=norm2_shift, cotangent=cotangent)


@jax.custom_vjp
def low(v):
    return lax.optimization_barrier(v.astype(jnp.bfloat16)).astype(jnp.float32)

@jax.custom_vjp
def low_back(v):
    return v

def low_keep(v):
    return (low(v), None)

def low_pass(kept, grad):
    return (grad,)

def back_keep(v):
    return (v, None)

def back_low(kept, grad):
    return (low(grad),)
low.defvjp(low_keep, low_pass)
low_back.defvjp(back_keep, back_low)
highest = lax.Precision.HIGHEST
norm_eps = 1e-06
query_span = 8
listed_blocks = 8
masked_score = -1e+30

def sequence_layout(nblocks, short_blocks, group_flag, seq_lengths):
    own_block = jnp.arange(nblocks, dtype=jnp.int32)
    is_long = group_flag > 0
    member = jnp.where(is_long, 0, own_block // short_blocks).astype(jnp.int32)
    start_block = jnp.where(is_long, 0, member * short_blocks).astype(jnp.int32)
    span_blocks = jnp.where(is_long, nblocks, short_blocks).astype(jnp.int32)
    seq_slots = jnp.arange(seq_lengths.shape[0], dtype=jnp.int32)
    valid_len = lax.optimization_barrier(jnp.sum(jnp.where(member[:, None] == seq_slots[None, :], seq_lengths[None, :].astype(jnp.int32), 0), axis=1)).astype(jnp.int32)
    return (own_block, start_block, span_blocks, valid_len)

def block_keys(nblocks, short_blocks, block_rows, group_flag, seq_lengths, random_ids):
    own_block, start_block, span_blocks, valid_len = sequence_layout(nblocks, short_blocks, group_flag, seq_lengths)
    end_block = start_block + span_blocks
    window = jnp.stack([own_block - 1, own_block, own_block + 1], axis=1)
    edge_blocks = jnp.stack([start_block, end_block - 1], axis=1)
    listed = jnp.concatenate([window, random_ids.astype(jnp.int32), edge_blocks], axis=1)
    inside = (listed >= start_block[:, None]) & (listed < end_block[:, None])
    column = jnp.arange(listed_blocks, dtype=jnp.int32)
    repeated = (column[None, :] >= 6) & (jnp.abs(listed - own_block[:, None]) <= 1)
    inside = inside & jnp.logical_not(repeated)
    places = (listed - start_block[:, None])[:, :, None] * block_rows + jnp.arange(block_rows, dtype=jnp.int32)[None, None, :]
    allowed = inside[:, :, None] & (places < valid_len[:, None, None])
    return (jnp.clip(listed, 0, nblocks - 1), allowed.reshape(nblocks, listed_blocks * block_rows))

def global_layout(nblocks, short_blocks, block_rows, group_flag, seq_lengths):
    seq_count = seq_lengths.shape[0]
    seq_slots = jnp.arange(seq_count, dtype=jnp.int32)
    is_long = group_flag > 0
    first_block = jnp.where(is_long, 0, seq_slots * short_blocks).astype(jnp.int32)
    last_block = jnp.where(is_long, nblocks - 1, seq_slots * short_blocks + short_blocks - 1).astype(jnp.int32)
    seq_valid = jnp.where(is_long, seq_lengths[0], seq_lengths).astype(jnp.int32)
    keep_seq = jnp.where(is_long, seq_slots == 0, True)
    global_ids = jnp.stack([first_block, last_block], axis=1).reshape(2 * seq_count)
    global_keep = jnp.repeat(keep_seq, 2).astype(jnp.float32)
    positions = jnp.arange(nblocks * block_rows, dtype=jnp.int32)
    offsets = positions[None, :] - first_block[:, None] * block_rows
    open_seq = (offsets >= 0) & (positions[None, :] < (last_block[:, None] + 1) * block_rows) & (offsets < seq_valid[:, None])
    open_rows = jnp.repeat(jnp.repeat(open_seq, 2, axis=0), block_rows, axis=0)
    return (global_ids, global_keep, open_rows)

def layer_norm(values, norm_gain, norm_shift):
    centred = values - lax.optimization_barrier(jnp.mean(values, axis=-1, keepdims=True))
    spread_inv = lax.rsqrt(lax.optimization_barrier(jnp.mean(centred * centred, axis=-1, keepdims=True)) + norm_eps)
    return centred * spread_inv * norm_gain + norm_shift

def attend(queries, keys_all, values_all, group_flag, seq_lengths, random_ids):
    nblocks = SEQ_LEN // BLOCK
    short_blocks = SHORT // BLOCK
    seq_count = seq_lengths.shape[0]
    factor = HEAD ** (-0.5)
    query_blocks = queries.reshape(nblocks, BLOCK, HEADS, HEAD)
    key_blocks = keys_all.reshape(nblocks, BLOCK, HEADS, HEAD)
    value_blocks = values_all.reshape(nblocks, BLOCK, HEADS, HEAD)
    listed, allowed = block_keys(nblocks, short_blocks, BLOCK, group_flag, seq_lengths, random_ids)
    global_ids, global_keep, open_rows = global_layout(nblocks, short_blocks, BLOCK, group_flag, seq_lengths)
    span_count = nblocks // query_span

    def one_span(span_item):
        span_queries, span_listed, span_allowed = span_item
        gathered_keys = key_blocks[span_listed].reshape(query_span, listed_blocks * BLOCK, HEADS, HEAD)
        gathered_values = value_blocks[span_listed].reshape(query_span, listed_blocks * BLOCK, HEADS, HEAD)
        scores = jnp.einsum('bqhe,bkhe->bhqk', span_queries, gathered_keys, precision=highest) * factor
        scores = jnp.where(span_allowed[:, None, None, :], low_back(scores), masked_score)
        weights = low(jax.nn.softmax(scores, axis=-1))
        return jnp.einsum('bhqk,bkhe->bqhe', weights, gathered_values, precision=highest)
    sparse = lax.map(jax.checkpoint(one_span), (query_blocks.reshape(span_count, query_span, BLOCK, HEADS, HEAD), listed.reshape(span_count, query_span, listed_blocks), allowed.reshape(span_count, query_span, listed_blocks * BLOCK)))
    global_queries = query_blocks[global_ids].reshape(2 * seq_count * BLOCK, HEADS, HEAD)
    scores = jnp.einsum('qhe,khe->hqk', global_queries, keys_all, precision=highest) * factor
    scores = jnp.where(open_rows[None, :, :], low_back(scores), masked_score)
    weights = low(jax.nn.softmax(scores, axis=-1))
    global_out = jnp.einsum('hqk,khe->qhe', weights, values_all, precision=highest)
    global_out = global_out.reshape(2 * seq_count, BLOCK, HEADS, HEAD) * global_keep[:, None, None, None]
    placed = jnp.zeros((nblocks, BLOCK, HEADS, HEAD), jnp.float32).at[global_ids].add(global_out)
    own_block = jnp.arange(nblocks, dtype=jnp.int32)
    is_global = jnp.any(own_block[:, None] == global_ids[None, :], axis=1)
    mixed = jnp.where(is_global[:, None, None, None], placed, sparse.reshape(nblocks, BLOCK, HEADS, HEAD))
    return mixed.reshape(SEQ_LEN, HEADS, HEAD)

def group_forward(inputs, params, group_flag, seq_lengths, random_ids):
    w_qkv, w_out, b_out, norm1_gain, norm1_shift, w_in, b_in, w_back, b_back, norm2_gain, norm2_shift = params
    feat_width = inputs.shape[1]
    projected = low(low_back(jnp.dot(inputs, w_qkv, precision=highest)))
    split_parts = projected.reshape(SEQ_LEN, 3, HEADS, HEAD)
    attention = attend(split_parts[:, 0], split_parts[:, 1], split_parts[:, 2], group_flag, seq_lengths, random_ids)
    attended = low(low_back(attention)).reshape(SEQ_LEN, feat_width)
    branch = low_back(jnp.dot(attended, w_out, precision=highest) + b_out)
    hidden = layer_norm(inputs + branch, norm1_gain, norm1_shift)
    inner_pre = low_back(jnp.dot(low(hidden), w_in, precision=highest) + b_in)
    active = low(jax.nn.gelu(inner_pre, approximate=False))
    second = low_back(jnp.dot(active, w_back, precision=highest) + b_back)
    return layer_norm(hidden + second, norm2_gain, norm2_shift)

def reference(tokens, group_bucket, lengths, random_blocks, w_qkv, w_out, b_out, norm1_gain, norm1_shift, w_in, b_in, w_back, b_back, norm2_gain, norm2_shift, cotangent):
    feat_width = tokens.shape[1]
    inputs = tokens.astype(jnp.float32).reshape(GROUPS, SEQ_LEN, feat_width)
    params = tuple((weight.astype(jnp.float32) for weight in (w_qkv, w_out, b_out, norm1_gain, norm1_shift, w_in, b_in, w_back, b_back, norm2_gain, norm2_shift)))

    def forward(group_inputs, group_params):

        def one_group(group_item):
            group_rows, group_flag, seq_lengths, random_ids = group_item
            return group_forward(group_rows, group_params, group_flag, seq_lengths, random_ids)
        return lax.map(one_group, (group_inputs, group_bucket, lengths, random_blocks))
    outputs, pull_back = jax.vjp(forward, inputs, params)
    grad_inputs, grads = pull_back(cotangent.astype(jnp.float32).reshape(GROUPS, SEQ_LEN, feat_width))
    return (outputs.reshape(TOKENS, feat_width).astype(jnp.bfloat16), grad_inputs.reshape(TOKENS, feat_width).astype(jnp.bfloat16), grads[0], grads[1], grads[2], grads[3], grads[4], grads[5], grads[6], grads[7], grads[8], grads[9], grads[10])
```

```python
import functools
import jax
import jax.numpy as jnp
from jax import lax
from jax.sharding import PartitionSpec as P
from jax.experimental import pallas as pl
from jax.experimental.pallas import tpu as pltpu

HEADS = 12
HEAD = 64
BLOCK = 64
SHORT = 1024
LISTED = 8
QUAD = 4
WIDE = QUAD * HEAD
SPAN = LISTED * BLOCK
MASKED = -1e30
NORM_EPS = 1e-06
NT = (((1,), (1,)), ((), ()))
TN = (((0,), (0,)), ((), ()))


def dot(a, b, dims=(((1,), (0,)), ((), ()))):
    return lax.dot_general(a, b, dims, preferred_element_type=jnp.float32)


def stack_heads(rows, head_mask):
    return jnp.concatenate([rows] * QUAD, axis=0) * head_mask


def pick_heads(full, lane_head):
    out = full[0:BLOCK]
    for h in range(1, QUAD):
        out = jnp.where(lane_head == h, full[h * BLOCK : (h + 1) * BLOCK], out)
    return out


def masked_span(scores, row_id, limits):
    parts = []
    for j in range(LISTED):
        parts.append(
            jnp.where(row_id < limits[j], scores[j * BLOCK : (j + 1) * BLOCK], MASKED)
        )
    return jnp.concatenate(parts, axis=0)


def attend_kernel(
    blocks, ids_ref, lim_ref, glob_ref, q_ref, k_ref, v_ref, hm_ref, o_ref, l_ref, kcat, vcat, acc
):
    row_id = lax.broadcasted_iota(jnp.int32, (BLOCK, WIDE), 0)
    lane_head = lax.broadcasted_iota(jnp.int32, (BLOCK, WIDE), 1) // HEAD
    chunk_row = lax.broadcasted_iota(jnp.int32, (SPAN, WIDE), 0)

    def one_block(b, carry):
        rows = pl.ds(pl.multiple_of(b * BLOCK, BLOCK), BLOCK)
        qm = stack_heads(q_ref[rows, :], hm_ref[...])
        for j in range(LISTED):
            src = pl.ds(pl.multiple_of(ids_ref[b * LISTED + j] * BLOCK, BLOCK), BLOCK)
            kcat[j * BLOCK : (j + 1) * BLOCK, :] = k_ref[src, :]
            vcat[j * BLOCK : (j + 1) * BLOCK, :] = v_ref[src, :]
        limits = [lim_ref[b * LISTED + j] for j in range(LISTED)]
        scores = masked_span(dot(kcat[...], qm, NT), row_id, limits)
        top = jnp.max(scores, axis=0, keepdims=True)
        grown = jnp.exp(scores - top)
        total = jnp.sum(grown, axis=0, keepdims=True)
        weights = (grown * (1.0 / total)).astype(jnp.bfloat16)
        full = dot(weights, vcat[...], TN)
        o_ref[rows, :] = pick_heads(full, lane_head).astype(jnp.bfloat16)
        l_ref[0, pl.ds(b, 1), :] = top + jnp.log(total)
        return carry

    lax.fori_loop(0, blocks, one_block, 0, unroll=UNROLL_F)

    def one_global(b, carry):
        @pl.when(glob_ref[b * 4] > 0)
        def _():
            rows = pl.ds(pl.multiple_of(b * BLOCK, BLOCK), BLOCK)
            qm = stack_heads(q_ref[rows, :], hm_ref[...])
            first = glob_ref[b * 4 + 1]
            valid = glob_ref[b * 4 + 3]
            acc[...] = jnp.zeros_like(acc)

            def one_chunk(c, state):
                top, total = state
                src = pl.ds(pl.multiple_of(first + c * SPAN, BLOCK), SPAN)
                scores = dot(k_ref[src, :], qm, NT)
                scores = jnp.where(chunk_row < valid - c * SPAN, scores, MASKED)
                newer = jnp.maximum(top, jnp.max(scores, axis=0, keepdims=True))
                shrink = jnp.exp(top - newer)
                grown = jnp.exp(scores - newer)
                acc[...] = acc[...] * shrink + dot(v_ref[src, :], grown.astype(jnp.bfloat16), TN)
                return (newer, total * shrink + jnp.sum(grown, axis=0, keepdims=True))

            top, total = lax.fori_loop(
                0,
                glob_ref[b * 4 + 2],
                one_chunk,
                (jnp.full((1, WIDE), MASKED, jnp.float32), jnp.zeros((1, WIDE), jnp.float32)),
            )
            full = (acc[...] * (1.0 / total)).T
            o_ref[rows, :] = pick_heads(full, lane_head).astype(jnp.bfloat16)
            l_ref[0, pl.ds(b, 1), :] = top + jnp.log(total)

        return carry

    lax.fori_loop(0, blocks, one_global, 0)

UNROLL_F = 2
UNROLL_B = 2

def smem():
    return pl.BlockSpec(memory_space=pltpu.SMEM)


def attend(ids, limits, glob, queries, kv, head_mask):
    rows, feat = queries.shape
    keys = kv.shape[0]
    quads = feat // WIDE
    blocks = rows // BLOCK
    pad_blocks = -(-blocks // 8) * 8
    return pl.pallas_call(
        functools.partial(attend_kernel, blocks),
        grid=(quads,),
        out_shape=(
            jax.ShapeDtypeStruct((rows, feat), jnp.bfloat16),
            jax.ShapeDtypeStruct((quads, pad_blocks, WIDE), jnp.float32),
        ),
        in_specs=[
            smem(),
            smem(),
            smem(),
            pl.BlockSpec((rows, WIDE), lambda i: (0, i)),
            pl.BlockSpec((keys, WIDE), lambda i: (0, i)),
            pl.BlockSpec((keys, WIDE), lambda i: (0, i + quads)),
            pl.BlockSpec((WIDE, WIDE), lambda i: (0, 0)),
        ],
        out_specs=[
            pl.BlockSpec((rows, WIDE), lambda i: (0, i)),
            pl.BlockSpec((1, pad_blocks, WIDE), lambda i: (i, 0, 0)),
        ],
        scratch_shapes=[
            pltpu.VMEM((SPAN, WIDE), jnp.bfloat16),
            pltpu.VMEM((SPAN, WIDE), jnp.bfloat16),
            pltpu.VMEM((WIDE, WIDE), jnp.float32),
        ],
        compiler_params=pltpu.CompilerParams(vmem_limit_bytes=56 * 2**20),
        name="attend",
    )(ids, limits, glob, queries, kv, kv, head_mask)


def attend_back_kernel(
    blocks, ids_ref, lim_ref, glob_ref, q_ref, k_ref, v_ref, g_ref, o_ref, l_ref, hm_ref,
    dq_ref, dk_ref, dv_ref, kcat, vcat, dk_sum, dv_sum, acc,
):
    row_id = lax.broadcasted_iota(jnp.int32, (BLOCK, WIDE), 0)
    lane_head = lax.broadcasted_iota(jnp.int32, (BLOCK, WIDE), 1) // HEAD
    chunk_row = lax.broadcasted_iota(jnp.int32, (SPAN, WIDE), 0)
    dk_sum[...] = jnp.zeros_like(dk_sum)
    dv_sum[...] = jnp.zeros_like(dv_sum)
    factor = HEAD ** (-0.5)

    def one_block(b, carry):
        rows = pl.ds(pl.multiple_of(b * BLOCK, BLOCK), BLOCK)
        keep = jnp.where(glob_ref[b * 4] > 0, 0.0, 1.0).astype(jnp.bfloat16)
        qm = stack_heads(q_ref[rows, :], hm_ref[...])
        gm = stack_heads(g_ref[rows, :] * keep, hm_ref[...])
        starts = [pl.multiple_of(ids_ref[b * LISTED + j] * BLOCK, BLOCK) for j in range(LISTED)]
        for j in range(LISTED):
            kcat[j * BLOCK : (j + 1) * BLOCK, :] = k_ref[pl.ds(starts[j], BLOCK), :]
            vcat[j * BLOCK : (j + 1) * BLOCK, :] = v_ref[pl.ds(starts[j], BLOCK), :]
        limits = [lim_ref[b * LISTED + j] for j in range(LISTED)]
        scores = masked_span(dot(kcat[...], qm, NT), row_id, limits)
        chance = jnp.exp(scores - l_ref[0, pl.ds(b, 1), :])
        grad_w = dot(vcat[...], gm, NT)
        mean = jnp.sum(chance * grad_w, axis=0, keepdims=True)
        grad_s = (chance * (grad_w - mean)).astype(jnp.bfloat16)
        dk_part = dot(grad_s, qm)
        dv_part = dot(chance.astype(jnp.bfloat16), gm)
        for j in range(LISTED):
            dst = pl.ds(starts[j], BLOCK)
            dk_sum[dst, :] += dk_part[j * BLOCK : (j + 1) * BLOCK]
            dv_sum[dst, :] += dv_part[j * BLOCK : (j + 1) * BLOCK]
        full = dot(grad_s, kcat[...], TN)
        dq_ref[rows, :] = (pick_heads(full, lane_head) * factor).astype(jnp.bfloat16)
        return carry

    lax.fori_loop(0, blocks, one_block, 0, unroll=UNROLL_B)

    def one_global(b, carry):
        @pl.when(glob_ref[b * 4] > 0)
        def _():
            rows = pl.ds(pl.multiple_of(b * BLOCK, BLOCK), BLOCK)
            qm = stack_heads(q_ref[rows, :], hm_ref[...])
            gm = stack_heads(g_ref[rows, :], hm_ref[...])
            first = glob_ref[b * 4 + 1]
            valid = glob_ref[b * 4 + 3]
            log_total = l_ref[0, pl.ds(b, 1), :]
            both = (g_ref[rows, :].astype(jnp.float32) * o_ref[rows, :].astype(jnp.float32)).T
            mean = jnp.concatenate(
                [
                    jnp.sum(both[h * HEAD : (h + 1) * HEAD], axis=0, keepdims=True)
                    for h in range(QUAD)
                ],
                axis=1,
            )
            acc[...] = jnp.zeros_like(acc)

            def one_chunk(c, carry):
                src = pl.ds(pl.multiple_of(first + c * SPAN, BLOCK), SPAN)
                scores = dot(k_ref[src, :], qm, NT)
                scores = jnp.where(chunk_row < valid - c * SPAN, scores, MASKED)
                chance = jnp.exp(scores - log_total)
                grad_w = dot(v_ref[src, :], gm, NT)
                grad_s = (chance * (grad_w - mean)).astype(jnp.bfloat16)
                dk_sum[src, :] += dot(grad_s, qm)
                dv_sum[src, :] += dot(chance.astype(jnp.bfloat16), gm)
                acc[...] += dot(grad_s, k_ref[src, :], TN)
                return carry

            lax.fori_loop(0, glob_ref[b * 4 + 2], one_chunk, 0)
            dq_ref[rows, :] = (pick_heads(acc[...], lane_head) * factor).astype(jnp.bfloat16)

        return carry

    lax.fori_loop(0, blocks, one_global, 0)
    dk_ref[...] = dk_sum[...].astype(jnp.bfloat16)
    dv_ref[...] = dv_sum[...].astype(jnp.bfloat16)


def attend_back(ids, limits, glob, queries, kv, grads, mixed, logs, head_mask):
    rows, feat = queries.shape
    keys = kv.shape[0]
    quads = feat // WIDE
    blocks = rows // BLOCK
    pad_blocks = logs.shape[1]
    row_spec = pl.BlockSpec((rows, WIDE), lambda i: (0, i))
    key_spec = pl.BlockSpec((keys, WIDE), lambda i: (0, i))
    return pl.pallas_call(
        functools.partial(attend_back_kernel, blocks),
        grid=(quads,),
        out_shape=(
            jax.ShapeDtypeStruct((rows, feat), jnp.bfloat16),
            jax.ShapeDtypeStruct((keys, feat), jnp.bfloat16),
            jax.ShapeDtypeStruct((keys, feat), jnp.bfloat16),
        ),
        in_specs=[
            smem(),
            smem(),
            smem(),
            row_spec,
            key_spec,
            pl.BlockSpec((keys, WIDE), lambda i: (0, i + quads)),
            row_spec,
            row_spec,
            pl.BlockSpec((1, pad_blocks, WIDE), lambda i: (i, 0, 0)),
            pl.BlockSpec((WIDE, WIDE), lambda i: (0, 0)),
        ],
        out_specs=[row_spec, key_spec, key_spec],
        scratch_shapes=[
            pltpu.VMEM((SPAN, WIDE), jnp.bfloat16),
            pltpu.VMEM((SPAN, WIDE), jnp.bfloat16),
            pltpu.VMEM((keys, WIDE), jnp.float32),
            pltpu.VMEM((keys, WIDE), jnp.float32),
            pltpu.VMEM((WIDE, WIDE), jnp.float32),
        ],
        compiler_params=pltpu.CompilerParams(vmem_limit_bytes=56 * 2**20),
        name="attend_back",
    )(ids, limits, glob, queries, kv, kv, grads, mixed, logs, head_mask)


def attention_tables(part, blocks, nblocks, group_flag, seq_lengths, random_ids):
    short_blocks = SHORT // BLOCK
    own = part * blocks + jnp.arange(blocks, dtype=jnp.int32)
    is_long = group_flag > 0
    member = jnp.where(is_long, 0, own // short_blocks)
    first = jnp.where(is_long, 0, member * short_blocks)
    span = jnp.where(is_long, nblocks, short_blocks)
    slots = jnp.arange(seq_lengths.shape[0], dtype=jnp.int32)
    valid = jnp.sum(jnp.where(member[:, None] == slots[None, :], seq_lengths[None, :], 0), axis=1)
    last = first + span - 1
    own_random = lax.dynamic_slice_in_dim(random_ids, part * blocks, blocks, 0)
    listed = jnp.concatenate(
        [jnp.stack([own - 1, own, own + 1], axis=1), own_random, jnp.stack([first, last], axis=1)],
        axis=1,
    )
    inside = (listed >= first[:, None]) & (listed <= last[:, None])
    column = jnp.arange(LISTED, dtype=jnp.int32)
    repeated = (column[None, :] >= 6) & (jnp.abs(listed - own[:, None]) <= 1)
    limits = valid[:, None] - (listed - first[:, None]) * BLOCK
    limits = jnp.where(inside & jnp.logical_not(repeated), limits, 0)
    ids = jnp.clip(listed, 0, nblocks - 1)
    is_edge = ((own == first) | (own == last)).astype(jnp.int32)
    chunks = jnp.broadcast_to(span * BLOCK // SPAN, own.shape)
    glob = jnp.stack([is_edge, first * BLOCK, chunks, valid], axis=1).astype(jnp.int32)
    return ids.reshape(-1), limits.astype(jnp.int32).reshape(-1), glob.reshape(-1)


def head_stack_mask():
    r = lax.broadcasted_iota(jnp.int32, (WIDE, WIDE), 0) // HEAD
    c = lax.broadcasted_iota(jnp.int32, (WIDE, WIDE), 1) // HEAD
    return (r == c).astype(jnp.bfloat16)


def plain_dot(left, right):
    return dot(left, right)


def left_dot(left, right):
    return dot(left, right, TN)


def right_dot(left, right):
    return dot(left, right, NT)


def normalize(values, norm_gain, norm_shift):
    centred = values - jnp.mean(values, axis=-1, keepdims=True)
    spread_inv = lax.rsqrt(jnp.mean(centred * centred, axis=-1, keepdims=True) + NORM_EPS)
    unit_value = centred * spread_inv
    return (unit_value * norm_gain + norm_shift, unit_value, spread_inv)


def normalize_back(grad_values, unit_value, spread_inv, norm_gain):
    scaled = grad_values * norm_gain
    centred = (
        scaled
        - jnp.mean(scaled, axis=-1, keepdims=True)
        - unit_value * jnp.mean(scaled * unit_value, axis=-1, keepdims=True)
    )
    return (
        spread_inv * centred,
        jnp.sum(grad_values * unit_value, axis=0),
        jnp.sum(grad_values, axis=0),
    )


def per_device(
    tokens,
    group_bucket,
    lengths,
    random_blocks,
    w_qkv,
    w_out,
    b_out,
    norm1_gain,
    norm1_shift,
    w_in,
    b_in,
    w_back,
    b_back,
    norm2_gain,
    norm2_shift,
    cotangent,
):
    low = jnp.bfloat16
    seq_parts = lax.axis_size("seq")
    part = lax.axis_index("seq")
    tok_rows, feat = tokens.shape
    blocks = tok_rows // BLOCK
    nblocks = blocks * seq_parts
    tables = attention_tables(
        part, blocks, nblocks, group_bucket[0], lengths[0], random_blocks[0]
    )
    head_mask = head_stack_mask()
    w_q, w_kv = w_qkv[:, :feat], w_qkv[:, feat:]
    inputs = tokens.astype(jnp.float32)
    group_tokens = lax.all_gather(tokens, "seq", axis=0, tiled=True)
    queries = plain_dot(tokens, w_q).astype(low) * low(HEAD ** (-0.5))
    kv = plain_dot(group_tokens, w_kv).astype(low)
    mixed, logs = attend(*tables, queries, kv, head_mask)

    branch = plain_dot(mixed, w_out) + b_out
    hidden, unit_first, spread_first = normalize(inputs + branch, norm1_gain, norm1_shift)
    hidden_low = hidden.astype(low)
    inner_pre = plain_dot(hidden_low, w_in) + b_in
    active, gelu_pull = jax.vjp(lambda value: jax.nn.gelu(value, approximate=False), inner_pre)
    active_low = active.astype(low)
    second = plain_dot(active_low, w_back) + b_back
    layer_out, unit_second, spread_second = normalize(hidden + second, norm2_gain, norm2_shift)
    grad_pre2, grad_gain2, grad_shift2 = normalize_back(
        cotangent.astype(jnp.float32), unit_second, spread_second, norm2_gain
    )
    grad_second = grad_pre2.astype(low)
    grad_w_back = left_dot(active_low, grad_second)
    grad_b_back = jnp.sum(grad_second.astype(jnp.float32), axis=0)
    grad_inner = gelu_pull(right_dot(grad_second, w_back))[0].astype(low)
    grad_w_in = left_dot(hidden_low, grad_inner)
    grad_b_in = jnp.sum(grad_inner.astype(jnp.float32), axis=0)
    grad_hidden = grad_pre2 + right_dot(grad_inner, w_in)
    grad_pre1, grad_gain1, grad_shift1 = normalize_back(
        grad_hidden, unit_first, spread_first, norm1_gain
    )
    grad_branch = grad_pre1.astype(low)
    grad_w_out = left_dot(mixed, grad_branch)
    grad_b_out = jnp.sum(grad_branch.astype(jnp.float32), axis=0)
    grad_mixed = right_dot(grad_branch, w_out).astype(low)

    both = ("batch", "seq")
    early = lax.psum((grad_w_in.astype(low), grad_w_back.astype(low), grad_w_out.astype(low)), both)
    dq, dk, dv = attend_back(*tables, queries, kv, grad_mixed, mixed, logs, head_mask)
    w_k, w_v = w_kv[:, :feat], w_kv[:, feat:]
    partial = (right_dot(dk, w_k) + right_dot(dv, w_v)).astype(low)
    summed_part = lax.psum_scatter(partial, "seq", scatter_dimension=0, tiled=True)
    grad_tokens = (
        grad_pre1 + right_dot(dq, w_q) + summed_part.astype(jnp.float32)
    ).astype(low)
    grad_w_qkv = jnp.concatenate(
        [left_dot(tokens, dq), left_dot(group_tokens, dk), left_dot(group_tokens, dv)], axis=1
    ).astype(low)
    late = lax.psum(grad_w_qkv, both)
    small = lax.psum(
        (
            grad_b_out,
            grad_gain1,
            grad_shift1,
            grad_b_in,
            grad_b_back,
            grad_gain2,
            grad_shift2,
        ),
        both,
    )
    wide = jnp.float32
    return (
        layer_out.astype(low),
        grad_tokens,
        late.astype(wide),
        early[2].astype(wide),
        small[0],
        small[1],
        small[2],
        early[0].astype(wide),
        small[3],
        early[1].astype(wide),
        small[4],
        small[5],
        small[6],
    )


def solution(mesh):
    rows = P(("batch", "seq"), None)
    whole = P()
    placed = (rows, P("batch"), P("batch", None), P("batch", None, None)) + (whole,) * 11 + (rows,)
    return jax.shard_map(
        per_device,
        mesh=mesh,
        in_specs=placed,
        out_specs=(rows, rows) + (whole,) * 11,
        check_vma=False,
    )
```

```python
import functools
import jax
import jax.numpy as jnp
from jax import lax
from jax.sharding import PartitionSpec as P
from jax.experimental import pallas as pl
from jax.experimental.pallas import tpu as pltpu

HEADS = 12
HEAD = 64
BLOCK = 64
SHORT = 1024
LISTED = 8
QUAD = 4
WIDE = QUAD * HEAD
SPAN = LISTED * BLOCK
MASKED = -1e30
NORM_EPS = 1e-06
NT = (((1,), (1,)), ((), ()))
TN = (((0,), (0,)), ((), ()))


def dot(a, b, dims=(((1,), (0,)), ((), ()))):
    return lax.dot_general(a, b, dims, preferred_element_type=jnp.float32)


def stack_heads(rows, head_mask):
    return jnp.concatenate([rows] * QUAD, axis=0) * head_mask


def pick_heads(full, lane_head):
    out = full[0:BLOCK]
    for h in range(1, QUAD):
        out = jnp.where(lane_head == h, full[h * BLOCK : (h + 1) * BLOCK], out)
    return out


def masked_span(scores, row_id, limits):
    parts = []
    for j in range(LISTED):
        parts.append(
            jnp.where(row_id < limits[j], scores[j * BLOCK : (j + 1) * BLOCK], MASKED)
        )
    return jnp.concatenate(parts, axis=0)


def attend_kernel(
    blocks, ids_ref, lim_ref, glob_ref, q_ref, k_ref, v_ref, hm_ref, o_ref, l_ref, kcat, vcat, acc
):
    row_id = lax.broadcasted_iota(jnp.int32, (BLOCK, WIDE), 0)
    lane_head = lax.broadcasted_iota(jnp.int32, (BLOCK, WIDE), 1) // HEAD
    chunk_row = lax.broadcasted_iota(jnp.int32, (SPAN, WIDE), 0)

    def one_block(b, carry):
        rows = pl.ds(pl.multiple_of(b * BLOCK, BLOCK), BLOCK)
        qm = stack_heads(q_ref[rows, :], hm_ref[...])
        for j in range(LISTED):
            src = pl.ds(pl.multiple_of(ids_ref[b * LISTED + j] * BLOCK, BLOCK), BLOCK)
            kcat[j * BLOCK : (j + 1) * BLOCK, :] = k_ref[src, :]
            vcat[j * BLOCK : (j + 1) * BLOCK, :] = v_ref[src, :]
        limits = [lim_ref[b * LISTED + j] for j in range(LISTED)]
        scores = masked_span(dot(kcat[...], qm, NT), row_id, limits)
        top = jnp.max(scores, axis=0, keepdims=True)
        grown = jnp.exp(scores - top)
        total = jnp.sum(grown, axis=0, keepdims=True)
        weights = (grown * (1.0 / total)).astype(jnp.bfloat16)
        full = dot(weights, vcat[...], TN)
        o_ref[rows, :] = pick_heads(full, lane_head).astype(jnp.bfloat16)
        l_ref[0, pl.ds(b, 1), :] = top + jnp.log(total)
        return carry

    lax.fori_loop(0, blocks, one_block, 0, unroll=UNROLL_F)

    def one_global(b, carry):
        @pl.when(glob_ref[b * 4] > 0)
        def _():
            rows = pl.ds(pl.multiple_of(b * BLOCK, BLOCK), BLOCK)
            qm = stack_heads(q_ref[rows, :], hm_ref[...])
            first = glob_ref[b * 4 + 1]
            valid = glob_ref[b * 4 + 3]
            acc[...] = jnp.zeros_like(acc)

            def one_chunk(c, state):
                top, total = state
                src = pl.ds(pl.multiple_of(first + c * SPAN, BLOCK), SPAN)
                scores = dot(k_ref[src, :], qm, NT)
                scores = jnp.where(chunk_row < valid - c * SPAN, scores, MASKED)
                newer = jnp.maximum(top, jnp.max(scores, axis=0, keepdims=True))
                shrink = jnp.exp(top - newer)
                grown = jnp.exp(scores - newer)
                acc[...] = acc[...] * shrink + dot(v_ref[src, :], grown.astype(jnp.bfloat16), TN)
                return (newer, total * shrink + jnp.sum(grown, axis=0, keepdims=True))

            top, total = lax.fori_loop(
                0,
                glob_ref[b * 4 + 2],
                one_chunk,
                (jnp.full((1, WIDE), MASKED, jnp.float32), jnp.zeros((1, WIDE), jnp.float32)),
            )
            full = (acc[...] * (1.0 / total)).T
            o_ref[rows, :] = pick_heads(full, lane_head).astype(jnp.bfloat16)
            l_ref[0, pl.ds(b, 1), :] = top + jnp.log(total)

        return carry

    lax.fori_loop(0, blocks, one_global, 0)

UNROLL_F = 2
UNROLL_B = 2

def smem():
    return pl.BlockSpec(memory_space=pltpu.SMEM)


def attend(ids, limits, glob, queries, kv, head_mask):
    rows, feat = queries.shape
    keys = kv.shape[0]
    quads = feat // WIDE
    blocks = rows // BLOCK
    pad_blocks = -(-blocks // 8) * 8
    return pl.pallas_call(
        functools.partial(attend_kernel, blocks),
        grid=(quads,),
        out_shape=(
            jax.ShapeDtypeStruct((rows, feat), jnp.bfloat16),
            jax.ShapeDtypeStruct((quads, pad_blocks, WIDE), jnp.float32),
        ),
        in_specs=[
            smem(),
            smem(),
            smem(),
            pl.BlockSpec((rows, WIDE), lambda i: (0, i)),
            pl.BlockSpec((keys, WIDE), lambda i: (0, i)),
            pl.BlockSpec((keys, WIDE), lambda i: (0, i + quads)),
            pl.BlockSpec((WIDE, WIDE), lambda i: (0, 0)),
        ],
        out_specs=[
            pl.BlockSpec((rows, WIDE), lambda i: (0, i)),
            pl.BlockSpec((1, pad_blocks, WIDE), lambda i: (i, 0, 0)),
        ],
        scratch_shapes=[
            pltpu.VMEM((SPAN, WIDE), jnp.bfloat16),
            pltpu.VMEM((SPAN, WIDE), jnp.bfloat16),
            pltpu.VMEM((WIDE, WIDE), jnp.float32),
        ],
        compiler_params=pltpu.CompilerParams(vmem_limit_bytes=56 * 2**20),
        name="attend",
    )(ids, limits, glob, queries, kv, kv, head_mask)


def attend_back_kernel(
    blocks, ids_ref, lim_ref, glob_ref, q_ref, k_ref, v_ref, g_ref, o_ref, l_ref, hm_ref,
    dq_ref, dk_ref, dv_ref, kcat, vcat, dk_sum, dv_sum, acc,
):
    row_id = lax.broadcasted_iota(jnp.int32, (BLOCK, WIDE), 0)
    lane_head = lax.broadcasted_iota(jnp.int32, (BLOCK, WIDE), 1) // HEAD
    chunk_row = lax.broadcasted_iota(jnp.int32, (SPAN, WIDE), 0)
    dk_sum[...] = jnp.zeros_like(dk_sum)
    dv_sum[...] = jnp.zeros_like(dv_sum)
    factor = HEAD ** (-0.5)

    def one_block(b, carry):
        rows = pl.ds(pl.multiple_of(b * BLOCK, BLOCK), BLOCK)
        keep = jnp.where(glob_ref[b * 4] > 0, 0.0, 1.0).astype(jnp.bfloat16)
        qm = stack_heads(q_ref[rows, :], hm_ref[...])
        gm = stack_heads(g_ref[rows, :] * keep, hm_ref[...])
        starts = [pl.multiple_of(ids_ref[b * LISTED + j] * BLOCK, BLOCK) for j in range(LISTED)]
        for j in range(LISTED):
            kcat[j * BLOCK : (j + 1) * BLOCK, :] = k_ref[pl.ds(starts[j], BLOCK), :]
            vcat[j * BLOCK : (j + 1) * BLOCK, :] = v_ref[pl.ds(starts[j], BLOCK), :]
        limits = [lim_ref[b * LISTED + j] for j in range(LISTED)]
        scores = masked_span(dot(kcat[...], qm, NT), row_id, limits)
        chance = jnp.exp(scores - l_ref[0, pl.ds(b, 1), :])
        grad_w = dot(vcat[...], gm, NT)
        mean = jnp.sum(chance * grad_w, axis=0, keepdims=True)
        grad_s = (chance * (grad_w - mean)).astype(jnp.bfloat16)
        dk_part = dot(grad_s, qm)
        dv_part = dot(chance.astype(jnp.bfloat16), gm)
        for j in range(LISTED):
            dst = pl.ds(starts[j], BLOCK)
            dk_sum[dst, :] += dk_part[j * BLOCK : (j + 1) * BLOCK]
            dv_sum[dst, :] += dv_part[j * BLOCK : (j + 1) * BLOCK]
        full = dot(grad_s, kcat[...], TN)
        dq_ref[rows, :] = (pick_heads(full, lane_head) * factor).astype(jnp.bfloat16)
        return carry

    lax.fori_loop(0, blocks, one_block, 0, unroll=UNROLL_B)

    def one_global(b, carry):
        @pl.when(glob_ref[b * 4] > 0)
        def _():
            rows = pl.ds(pl.multiple_of(b * BLOCK, BLOCK), BLOCK)
            qm = stack_heads(q_ref[rows, :], hm_ref[...])
            gm = stack_heads(g_ref[rows, :], hm_ref[...])
            first = glob_ref[b * 4 + 1]
            valid = glob_ref[b * 4 + 3]
            log_total = l_ref[0, pl.ds(b, 1), :]
            both = (g_ref[rows, :].astype(jnp.float32) * o_ref[rows, :].astype(jnp.float32)).T
            mean = jnp.concatenate(
                [
                    jnp.sum(both[h * HEAD : (h + 1) * HEAD], axis=0, keepdims=True)
                    for h in range(QUAD)
                ],
                axis=1,
            )
            acc[...] = jnp.zeros_like(acc)

            def one_chunk(c, carry):
                src = pl.ds(pl.multiple_of(first + c * SPAN, BLOCK), SPAN)
                scores = dot(k_ref[src, :], qm, NT)
                scores = jnp.where(chunk_row < valid - c * SPAN, scores, MASKED)
                chance = jnp.exp(scores - log_total)
                grad_w = dot(v_ref[src, :], gm, NT)
                grad_s = (chance * (grad_w - mean)).astype(jnp.bfloat16)
                dk_sum[src, :] += dot(grad_s, qm)
                dv_sum[src, :] += dot(chance.astype(jnp.bfloat16), gm)
                acc[...] += dot(grad_s, k_ref[src, :], TN)
                return carry

            lax.fori_loop(0, glob_ref[b * 4 + 2], one_chunk, 0)
            dq_ref[rows, :] = (pick_heads(acc[...], lane_head) * factor).astype(jnp.bfloat16)

        return carry

    lax.fori_loop(0, blocks, one_global, 0)
    dk_ref[...] = dk_sum[...].astype(jnp.bfloat16)
    dv_ref[...] = dv_sum[...].astype(jnp.bfloat16)


def attend_back(ids, limits, glob, queries, kv, grads, mixed, logs, head_mask):
    rows, feat = queries.shape
    keys = kv.shape[0]
    quads = feat // WIDE
    blocks = rows // BLOCK
    pad_blocks = logs.shape[1]
    row_spec = pl.BlockSpec((rows, WIDE), lambda i: (0, i))
    key_spec = pl.BlockSpec((keys, WIDE), lambda i: (0, i))
    return pl.pallas_call(
        functools.partial(attend_back_kernel, blocks),
        grid=(quads,),
        out_shape=(
            jax.ShapeDtypeStruct((rows, feat), jnp.bfloat16),
            jax.ShapeDtypeStruct((keys, feat), jnp.bfloat16),
            jax.ShapeDtypeStruct((keys, feat), jnp.bfloat16),
        ),
        in_specs=[
            smem(),
            smem(),
            smem(),
            row_spec,
            key_spec,
            pl.BlockSpec((keys, WIDE), lambda i: (0, i + quads)),
            row_spec,
            row_spec,
            pl.BlockSpec((1, pad_blocks, WIDE), lambda i: (i, 0, 0)),
            pl.BlockSpec((WIDE, WIDE), lambda i: (0, 0)),
        ],
        out_specs=[row_spec, key_spec, key_spec],
        scratch_shapes=[
            pltpu.VMEM((SPAN, WIDE), jnp.bfloat16),
            pltpu.VMEM((SPAN, WIDE), jnp.bfloat16),
            pltpu.VMEM((keys, WIDE), jnp.float32),
            pltpu.VMEM((keys, WIDE), jnp.float32),
            pltpu.VMEM((WIDE, WIDE), jnp.float32),
        ],
        compiler_params=pltpu.CompilerParams(vmem_limit_bytes=56 * 2**20),
        name="attend_back",
    )(ids, limits, glob, queries, kv, kv, grads, mixed, logs, head_mask)


def attention_tables(part, blocks, nblocks, group_flag, seq_lengths, random_ids):
    short_blocks = SHORT // BLOCK
    own = part * blocks + jnp.arange(blocks, dtype=jnp.int32)
    is_long = group_flag > 0
    member = jnp.where(is_long, 0, own // short_blocks)
    first = jnp.where(is_long, 0, member * short_blocks)
    span = jnp.where(is_long, nblocks, short_blocks)
    slots = jnp.arange(seq_lengths.shape[0], dtype=jnp.int32)
    valid = jnp.sum(jnp.where(member[:, None] == slots[None, :], seq_lengths[None, :], 0), axis=1)
    last = first + span - 1
    own_random = lax.dynamic_slice_in_dim(random_ids, part * blocks, blocks, 0)
    listed = jnp.concatenate(
        [jnp.stack([own - 1, own, own + 1], axis=1), own_random, jnp.stack([first, last], axis=1)],
        axis=1,
    )
    inside = (listed >= first[:, None]) & (listed <= last[:, None])
    column = jnp.arange(LISTED, dtype=jnp.int32)
    repeated = (column[None, :] >= 6) & (jnp.abs(listed - own[:, None]) <= 1)
    limits = valid[:, None] - (listed - first[:, None]) * BLOCK
    limits = jnp.where(inside & jnp.logical_not(repeated), limits, 0)
    ids = jnp.clip(listed, 0, nblocks - 1)
    is_edge = ((own == first) | (own == last)).astype(jnp.int32)
    chunks = jnp.broadcast_to(span * BLOCK // SPAN, own.shape)
    glob = jnp.stack([is_edge, first * BLOCK, chunks, valid], axis=1).astype(jnp.int32)
    return ids.reshape(-1), limits.astype(jnp.int32).reshape(-1), glob.reshape(-1)


def head_stack_mask():
    r = lax.broadcasted_iota(jnp.int32, (WIDE, WIDE), 0) // HEAD
    c = lax.broadcasted_iota(jnp.int32, (WIDE, WIDE), 1) // HEAD
    return (r == c).astype(jnp.bfloat16)

BLOCK8 = 8


def finish_kernel(
    cut, w_in_ref, w_back_ref, w_out_ref, small_ref, dq_ref, dk_ref, dv_ref, tok_ref, w_ref, pre_ref,
    out_ref, gtok_ref, sum_ref,
    work, got0, got1, got2, got3, piece, slabs, part, part_in, total_ref, small_in,
    send_sem, recv_sem, local_sem,
):
    batch, seq = lax.axis_index("batch"), lax.axis_index("seq")
    inner = lax.rem(batch, BLOCK8)
    base = batch - inner
    x, z = lax.rem(inner, 2), lax.div(inner, 2)
    core, y = lax.rem(seq, 2), lax.div(seq, 2)

    def device(z, x, y, core):
        return (base + z * 2 + x, y * 2 + core)

    sibling = device(z, x, y, 1 - core)
    over_x = device(z, 1 - x, y, core)
    over_y = device(z, x, 1 - y, core)
    over_z = [device(lax.rem(z + k, 4), x, y, core) for k in (1, 2, 3)]
    partners = [sibling, over_x, over_y] + over_z
    barrier = pltpu.get_barrier_semaphore()
    for other in partners:
        pl.semaphore_signal(barrier, inc=1, device_id=other, device_id_type=pl.DeviceIdType.MESH)
    pl.semaphore_wait(barrier, len(partners))

    tick = [0, 0]

    def send(src, dst, other, keep=True):
        k = tick[0]
        tick[0] += 1
        copy = pltpu.make_async_remote_copy(
            src_ref=src,
            dst_ref=dst,
            send_sem=send_sem.at[k],
            recv_sem=recv_sem.at[k],
            device_id=other,
            device_id_type=pl.DeviceIdType.MESH,
        )
        copy.start()
        if keep:
            started.append(copy)
        return copy

    def local(src, dst):
        k = tick[1]
        tick[1] += 1
        copy = pltpu.make_async_copy(src, dst, local_sem.at[k])
        copy.start()
        return copy

    started = []
    rows, feat = gtok_ref.shape
    half = rows // 2
    quarter = half // 4
    mine = pl.multiple_of(core * half, half)
    theirs = pl.multiple_of((1 - core) * half, half)
    own = x * 2 + y
    columns = [pl.ds(0, cut), pl.ds(cut, feat - cut)]

    def add_rows(dst, src, count, step=64):
        def one(i, carry):
            at = pl.ds(pl.multiple_of(i * step, step), step)
            dst[at, :] = dst[at, :] + src[at, :]
            return carry

        lax.fori_loop(0, count // step, one, 0)

    def first_step(k, n, src):
        away = send(src.at[pl.ds(theirs, half), :], got0.at[k, n], sibling)
        here = local(src.at[pl.ds(mine, half), :], work.at[k, n])
        return away, here

    def first_sum(k, n, pair):
        away, here = pair
        here.wait()
        away.wait_recv()
        add_rows(work.at[k, n], got0.at[k, n], half)

    def second_step(k):
        a = [
            send(work.at[k, 2 * (1 - x) + j, :, columns[0]], got1.at[k, j, :, columns[0]], over_x)
            for j in range(2)
        ]
        b = [
            send(work.at[k, 2 * j + 1 - y, :, columns[1]], got1.at[k, j, :, columns[1]], over_y)
            for j in range(2)
        ]
        return a, b

    def third_step(k, moves):
        a, b = moves
        for j in range(2):
            a[j].wait_recv()
            add_rows(work.at[k, 2 * x + j, :, columns[0]], got1.at[k, j, :, columns[0]], half)
        nxt_a = send(
            work.at[k, 2 * x + 1 - y, :, columns[0]], got2.at[k, :, columns[0]], over_y
        )
        for j in range(2):
            b[j].wait_recv()
            add_rows(work.at[k, 2 * j + y, :, columns[1]], got1.at[k, j, :, columns[1]], half)
        nxt_b = send(
            work.at[k, 2 * (1 - x) + y, :, columns[1]], got2.at[k, :, columns[1]], over_x
        )
        return nxt_a, nxt_b

    def fourth_step(k, moves):
        for move, column in zip(moves, columns):
            move.wait_recv()
            add_rows(work.at[k, own, :, column], got2.at[k, :, column], half)
        return [
            send(
                work.at[k, own, pl.ds(pl.multiple_of(lax.rem(z + d, 4) * quarter, quarter), quarter), :],
                got3.at[k, d - 1],
                over_z[d - 1],
            )
            for d in (1, 2, 3)
        ]

    def spread_z(k, moves):
        for move in moves:
            move.wait_recv()
        total = work[k, own, pl.ds(pl.multiple_of(z * quarter, quarter), quarter), :].astype(jnp.float32)
        for d in range(3):
            total = total + got3[k, d].astype(jnp.float32)
        piece[k] = total.astype(jnp.bfloat16)
        place = out_ref.at[k, own, pl.ds(pl.multiple_of(mine + z * quarter, quarter), quarter), :]
        return [send(piece.at[k], place, other) for other in over_z] + [local(piece.at[k], place)]

    def spread_second(k, moves):
        for move in moves[:3]:
            move.wait_recv()
        moves[3].wait()
        a = out_ref.at[k, own, pl.ds(mine, half), columns[0]]
        b = out_ref.at[k, own, pl.ds(mine, half), columns[1]]
        return send(a, a, over_y), send(b, b, over_x)

    def spread_third(k, moves):
        moves[0].wait_recv()
        moves[1].wait_recv()
        result = []
        for j in range(2):
            a = out_ref.at[k, 2 * x + j, pl.ds(mine, half), columns[0]]
            result.append(send(a, a, over_x))
        for j in range(2):
            b = out_ref.at[k, 2 * j + y, pl.ds(mine, half), columns[1]]
            result.append(send(b, b, over_y))
        return result

    def spread_cores(k, moves):
        for move in moves:
            move.wait_recv()
        place = out_ref.at[k, :, pl.ds(mine, half), :]
        return send(place, place, sibling)

    def small_step(s, other):
        move = send(sum_ref if s else small_ref, small_in.at[s], other, False)
        return move

    def small_add(s, move):
        move.wait()
        sum_ref[...] = (sum_ref if s else small_ref)[...] + small_in[s]

    small_partners = [
        sibling,
        over_x,
        over_y,
        device(z + 1 - 2 * lax.rem(z, 2), x, y, core),
        device(lax.rem(z + 2, 4), x, y, core),
    ]

    def token_part(py, pc):
        at = pl.ds(pl.multiple_of((py * 2 + pc) * rows, rows), rows)
        return dot(dk_ref[at, :], w_ref[:, feat : 2 * feat], NT) + dot(
            dv_ref[at, :], w_ref[:, 2 * feat : 3 * feat], NT
        )

    def weight_rows(columns_at, store):
        at = pl.ds(pl.multiple_of(seq * rows, rows), rows)
        store(0, dot(tok_ref[at, columns_at], dq_ref[...], TN).astype(jnp.bfloat16))
        store(1, dot(tok_ref[:, columns_at], dk_ref[...], TN).astype(jnp.bfloat16))
        store(2, dot(tok_ref[:, columns_at], dv_ref[...], TN).astype(jnp.bfloat16))

    pre_copy = local(pre_ref, total_ref)
    firsts = [[first_step(k, n, src.at[n]) for n in range(4)] for k, src in ((0, w_in_ref), (1, w_back_ref))]
    out_first = first_step(2, 3, w_out_ref)
    small_move = small_step(0, small_partners[0])
    part[0] = token_part(1 - y, 1 - core).astype(jnp.bfloat16)
    far = send(part.at[0], part_in.at[0], sibling)
    for n in range(4):
        first_sum(0, n, firsts[0][n])
    seconds = [second_step(0), None, None]
    part[1] = token_part(y, 1 - core).astype(jnp.bfloat16)
    near = send(part.at[1], part_in.at[1], sibling)
    for n in range(4):
        first_sum(1, n, firsts[1][n])
    seconds[1] = second_step(1)
    small_add(0, small_move)
    small_move = small_step(1, small_partners[1])
    part[2] = token_part(1 - y, core).astype(jnp.bfloat16)
    far.wait_recv()
    add_rows(part.at[2], part_in.at[0], rows)
    cross = send(part.at[2], part_in.at[2], over_y)

    def store_away(n, value):
        slabs[n] = value

    def store_here(n, value):
        work[2, n] = value

    weight_rows(pl.ds(theirs, half), store_away)
    away = [send(slabs.at[n], got0.at[2, n], sibling) for n in range(3)]
    thirds = [third_step(0, seconds[0]), None, None]
    weight_rows(pl.ds(mine, half), store_here)
    thirds[1] = third_step(1, seconds[1])
    small_add(1, small_move)
    small_move = small_step(2, small_partners[2])
    for n in range(3):
        away[n].wait_recv()
        add_rows(work.at[2, n], got0.at[2, n], half)
    first_sum(2, 3, out_first)
    seconds[2] = second_step(2)
    fourths = [fourth_step(0, thirds[0]), None, None]
    pre_copy.wait()
    total_ref[...] = (
        total_ref[...] + dot(dq_ref[...], w_ref[:, 0:feat], NT) + token_part(y, core)
    )
    fourths[1] = fourth_step(1, thirds[1])
    spreads = [spread_z(0, fourths[0]), None, None]
    small_add(2, small_move)
    small_move = small_step(3, small_partners[3])
    thirds[2] = third_step(2, seconds[2])
    spreads[1] = spread_z(1, fourths[1])
    seconds_out = [spread_second(0, spreads[0]), None, None]
    small_add(3, small_move)
    small_move = small_step(4, small_partners[4])
    fourths[2] = fourth_step(2, thirds[2])
    seconds_out[1] = spread_second(1, spreads[1])
    thirds_out = [spread_third(0, seconds_out[0]), None, None]
    spreads[2] = spread_z(2, fourths[2])
    thirds_out[1] = spread_third(1, seconds_out[1])
    lasts = [spread_cores(0, thirds_out[0])]
    seconds_out[2] = spread_second(2, spreads[2])
    small_add(4, small_move)
    thirds_out[2] = spread_third(2, seconds_out[2])
    lasts.append(spread_cores(1, thirds_out[1]))
    near.wait_recv()
    cross.wait_recv()
    gtok_ref[...] = (
        total_ref[...] + part_in[1].astype(jnp.float32) + part_in[2].astype(jnp.float32)
    ).astype(jnp.bfloat16)
    lasts.append(spread_cores(2, thirds_out[2]))
    for move in lasts:
        move.wait_recv()
    for copy in started:
        copy.wait_send()


def finish(w_in_grad, w_back_grad, w_out_grad, small, dq, dk, dv, group_tokens, w_qkv, grad_pre1):
    rows, feat = dq.shape
    half = rows // 2
    low = jnp.bfloat16
    vmem = pl.BlockSpec(memory_space=pltpu.VMEM)
    anywhere = pl.BlockSpec(memory_space=pl.ANY)
    return pl.pallas_call(
        functools.partial(finish_kernel, feat // 2),
        out_shape=(
            jax.ShapeDtypeStruct((3, 4, rows, feat), low),
            jax.ShapeDtypeStruct((rows, feat), low),
            jax.ShapeDtypeStruct(small.shape, jnp.float32),
        ),
        in_specs=[anywhere, anywhere, anywhere, vmem, vmem, vmem, vmem, vmem, vmem, anywhere],
        out_specs=(anywhere, vmem, vmem),
        scratch_shapes=[
            pltpu.VMEM((3, 4, half, feat), low),
            pltpu.VMEM((3, 4, half, feat), low),
            pltpu.VMEM((3, 2, half, feat), low),
            pltpu.VMEM((3, half, feat), low),
            pltpu.VMEM((3, 3, half // 4, feat), low),
            pltpu.VMEM((3, half // 4, feat), low),
            pltpu.VMEM((3, half, feat), low),
            pltpu.VMEM((3, rows, feat), low),
            pltpu.VMEM((3, rows, feat), low),
            pltpu.VMEM((rows, feat), jnp.float32),
            pltpu.VMEM((5,) + small.shape, jnp.float32),
            pltpu.SemaphoreType.DMA((128,)),
            pltpu.SemaphoreType.DMA((128,)),
            pltpu.SemaphoreType.DMA((32,)),
        ],
        compiler_params=pltpu.CompilerParams(
            collective_id=0, has_side_effects=True, vmem_limit_bytes=60 * 2**20
        ),
        name="finish",
    )(w_in_grad, w_back_grad, w_out_grad, small, dq, dk, dv, group_tokens, w_qkv, grad_pre1)


def plain_dot(left, right):
    return dot(left, right)


def left_dot(left, right):
    return dot(left, right, TN)


def right_dot(left, right):
    return dot(left, right, NT)


def normalize(values, norm_gain, norm_shift):
    centred = values - jnp.mean(values, axis=-1, keepdims=True)
    spread_inv = lax.rsqrt(jnp.mean(centred * centred, axis=-1, keepdims=True) + NORM_EPS)
    unit_value = centred * spread_inv
    return (unit_value * norm_gain + norm_shift, unit_value, spread_inv)


def normalize_back(grad_values, unit_value, spread_inv, norm_gain):
    scaled = grad_values * norm_gain
    centred = (
        scaled
        - jnp.mean(scaled, axis=-1, keepdims=True)
        - unit_value * jnp.mean(scaled * unit_value, axis=-1, keepdims=True)
    )
    return (
        spread_inv * centred,
        jnp.sum(grad_values * unit_value, axis=0),
        jnp.sum(grad_values, axis=0),
    )


def per_device(
    tokens,
    group_bucket,
    lengths,
    random_blocks,
    w_qkv,
    w_out,
    b_out,
    norm1_gain,
    norm1_shift,
    w_in,
    b_in,
    w_back,
    b_back,
    norm2_gain,
    norm2_shift,
    cotangent,
):
    low = jnp.bfloat16
    seq_parts = lax.axis_size("seq")
    part = lax.axis_index("seq")
    tok_rows, feat = tokens.shape
    blocks = tok_rows // BLOCK
    nblocks = blocks * seq_parts
    tables = attention_tables(
        part, blocks, nblocks, group_bucket[0], lengths[0], random_blocks[0]
    )
    head_mask = head_stack_mask()
    w_q, w_kv = w_qkv[:, :feat], w_qkv[:, feat:]
    inputs = tokens.astype(jnp.float32)
    group_tokens = lax.all_gather(tokens, "seq", axis=0, tiled=True)
    queries = plain_dot(tokens, w_q).astype(low) * low(HEAD ** (-0.5))
    kv = plain_dot(group_tokens, w_kv).astype(low)
    mixed, logs = attend(*tables, queries, kv, head_mask)

    branch = plain_dot(mixed, w_out) + b_out
    hidden, unit_first, spread_first = normalize(inputs + branch, norm1_gain, norm1_shift)
    hidden_low = hidden.astype(low)
    inner_pre = plain_dot(hidden_low, w_in) + b_in
    active, gelu_pull = jax.vjp(lambda value: jax.nn.gelu(value, approximate=False), inner_pre)
    active_low = active.astype(low)
    second = plain_dot(active_low, w_back) + b_back
    layer_out, unit_second, spread_second = normalize(hidden + second, norm2_gain, norm2_shift)
    grad_pre2, grad_gain2, grad_shift2 = normalize_back(
        cotangent.astype(jnp.float32), unit_second, spread_second, norm2_gain
    )
    grad_second = grad_pre2.astype(low)
    grad_w_back = left_dot(active_low, grad_second).astype(low).reshape(4, tok_rows, feat)
    grad_b_back = jnp.sum(grad_second.astype(jnp.float32), axis=0)
    grad_inner = gelu_pull(right_dot(grad_second, w_back))[0].astype(low)
    grad_w_in = jnp.stack(
        [left_dot(hidden_low, grad_inner[:, n * feat : (n + 1) * feat]).astype(low) for n in range(4)]
    )
    grad_b_in = jnp.sum(grad_inner.astype(jnp.float32), axis=0)
    grad_hidden = grad_pre2 + right_dot(grad_inner, w_in)
    grad_pre1, grad_gain1, grad_shift1 = normalize_back(
        grad_hidden, unit_first, spread_first, norm1_gain
    )
    grad_branch = grad_pre1.astype(low)
    grad_w_out = left_dot(mixed, grad_branch).astype(low)
    grad_b_out = jnp.sum(grad_branch.astype(jnp.float32), axis=0)
    grad_mixed = right_dot(grad_branch, w_out).astype(low)

    def fold(value):
        return jnp.pad(value.reshape(-1, feat), ((0, 0), (0, 0)))

    small = jnp.concatenate(
        [
            fold(v)
            for v in (
                grad_b_out, grad_gain1, grad_shift1, grad_b_back, grad_gain2, grad_shift2, grad_b_in,
            )
        ],
        axis=0,
    )
    used = small.shape[0]
    small = jnp.pad(small, ((0, 16 - used), (0, 0)))
    dq, dk, dv = attend_back(*tables, queries, kv, grad_mixed, mixed, logs, head_mask)
    grads, grad_tokens, sums = finish(
        grad_w_in, grad_w_back, grad_w_out, small, dq, dk, dv, group_tokens, w_qkv, grad_pre1
    )
    wide = jnp.float32
    outer = lax.axis_size("batch") // BLOCK8
    if outer > 1:
        groups = [[o * BLOCK8 + i for o in range(outer)] for i in range(BLOCK8)]
        grads = lax.psum(grads.astype(wide), "batch", axis_index_groups=groups)
        sums = lax.psum(sums, "batch", axis_index_groups=groups)
    grads = grads.astype(wide)
    full_in = grads[0].transpose(1, 0, 2).reshape(w_in.shape)
    full_back = grads[1].reshape(w_back.shape)
    full_qkv = grads[2, :3].transpose(1, 0, 2).reshape(w_qkv.shape)
    full_out = grads[2, 3]
    return (
        layer_out.astype(low),
        grad_tokens,
        full_qkv,
        full_out,
        sums[0],
        sums[1],
        sums[2],
        full_in,
        sums[6:10].reshape(b_in.shape),
        full_back,
        sums[3],
        sums[4],
        sums[5],
    )


def solution(mesh):
    rows = P(("batch", "seq"), None)
    whole = P()
    placed = (rows, P("batch"), P("batch", None), P("batch", None, None)) + (whole,) * 11 + (rows,)
    return jax.shard_map(
        per_device,
        mesh=mesh,
        in_specs=placed,
        out_specs=(rows, rows) + (whole,) * 11,
        check_vma=False,
    )
```

```python
import functools
import jax
import jax.numpy as jnp
from jax import lax
from jax.sharding import PartitionSpec as P
from jax.experimental import pallas as pl
from jax.experimental.pallas import tpu as pltpu

HEADS = 12
HEAD = 64
BLOCK = 64
SHORT = 1024
LISTED = 8
QUAD = 4
WIDE = QUAD * HEAD
SPAN = LISTED * BLOCK
MASKED = -1e30
NORM_EPS = 1e-06
NT = (((1,), (1,)), ((), ()))
TN = (((0,), (0,)), ((), ()))


def dot(a, b, dims=(((1,), (0,)), ((), ()))):
    return lax.dot_general(a, b, dims, preferred_element_type=jnp.float32)


def stack_heads(rows, head_mask):
    return jnp.concatenate([rows] * QUAD, axis=0) * head_mask


def pick_heads(full, lane_head):
    out = full[0:BLOCK]
    for h in range(1, QUAD):
        out = jnp.where(lane_head == h, full[h * BLOCK : (h + 1) * BLOCK], out)
    return out


def masked_span(scores, row_id, limits):
    parts = []
    for j in range(LISTED):
        parts.append(
            jnp.where(row_id < limits[j], scores[j * BLOCK : (j + 1) * BLOCK], MASKED)
        )
    return jnp.concatenate(parts, axis=0)


def attend_kernel(
    blocks, ids_ref, lim_ref, glob_ref, q_ref, k_ref, v_ref, hm_ref, o_ref, l_ref, kcat, vcat, acc
):
    row_id = lax.broadcasted_iota(jnp.int32, (BLOCK, WIDE), 0)
    lane_head = lax.broadcasted_iota(jnp.int32, (BLOCK, WIDE), 1) // HEAD
    chunk_row = lax.broadcasted_iota(jnp.int32, (SHORT, WIDE), 0)

    def one_block(b, carry):
        rows = pl.ds(pl.multiple_of(b * BLOCK, BLOCK), BLOCK)
        qm = stack_heads(q_ref[rows, :], hm_ref[...])
        for j in range(LISTED):
            src = pl.ds(pl.multiple_of(ids_ref[b * LISTED + j] * BLOCK, BLOCK), BLOCK)
            kcat[j * BLOCK : (j + 1) * BLOCK, :] = k_ref[src, :]
            vcat[j * BLOCK : (j + 1) * BLOCK, :] = v_ref[src, :]
        limits = [lim_ref[b * LISTED + j] for j in range(LISTED)]
        scores = masked_span(dot(kcat[...], qm, NT), row_id, limits)
        top = jnp.max(scores, axis=0, keepdims=True)
        grown = jnp.exp(scores - top)
        total = jnp.sum(grown, axis=0, keepdims=True)
        weights = (grown * (1.0 / total)).astype(jnp.bfloat16)
        full = dot(weights, vcat[...], TN)
        o_ref[rows, :] = pick_heads(full, lane_head).astype(jnp.bfloat16)
        l_ref[0, pl.ds(b, 1), :] = top + jnp.log(total)
        return carry

    lax.fori_loop(0, blocks, one_block, 0, unroll=UNROLL_F)

    def one_global(b, carry):
        @pl.when(glob_ref[b * 4] > 0)
        def _():
            rows = pl.ds(pl.multiple_of(b * BLOCK, BLOCK), BLOCK)
            qm = stack_heads(q_ref[rows, :], hm_ref[...])
            first = glob_ref[b * 4 + 1]
            valid = glob_ref[b * 4 + 3]
            acc[...] = jnp.zeros_like(acc)

            def one_chunk(c, state):
                top, total = state
                src = pl.ds(pl.multiple_of(first + c * SHORT, BLOCK), SHORT)
                scores = dot(k_ref[src, :], qm, NT)
                scores = jnp.where(chunk_row < valid - c * SHORT, scores, MASKED)
                newer = jnp.maximum(top, jnp.max(scores, axis=0, keepdims=True))
                shrink = jnp.exp(top - newer)
                grown = jnp.exp(scores - newer)
                acc[...] = acc[...] * shrink + dot(v_ref[src, :], grown.astype(jnp.bfloat16), TN)
                return (newer, total * shrink + jnp.sum(grown, axis=0, keepdims=True))

            top, total = lax.fori_loop(
                0,
                glob_ref[b * 4 + 2],
                one_chunk,
                (jnp.full((1, WIDE), MASKED, jnp.float32), jnp.zeros((1, WIDE), jnp.float32)),
            )
            full = (acc[...] * (1.0 / total)).T
            o_ref[rows, :] = pick_heads(full, lane_head).astype(jnp.bfloat16)
            l_ref[0, pl.ds(b, 1), :] = top + jnp.log(total)

        return carry

    lax.fori_loop(0, blocks, one_global, 0)

UNROLL_F = 12
UNROLL_B = 6

def smem():
    return pl.BlockSpec(memory_space=pltpu.SMEM)


def attend(ids, limits, glob, queries, kv, head_mask):
    rows, feat = queries.shape
    keys = kv.shape[0]
    quads = feat // WIDE
    blocks = rows // BLOCK
    pad_blocks = -(-blocks // 8) * 8
    return pl.pallas_call(
        functools.partial(attend_kernel, blocks),
        grid=(quads,),
        out_shape=(
            jax.ShapeDtypeStruct((rows, feat), jnp.bfloat16),
            jax.ShapeDtypeStruct((quads, pad_blocks, WIDE), jnp.float32),
        ),
        in_specs=[
            smem(),
            smem(),
            smem(),
            pl.BlockSpec((rows, WIDE), lambda i: (0, i)),
            pl.BlockSpec((keys, WIDE), lambda i: (0, i)),
            pl.BlockSpec((keys, WIDE), lambda i: (0, i + quads)),
            pl.BlockSpec((WIDE, WIDE), lambda i: (0, 0)),
        ],
        out_specs=[
            pl.BlockSpec((rows, WIDE), lambda i: (0, i)),
            pl.BlockSpec((1, pad_blocks, WIDE), lambda i: (i, 0, 0)),
        ],
        scratch_shapes=[
            pltpu.VMEM((SPAN, WIDE), jnp.bfloat16),
            pltpu.VMEM((SPAN, WIDE), jnp.bfloat16),
            pltpu.VMEM((WIDE, WIDE), jnp.float32),
        ],
        compiler_params=pltpu.CompilerParams(vmem_limit_bytes=56 * 2**20),
        name="attend",
    )(ids, limits, glob, queries, kv, kv, head_mask)


def attend_back_kernel(
    blocks, ids_ref, lim_ref, glob_ref, q_ref, k_ref, v_ref, g_ref, o_ref, l_ref, hm_ref,
    dq_ref, dk_ref, dv_ref, kcat, vcat, dk_sum, dv_sum, acc,
):
    row_id = lax.broadcasted_iota(jnp.int32, (BLOCK, WIDE), 0)
    lane_head = lax.broadcasted_iota(jnp.int32, (BLOCK, WIDE), 1) // HEAD
    chunk_row = lax.broadcasted_iota(jnp.int32, (SHORT, WIDE), 0)
    dk_sum[...] = jnp.zeros_like(dk_sum)
    dv_sum[...] = jnp.zeros_like(dv_sum)
    factor = HEAD ** (-0.5)

    def one_block(b, carry):
        rows = pl.ds(pl.multiple_of(b * BLOCK, BLOCK), BLOCK)
        keep = jnp.where(glob_ref[b * 4] > 0, 0.0, 1.0).astype(jnp.bfloat16)
        qm = stack_heads(q_ref[rows, :], hm_ref[...])
        gm = stack_heads(g_ref[rows, :] * keep, hm_ref[...])
        starts = [pl.multiple_of(ids_ref[b * LISTED + j] * BLOCK, BLOCK) for j in range(LISTED)]
        for j in range(LISTED):
            kcat[j * BLOCK : (j + 1) * BLOCK, :] = k_ref[pl.ds(starts[j], BLOCK), :]
            vcat[j * BLOCK : (j + 1) * BLOCK, :] = v_ref[pl.ds(starts[j], BLOCK), :]
        limits = [lim_ref[b * LISTED + j] for j in range(LISTED)]
        scores = masked_span(dot(kcat[...], qm, NT), row_id, limits)
        chance = jnp.exp(scores - l_ref[0, pl.ds(b, 1), :])
        grad_w = dot(vcat[...], gm, NT)
        mean = jnp.sum(chance * grad_w, axis=0, keepdims=True)
        grad_s = (chance * (grad_w - mean)).astype(jnp.bfloat16)
        dk_part = dot(grad_s, qm)
        dv_part = dot(chance.astype(jnp.bfloat16), gm)
        for j in range(LISTED):
            dst = pl.ds(starts[j], BLOCK)
            dk_sum[dst, :] += dk_part[j * BLOCK : (j + 1) * BLOCK]
            dv_sum[dst, :] += dv_part[j * BLOCK : (j + 1) * BLOCK]
        full = dot(grad_s, kcat[...], TN)
        dq_ref[rows, :] = (pick_heads(full, lane_head) * factor).astype(jnp.bfloat16)
        return carry

    lax.fori_loop(0, blocks, one_block, 0, unroll=UNROLL_B)

    def one_global(b, carry):
        @pl.when(glob_ref[b * 4] > 0)
        def _():
            rows = pl.ds(pl.multiple_of(b * BLOCK, BLOCK), BLOCK)
            qm = stack_heads(q_ref[rows, :], hm_ref[...])
            gm = stack_heads(g_ref[rows, :], hm_ref[...])
            first = glob_ref[b * 4 + 1]
            valid = glob_ref[b * 4 + 3]
            log_total = l_ref[0, pl.ds(b, 1), :]
            both = (g_ref[rows, :].astype(jnp.float32) * o_ref[rows, :].astype(jnp.float32)).T
            mean = jnp.concatenate(
                [
                    jnp.sum(both[h * HEAD : (h + 1) * HEAD], axis=0, keepdims=True)
                    for h in range(QUAD)
                ],
                axis=1,
            )
            acc[...] = jnp.zeros_like(acc)

            def one_chunk(c, carry):
                src = pl.ds(pl.multiple_of(first + c * SHORT, BLOCK), SHORT)
                scores = dot(k_ref[src, :], qm, NT)
                scores = jnp.where(chunk_row < valid - c * SHORT, scores, MASKED)
                chance = jnp.exp(scores - log_total)
                grad_w = dot(v_ref[src, :], gm, NT)
                grad_s = (chance * (grad_w - mean)).astype(jnp.bfloat16)
                dk_sum[src, :] += dot(grad_s, qm)
                dv_sum[src, :] += dot(chance.astype(jnp.bfloat16), gm)
                acc[...] += dot(grad_s, k_ref[src, :], TN)
                return carry

            lax.fori_loop(0, glob_ref[b * 4 + 2], one_chunk, 0)
            dq_ref[rows, :] = (pick_heads(acc[...], lane_head) * factor).astype(jnp.bfloat16)

        return carry

    lax.fori_loop(0, blocks, one_global, 0)
    dk_ref[...] = dk_sum[...].astype(jnp.bfloat16)
    dv_ref[...] = dv_sum[...].astype(jnp.bfloat16)


def attend_back(ids, limits, glob, queries, kv, grads, mixed, logs, head_mask):
    rows, feat = queries.shape
    keys = kv.shape[0]
    quads = feat // WIDE
    blocks = rows // BLOCK
    pad_blocks = logs.shape[1]
    row_spec = pl.BlockSpec((rows, WIDE), lambda i: (0, i))
    key_spec = pl.BlockSpec((keys, WIDE), lambda i: (0, i))
    return pl.pallas_call(
        functools.partial(attend_back_kernel, blocks),
        grid=(quads,),
        out_shape=(
            jax.ShapeDtypeStruct((rows, feat), jnp.bfloat16),
            jax.ShapeDtypeStruct((keys, feat), jnp.bfloat16),
            jax.ShapeDtypeStruct((keys, feat), jnp.bfloat16),
        ),
        in_specs=[
            smem(),
            smem(),
            smem(),
            row_spec,
            key_spec,
            pl.BlockSpec((keys, WIDE), lambda i: (0, i + quads)),
            row_spec,
            row_spec,
            pl.BlockSpec((1, pad_blocks, WIDE), lambda i: (i, 0, 0)),
            pl.BlockSpec((WIDE, WIDE), lambda i: (0, 0)),
        ],
        out_specs=[row_spec, key_spec, key_spec],
        scratch_shapes=[
            pltpu.VMEM((SPAN, WIDE), jnp.bfloat16),
            pltpu.VMEM((SPAN, WIDE), jnp.bfloat16),
            pltpu.VMEM((keys, WIDE), jnp.float32),
            pltpu.VMEM((keys, WIDE), jnp.float32),
            pltpu.VMEM((WIDE, WIDE), jnp.float32),
        ],
        compiler_params=pltpu.CompilerParams(vmem_limit_bytes=56 * 2**20),
        name="attend_back",
    )(ids, limits, glob, queries, kv, kv, grads, mixed, logs, head_mask)


def attention_tables(part, blocks, nblocks, group_flag, seq_lengths, random_ids):
    short_blocks = SHORT // BLOCK
    own = part * blocks + jnp.arange(blocks, dtype=jnp.int32)
    is_long = group_flag > 0
    member = jnp.where(is_long, 0, own // short_blocks)
    first = jnp.where(is_long, 0, member * short_blocks)
    span = jnp.where(is_long, nblocks, short_blocks)
    slots = jnp.arange(seq_lengths.shape[0], dtype=jnp.int32)
    valid = jnp.sum(jnp.where(member[:, None] == slots[None, :], seq_lengths[None, :], 0), axis=1)
    last = first + span - 1
    own_random = lax.dynamic_slice_in_dim(random_ids, part * blocks, blocks, 0)
    listed = jnp.concatenate(
        [jnp.stack([own - 1, own, own + 1], axis=1), own_random, jnp.stack([first, last], axis=1)],
        axis=1,
    )
    inside = (listed >= first[:, None]) & (listed <= last[:, None])
    column = jnp.arange(LISTED, dtype=jnp.int32)
    repeated = (column[None, :] >= 6) & (jnp.abs(listed - own[:, None]) <= 1)
    limits = valid[:, None] - (listed - first[:, None]) * BLOCK
    limits = jnp.where(inside & jnp.logical_not(repeated), limits, 0)
    ids = jnp.clip(listed, 0, nblocks - 1)
    is_edge = ((own == first) | (own == last)).astype(jnp.int32)
    chunks = jnp.broadcast_to(span // short_blocks, own.shape)
    glob = jnp.stack([is_edge, first * BLOCK, chunks, valid], axis=1).astype(jnp.int32)
    return ids.reshape(-1), limits.astype(jnp.int32).reshape(-1), glob.reshape(-1)


def head_stack_mask():
    r = lax.broadcasted_iota(jnp.int32, (WIDE, WIDE), 0) // HEAD
    c = lax.broadcasted_iota(jnp.int32, (WIDE, WIDE), 1) // HEAD
    return (r == c).astype(jnp.bfloat16)


BLOCK8 = 8


def grid_place():
    batch, seq = lax.axis_index("batch"), lax.axis_index("seq")
    inner = lax.rem(batch, BLOCK8)
    base = batch - inner
    x, z = lax.rem(inner, 2), lax.div(inner, 2)
    core, y = lax.rem(seq, 2), lax.div(seq, 2)
    near, far = lax.rem(z, 2), lax.div(z, 2)

    def device(core=core, x=x, y=y, near=near, far=far):
        return (base + (far * 2 + near) * 2 + x, y * 2 + core)

    return core, x, y, near, far, device


class Copies:
    def __init__(self, send_sem, recv_sem, local_sem):
        self.send_sem, self.recv_sem, self.local_sem = send_sem, recv_sem, local_sem
        self.sent, self.held, self.started = 0, 0, []

    def send(self, src, dst, other, keep=True):
        copy = pltpu.make_async_remote_copy(
            src_ref=src,
            dst_ref=dst,
            send_sem=self.send_sem.at[self.sent],
            recv_sem=self.recv_sem.at[self.sent],
            device_id=other,
            device_id_type=pl.DeviceIdType.MESH,
        )
        self.sent += 1
        copy.start()
        if keep:
            self.started.append(copy)
        return copy

    def local(self, src, dst):
        copy = pltpu.make_async_copy(src, dst, self.local_sem.at[self.held])
        self.held += 1
        copy.start()
        return copy

    def finish(self):
        for copy in self.started:
            copy.wait_send()


def greet(partners):
    barrier = pltpu.get_barrier_semaphore()
    for other in partners:
        pl.semaphore_signal(barrier, inc=1, device_id=other, device_id_type=pl.DeviceIdType.MESH)
    pl.semaphore_wait(barrier, len(partners))


def add_rows(dst, src, step=64):
    count, lead = dst.shape[-2], dst.shape[:-2]
    step = step if count % step == 0 else step // 2

    def one(i, carry):
        at = pl.ds(pl.multiple_of(i * step, step), step)
        if len(lead) == 0:
            dst[at, :] = dst[at, :] + src[at, :]
        elif len(lead) == 1:
            for a in range(lead[0]):
                dst[a, at, :] = dst[a, at, :] + src[a, at, :]
        else:
            for a in range(lead[0]):
                for b in range(lead[1]):
                    dst[a, b, at, :] = dst[a, b, at, :] + src[a, b, at, :]
        return carry

    lax.fori_loop(0, count // step, one, 0)


ORDERS = (("x", "y", "near", "far"), ("y", "near", "x", "far"), ("near", "x", "y", "far"))


def region(fixed, half):
    first = fixed["x"] if "x" in fixed else slice(None)
    second = fixed["y"] if "y" in fixed else slice(None)
    count, start = half, 0
    if "near" in fixed:
        count = half // 2
        start = fixed["near"] * count
    if "far" in fixed:
        start = start + fixed["far"] * (count // 2)
        count = count // 2
    rows = pl.ds(start if isinstance(start, int) else pl.multiple_of(start, count), count)
    return first, second, rows


def region_shape(names, half):
    lead = tuple(2 for name in ("x", "y") if name not in names)
    rows = half // (2 if "near" in names else 1) // (2 if "far" in names else 1)
    return lead + (rows,)


def step_shapes(half, cuts):
    return [
        region_shape(ORDERS[p][: s + 1], half) + (cuts[p + 1] - cuts[p],)
        for p in range(len(ORDERS))
        for s in range(4)
    ]


class Rings:
    def __init__(self, copies, half, cuts, bits, device, got):
        self.copies, self.half, self.bits, self.device, self.got = copies, half, bits, device, got
        self.columns = [pl.ds(cuts[p], cuts[p + 1] - cuts[p]) for p in range(len(ORDERS))]

    def other(self, name):
        return self.device(**{name: 1 - self.bits[name]})

    def part(self, ref, fixed, p, offset=0):
        first, second, rows = region(fixed, self.half)
        if not isinstance(offset, int):
            start = rows.start + offset
            rows = pl.ds(pl.multiple_of(start, rows.size), rows.size)
        return ref.at[first, second, rows, self.columns[p]]

    def fixed(self, p, s, flip=False):
        names = ORDERS[p][: s + 1]
        result = {name: self.bits[name] for name in names}
        if flip:
            result[names[-1]] = 1 - result[names[-1]]
        return result

    def reduce_send(self, k, work, p, s):
        return self.copies.send(
            self.part(work, self.fixed(p, s, True), p), self.got[p * 4 + s].at[k], self.other(ORDERS[p][s])
        )

    def reduce_add(self, k, work, p, s, move):
        move.wait_recv()
        add_rows(self.part(work, self.fixed(p, s), p), self.got[p * 4 + s].at[k])

    def spread(self, out, p, s, offset):
        place = self.part(out, self.fixed(p, s), p, offset)
        return self.copies.send(place, place, self.other(ORDERS[p][s]))


def finish_kernel(
    cuts, w_in_ref, w_back_ref, w_out_ref, small_ref, dq_hbm, dk_hbm, dv_hbm, tok_hbm, w_hbm, pre_ref,
    out_ref, gtok_ref, sum_ref,
    work, got0, *rest,
):
    got, rest = rest[:12], rest[12:]
    (slabs, part, part_in, total_ref, small_in, dq_ref, dk_ref, dv_ref, tok_ref, w_ref,
     send_sem, recv_sem, local_sem) = rest
    core, x, y, near, far, device = grid_place()
    bits = {"x": x, "y": y, "near": near, "far": far}
    seq = lax.axis_index("seq")
    sibling = device(core=1 - core)
    others = {name: device(**{name: 1 - bits[name]}) for name in bits}
    copies = Copies(send_sem, recv_sem, local_sem)
    rows, feat = gtok_ref.shape
    half = rows // 2
    rings = Rings(copies, half, cuts, bits, device, got)
    loads = [
        copies.local(src, dst)
        for src, dst in (
            (w_hbm, w_ref), (dk_hbm, dk_ref), (dv_hbm, dv_ref),
            (tok_hbm, tok_ref), (dq_hbm, dq_ref), (pre_ref, total_ref),
        )
    ]
    greet([sibling] + list(others.values()))
    mine = pl.multiple_of(core * half, half)
    theirs = pl.multiple_of((1 - core) * half, half)
    slab_ids = [(i, j) for i in range(2) for j in range(2)]

    def first_step(k, i, j, src):
        away = copies.send(src.at[pl.ds(theirs, half), :], got0.at[k, i, j], sibling)
        here = copies.local(src.at[pl.ds(mine, half), :], work.at[k, i, j])
        return away, here

    def first_sum(k, i, j, pair):
        away, here = pair
        here.wait()
        away.wait_recv()
        add_rows(work.at[k, i, j], got0.at[k, i, j])

    moves = {}

    def reduce_step(k, s):
        for p in range(3):
            if s > 0:
                rings.reduce_add(k, work.at[k], p, s - 1, moves[k, p, s - 1])
            if s < 4:
                moves[k, p, s] = rings.reduce_send(k, work.at[k], p, s)

    def spread_start(k):
        reduce_step(k, 4)
        own = region(bits, half)[2]
        src = work.at[k, x, y, own, :]
        dst = out_ref.at[k, x, y, pl.ds(pl.multiple_of(mine + own.start, own.size), own.size), :]
        copies.local(src, dst).wait()

    def spread_step(k, s):
        for p in range(3):
            if s < 3:
                moves[k, p, s + 1].wait_recv()
            moves[k, p, s] = rings.spread(out_ref.at[k], p, s, mine)

    def spread_cores(k):
        for p in range(3):
            moves[k, p, 0].wait_recv()
        place = out_ref.at[k, :, :, pl.ds(mine, half), :]
        moves[k] = copies.send(place, place, sibling)

    small_partners = [sibling] + [others[name] for name in ("x", "y", "near", "far")]

    def small_step(s):
        moves["small"] = copies.send(
            sum_ref if s else small_ref, small_in.at[s], small_partners[s], False
        )

    def small_add(s):
        moves["small"].wait()
        sum_ref[...] = (sum_ref if s else small_ref)[...] + small_in[s]

    def token_part(py, pc):
        at = pl.ds(pl.multiple_of((py * 2 + pc) * rows, rows), rows)
        return dot(dk_ref[at, :], w_ref[:, feat : 2 * feat], NT) + dot(
            dv_ref[at, :], w_ref[:, 2 * feat : 3 * feat], NT
        )

    def weight_rows(columns_at, store):
        at = pl.ds(pl.multiple_of(seq * rows, rows), rows)
        store(0, dot(tok_ref[at, columns_at], dq_ref[...], TN).astype(jnp.bfloat16))
        store(1, dot(tok_ref[:, columns_at], dk_ref[...], TN).astype(jnp.bfloat16))
        store(2, dot(tok_ref[:, columns_at], dv_ref[...], TN).astype(jnp.bfloat16))

    def store_away(n, value):
        slabs[n] = value

    def store_here(n, value):
        work[2, n // 2, n % 2] = value

    firsts = {
        (k, i, j): first_step(k, i, j, src.at[2 * i + j])
        for k, src in ((0, w_in_ref), (1, w_back_ref))
        for i, j in slab_ids
    }
    out_first = first_step(2, 1, 1, w_out_ref)
    small_step(0)
    for load in loads[:3]:
        load.wait()
    part[0] = token_part(1 - y, 1 - core).astype(jnp.bfloat16)
    away_far = copies.send(part.at[0], part_in.at[0], sibling)
    for i, j in slab_ids:
        first_sum(0, i, j, firsts[0, i, j])
    reduce_step(0, 0)
    part[1] = token_part(y, 1 - core).astype(jnp.bfloat16)
    away_near = copies.send(part.at[1], part_in.at[1], sibling)
    for i, j in slab_ids:
        first_sum(1, i, j, firsts[1, i, j])
    reduce_step(1, 0)
    small_add(0)
    small_step(1)
    part[2] = token_part(1 - y, core).astype(jnp.bfloat16)
    away_far.wait_recv()
    add_rows(part.at[2], part_in.at[0])
    cross = copies.send(part.at[2], part_in.at[2], others["y"])
    for load in loads[3:5]:
        load.wait()
    weight_rows(pl.ds(theirs, half), store_away)
    away = [copies.send(slabs.at[n], got0.at[2, n // 2, n % 2], sibling) for n in range(3)]
    reduce_step(0, 1)
    weight_rows(pl.ds(mine, half), store_here)
    small_add(1)
    small_step(2)
    for n in range(3):
        away[n].wait_recv()
        add_rows(work.at[2, n // 2, n % 2], got0.at[2, n // 2, n % 2])
    first_sum(2, 1, 1, out_first)
    reduce_step(2, 0)
    reduce_step(1, 1)
    reduce_step(0, 2)
    loads[5].wait()
    total_ref[...] = total_ref[...] + dot(dq_ref[...], w_ref[:, 0:feat], NT) + token_part(y, core)
    reduce_step(0, 3)
    reduce_step(1, 2)
    small_add(2)
    small_step(3)
    spread_start(0)
    spread_step(0, 3)
    reduce_step(2, 1)
    reduce_step(1, 3)
    spread_step(0, 2)
    spread_start(1)
    spread_step(1, 3)
    small_add(3)
    small_step(4)
    reduce_step(2, 2)
    spread_step(0, 1)
    spread_step(1, 2)
    reduce_step(2, 3)
    spread_step(0, 0)
    spread_step(1, 1)
    spread_start(2)
    spread_step(2, 3)
    small_add(4)
    spread_cores(0)
    spread_step(1, 0)
    spread_step(2, 2)
    spread_step(2, 1)
    spread_cores(1)
    spread_step(2, 0)
    away_near.wait_recv()
    cross.wait_recv()
    gtok_ref[...] = (
        total_ref[...] + part_in[1].astype(jnp.float32) + part_in[2].astype(jnp.float32)
    ).astype(jnp.bfloat16)
    spread_cores(2)
    for k in range(3):
        moves[k].wait_recv()
    copies.finish()


CUTS = (0, 384, 512, 768)


def finish(w_in_grad, w_back_grad, w_out_grad, small, dq, dk, dv, group_tokens, w_qkv, grad_pre1):
    rows, feat = dq.shape
    half = rows // 2
    low = jnp.bfloat16
    vmem = pl.BlockSpec(memory_space=pltpu.VMEM)
    anywhere = pl.BlockSpec(memory_space=pl.ANY)
    cuts = CUTS
    return pl.pallas_call(
        functools.partial(finish_kernel, cuts),
        out_shape=(
            jax.ShapeDtypeStruct((3, 2, 2, rows, feat), low),
            jax.ShapeDtypeStruct((rows, feat), low),
            jax.ShapeDtypeStruct(small.shape, jnp.float32),
        ),
        in_specs=[anywhere] * 3 + [vmem] + [anywhere] * 6,
        out_specs=(anywhere, vmem, vmem),
        scratch_shapes=[
            pltpu.VMEM((3, 2, 2, half, feat), low),
            pltpu.VMEM((3, 2, 2, half, feat), low),
        ]
        + [pltpu.VMEM((3,) + shape, low) for shape in step_shapes(half, cuts)]
        + [
            pltpu.VMEM((3, half, feat), low),
            pltpu.VMEM((3, rows, feat), low),
            pltpu.VMEM((3, rows, feat), low),
            pltpu.VMEM((rows, feat), jnp.float32),
            pltpu.VMEM((5,) + small.shape, jnp.float32),
            pltpu.VMEM(dq.shape, low),
            pltpu.VMEM(dk.shape, low),
            pltpu.VMEM(dv.shape, low),
            pltpu.VMEM(group_tokens.shape, low),
            pltpu.VMEM(w_qkv.shape, low),
            pltpu.SemaphoreType.DMA((128,)),
            pltpu.SemaphoreType.DMA((128,)),
            pltpu.SemaphoreType.DMA((32,)),
        ],
        compiler_params=pltpu.CompilerParams(
            collective_id=0, has_side_effects=True, vmem_limit_bytes=60 * 2**20
        ),
        name="finish",
    )(w_in_grad, w_back_grad, w_out_grad, small, dq, dk, dv, group_tokens, w_qkv, grad_pre1)


def widen_kernel(*refs):
    count = len(refs) // 2
    for src, dst in zip(refs[:count], refs[count:]):
        dst[...] = src[0, 0, 0].astype(jnp.float32)


def widen(grads, shapes):
    rows, feat = grads.shape[-2:]
    step = rows // 3
    slabs = shapes[0][1]

    def source(k):
        return pl.BlockSpec((1, 1, 1, step, feat), lambda n, i: (k, n // 2, n % 2, i, 0))

    def target(across):
        if across:
            return pl.BlockSpec((step, feat), lambda n, i: (i, n))
        return pl.BlockSpec((step, feat), lambda n, i: (n * 3 + i, 0))

    return pl.pallas_call(
        widen_kernel,
        grid=(slabs, 3),
        out_shape=[
            jax.ShapeDtypeStruct((rows, feat * n) if across else (rows * n, feat), jnp.float32)
            for _, n, across in shapes
        ],
        in_specs=[source(k) for k, _, _ in shapes],
        out_specs=[target(across) for _, _, across in shapes],
        compiler_params=pltpu.CompilerParams(vmem_limit_bytes=56 * 2**20),
        name="widen",
    )(*([grads] * len(shapes)))


def plain_dot(left, right):
    return dot(left, right)


def left_dot(left, right):
    return dot(left, right, TN)


def right_dot(left, right):
    return dot(left, right, NT)


def normalize(values, norm_gain, norm_shift):
    centred = values - jnp.mean(values, axis=-1, keepdims=True)
    spread_inv = lax.rsqrt(jnp.mean(centred * centred, axis=-1, keepdims=True) + NORM_EPS)
    unit_value = centred * spread_inv
    return (unit_value * norm_gain + norm_shift, unit_value, spread_inv)


def normalize_back(grad_values, unit_value, spread_inv, norm_gain):
    scaled = grad_values * norm_gain
    centred = (
        scaled
        - jnp.mean(scaled, axis=-1, keepdims=True)
        - unit_value * jnp.mean(scaled * unit_value, axis=-1, keepdims=True)
    )
    return (
        spread_inv * centred,
        jnp.sum(grad_values * unit_value, axis=0),
        jnp.sum(grad_values, axis=0),
    )


def per_device(
    tokens,
    group_bucket,
    lengths,
    random_blocks,
    w_qkv,
    w_out,
    b_out,
    norm1_gain,
    norm1_shift,
    w_in,
    b_in,
    w_back,
    b_back,
    norm2_gain,
    norm2_shift,
    cotangent,
):
    low = jnp.bfloat16
    seq_parts = lax.axis_size("seq")
    part = lax.axis_index("seq")
    tok_rows, feat = tokens.shape
    blocks = tok_rows // BLOCK
    nblocks = blocks * seq_parts
    tables = attention_tables(
        part, blocks, nblocks, group_bucket[0], lengths[0], random_blocks[0]
    )
    head_mask = head_stack_mask()
    w_q, w_kv = w_qkv[:, :feat], w_qkv[:, feat:]
    inputs = tokens.astype(jnp.float32)
    group_tokens = lax.all_gather(tokens, "seq", axis=0, tiled=True)
    queries = plain_dot(tokens, w_q).astype(low) * low(HEAD ** (-0.5))
    kv = plain_dot(group_tokens, w_kv).astype(low)
    mixed, logs = attend(*tables, queries, kv, head_mask)

    branch = plain_dot(mixed, w_out) + b_out
    hidden, unit_first, spread_first = normalize(inputs + branch, norm1_gain, norm1_shift)
    hidden_low = hidden.astype(low)
    inner_pre = plain_dot(hidden_low, w_in) + b_in
    active, gelu_pull = jax.vjp(lambda value: jax.nn.gelu(value, approximate=False), inner_pre)
    active_low = active.astype(low)
    second = plain_dot(active_low, w_back) + b_back
    layer_out, unit_second, spread_second = normalize(hidden + second, norm2_gain, norm2_shift)
    grad_pre2, grad_gain2, grad_shift2 = normalize_back(
        cotangent.astype(jnp.float32), unit_second, spread_second, norm2_gain
    )
    grad_second = grad_pre2.astype(low)
    grad_w_back = left_dot(active_low, grad_second).astype(low).reshape(4, tok_rows, feat)
    grad_b_back = jnp.sum(grad_second.astype(jnp.float32), axis=0)
    grad_inner = gelu_pull(right_dot(grad_second, w_back))[0].astype(low)
    grad_w_in = jnp.stack(
        [left_dot(hidden_low, grad_inner[:, n * feat : (n + 1) * feat]).astype(low) for n in range(4)]
    )
    grad_b_in = jnp.sum(grad_inner.astype(jnp.float32), axis=0)
    grad_hidden = grad_pre2 + right_dot(grad_inner, w_in)
    grad_pre1, grad_gain1, grad_shift1 = normalize_back(
        grad_hidden, unit_first, spread_first, norm1_gain
    )
    grad_branch = grad_pre1.astype(low)
    grad_w_out = left_dot(mixed, grad_branch).astype(low)
    grad_b_out = jnp.sum(grad_branch.astype(jnp.float32), axis=0)
    grad_mixed = right_dot(grad_branch, w_out).astype(low)

    def fold(value):
        return jnp.pad(value.reshape(-1, feat), ((0, 0), (0, 0)))

    small = jnp.concatenate(
        [
            fold(v)
            for v in (
                grad_b_out, grad_gain1, grad_shift1, grad_b_back, grad_gain2, grad_shift2, grad_b_in,
            )
        ],
        axis=0,
    )
    used = small.shape[0]
    small = jnp.pad(small, ((0, 16 - used), (0, 0)))
    dq, dk, dv = attend_back(*tables, queries, kv, grad_mixed, mixed, logs, head_mask)
    grads, grad_tokens, sums = finish(
        grad_w_in, grad_w_back, grad_w_out, small, dq, dk, dv, group_tokens, w_qkv, grad_pre1
    )
    wide = jnp.float32
    outer = lax.axis_size("batch") // BLOCK8
    if outer > 1:
        groups = [[o * BLOCK8 + i for o in range(outer)] for i in range(BLOCK8)]
        grads = lax.psum(grads.astype(wide), "batch", axis_index_groups=groups)
        sums = lax.psum(sums, "batch", axis_index_groups=groups)
    if outer > 1:
        grads = grads.astype(low)
    full_in, full_back = widen(grads, [(0, 4, True), (1, 4, False)])
    (full_qkv,) = widen(grads, [(2, 3, True)])
    full_out = grads[2, 1, 1].astype(wide)
    return (
        layer_out.astype(low),
        grad_tokens,
        full_qkv,
        full_out,
        sums[0],
        sums[1],
        sums[2],
        full_in,
        sums[6:10].reshape(b_in.shape),
        full_back,
        sums[3],
        sums[4],
        sums[5],
    )


def solution(mesh):
    rows = P(("batch", "seq"), None)
    whole = P()
    placed = (rows, P("batch"), P("batch", None), P("batch", None, None)) + (whole,) * 11 + (rows,)
    return jax.shard_map(
        per_device,
        mesh=mesh,
        in_specs=placed,
        out_specs=(rows, rows) + (whole,) * 11,
        check_vma=False,
    )
```

```python
import functools
import jax
import jax.numpy as jnp
from jax import lax
from jax.sharding import PartitionSpec as P
from jax.experimental import pallas as pl
from jax.experimental.pallas import tpu as pltpu

HEADS = 12
HEAD = 64
BLOCK = 64
SHORT = 1024
LISTED = 8
QUAD = 4
WIDE = QUAD * HEAD
SPAN = LISTED * BLOCK
MASKED = -1e30
NORM_EPS = 1e-06
NT = (((1,), (1,)), ((), ()))
TN = (((0,), (0,)), ((), ()))


def dot(a, b, dims=(((1,), (0,)), ((), ()))):
    return lax.dot_general(a, b, dims, preferred_element_type=jnp.float32)


def stack_heads(rows, head_mask):
    return jnp.concatenate([rows] * QUAD, axis=0) * head_mask


def pick_heads(full, lane_head):
    out = full[0:BLOCK]
    for h in range(1, QUAD):
        out = jnp.where(lane_head == h, full[h * BLOCK : (h + 1) * BLOCK], out)
    return out


def masked_span(scores, row_id, limits):
    parts = []
    for j in range(LISTED):
        parts.append(
            jnp.where(row_id < limits[j], scores[j * BLOCK : (j + 1) * BLOCK], MASKED)
        )
    return jnp.concatenate(parts, axis=0)


class Layout:
    def __init__(self, blocks, nblocks, bucket_ref, length_ref, random_ref):
        self.first_own = lax.axis_index("seq") * blocks
        self.nblocks, self.short = nblocks, SHORT // BLOCK
        self.is_long = bucket_ref[0] > 0
        self.length_ref, self.random_ref = length_ref, random_ref

    def sequence(self, b):
        own = self.first_own + b
        member = jnp.where(self.is_long, 0, own // self.short)
        first = member * self.short
        span = jnp.where(self.is_long, self.nblocks, self.short)
        return own, first, first + span - 1, self.length_ref[0, member]

    def listed(self, b):
        own, first, last, valid = self.sequence(b)
        starts, limits = [], []
        ids = [own - 1, own, own + 1]
        ids += [self.random_ref[0, own, j] for j in range(3)]
        ids += [first, last]
        for j, block in enumerate(ids):
            inside = (block >= first) & (block <= last)
            if j >= 6:
                inside = inside & (jnp.abs(block - own) > 1)
            limits.append(jnp.where(inside, valid - (block - first) * BLOCK, 0))
            block = jnp.minimum(jnp.maximum(block, 0), self.nblocks - 1)
            starts.append(pl.multiple_of(block * BLOCK, BLOCK))
        return starts, limits

    def whole(self, b):
        own, first, last, valid = self.sequence(b)
        chunks = jnp.where(self.is_long, self.nblocks // self.short, 1)
        return (own == first) | (own == last), first * BLOCK, chunks, valid


def fill_head_mask(hm_ref):
    r = lax.broadcasted_iota(jnp.int32, (WIDE, WIDE), 0) // HEAD
    c = lax.broadcasted_iota(jnp.int32, (WIDE, WIDE), 1) // HEAD
    hm_ref[...] = jnp.where(r == c, 1.0, 0.0).astype(jnp.bfloat16)


def attend_kernel(
    blocks, bucket_ref, length_ref, random_ref, q_ref, k_ref, v_ref, o_ref, l_ref, kcat, vcat, acc,
    hm_ref,
):
    layout = Layout(blocks, k_ref.shape[0] // BLOCK, bucket_ref, length_ref, random_ref)
    fill_head_mask(hm_ref)
    row_id = lax.broadcasted_iota(jnp.int32, (BLOCK, WIDE), 0)
    lane_head = lax.broadcasted_iota(jnp.int32, (BLOCK, WIDE), 1) // HEAD
    chunk_row = lax.broadcasted_iota(jnp.int32, (SHORT, WIDE), 0)

    def one_block(b, carry):
        rows = pl.ds(pl.multiple_of(b * BLOCK, BLOCK), BLOCK)
        qm = stack_heads(q_ref[rows, :], hm_ref[...])
        starts, limits = layout.listed(b)
        for j in range(LISTED):
            src = pl.ds(starts[j], BLOCK)
            kcat[j * BLOCK : (j + 1) * BLOCK, :] = k_ref[src, :]
            vcat[j * BLOCK : (j + 1) * BLOCK, :] = v_ref[src, :]
        scores = masked_span(dot(kcat[...], qm, NT), row_id, limits)
        top = jnp.max(scores, axis=0, keepdims=True)
        grown = jnp.exp(scores - top)
        total = jnp.sum(grown, axis=0, keepdims=True)
        weights = (grown * (1.0 / total)).astype(jnp.bfloat16)
        full = dot(weights, vcat[...], TN)
        o_ref[rows, :] = pick_heads(full, lane_head).astype(jnp.bfloat16)
        l_ref[0, pl.ds(b, 1), :] = top + jnp.log(total)
        return carry

    lax.fori_loop(0, blocks, one_block, 0, unroll=UNROLL_F)

    def one_global(b, carry):
        is_whole, first, chunks, valid = layout.whole(b)

        @pl.when(is_whole)
        def _():
            rows = pl.ds(pl.multiple_of(b * BLOCK, BLOCK), BLOCK)
            qm = stack_heads(q_ref[rows, :], hm_ref[...])
            acc[...] = jnp.zeros_like(acc)

            def one_chunk(c, state):
                top, total = state
                src = pl.ds(pl.multiple_of(first + c * SHORT, BLOCK), SHORT)
                scores = dot(k_ref[src, :], qm, NT)
                scores = jnp.where(chunk_row < valid - c * SHORT, scores, MASKED)
                newer = jnp.maximum(top, jnp.max(scores, axis=0, keepdims=True))
                shrink = jnp.exp(top - newer)
                grown = jnp.exp(scores - newer)
                acc[...] = acc[...] * shrink + dot(v_ref[src, :], grown.astype(jnp.bfloat16), TN)
                return (newer, total * shrink + jnp.sum(grown, axis=0, keepdims=True))

            top, total = lax.fori_loop(
                0,
                chunks,
                one_chunk,
                (jnp.full((1, WIDE), MASKED, jnp.float32), jnp.zeros((1, WIDE), jnp.float32)),
            )
            full = (acc[...] * (1.0 / total)).T
            o_ref[rows, :] = pick_heads(full, lane_head).astype(jnp.bfloat16)
            l_ref[0, pl.ds(b, 1), :] = top + jnp.log(total)

        return carry

    lax.fori_loop(0, blocks, one_global, 0)

UNROLL_F = 12
UNROLL_B = 6

def smem():
    return pl.BlockSpec(memory_space=pltpu.SMEM)


def attend(layout, queries, kv):
    rows, feat = queries.shape
    keys = kv.shape[0]
    quads = feat // WIDE
    blocks = rows // BLOCK
    pad_blocks = -(-blocks // 8) * 8
    return pl.pallas_call(
        functools.partial(attend_kernel, blocks),
        grid=(quads,),
        out_shape=(
            jax.ShapeDtypeStruct((rows, feat), jnp.bfloat16),
            jax.ShapeDtypeStruct((quads, pad_blocks, WIDE), jnp.float32),
        ),
        in_specs=[
            smem(),
            smem(),
            smem(),
            pl.BlockSpec((rows, WIDE), lambda i: (0, i)),
            pl.BlockSpec((keys, WIDE), lambda i: (0, i)),
            pl.BlockSpec((keys, WIDE), lambda i: (0, i + quads)),
        ],
        out_specs=[
            pl.BlockSpec((rows, WIDE), lambda i: (0, i)),
            pl.BlockSpec((1, pad_blocks, WIDE), lambda i: (i, 0, 0)),
        ],
        scratch_shapes=[
            pltpu.VMEM((SPAN, WIDE), jnp.bfloat16),
            pltpu.VMEM((SPAN, WIDE), jnp.bfloat16),
            pltpu.VMEM((WIDE, WIDE), jnp.float32),
            pltpu.VMEM((WIDE, WIDE), jnp.bfloat16),
        ],
        compiler_params=pltpu.CompilerParams(vmem_limit_bytes=56 * 2**20),
        name="attend",
    )(*layout, queries, kv, kv)


def attend_back_kernel(
    blocks, bucket_ref, length_ref, random_ref, q_ref, k_ref, v_ref, g_ref, o_ref, l_ref,
    dq_ref, dk_ref, dv_ref, kcat, vcat, dk_sum, dv_sum, acc, hm_ref,
):
    layout = Layout(blocks, k_ref.shape[0] // BLOCK, bucket_ref, length_ref, random_ref)
    fill_head_mask(hm_ref)
    row_id = lax.broadcasted_iota(jnp.int32, (BLOCK, WIDE), 0)
    lane_head = lax.broadcasted_iota(jnp.int32, (BLOCK, WIDE), 1) // HEAD
    chunk_row = lax.broadcasted_iota(jnp.int32, (SHORT, WIDE), 0)
    dk_sum[...] = jnp.zeros_like(dk_sum)
    dv_sum[...] = jnp.zeros_like(dv_sum)
    factor = HEAD ** (-0.5)

    def one_block(b, carry):
        rows = pl.ds(pl.multiple_of(b * BLOCK, BLOCK), BLOCK)
        keep = jnp.where(layout.whole(b)[0], 0.0, 1.0).astype(jnp.bfloat16)
        qm = stack_heads(q_ref[rows, :], hm_ref[...])
        gm = stack_heads(g_ref[rows, :] * keep, hm_ref[...])
        starts, limits = layout.listed(b)
        for j in range(LISTED):
            kcat[j * BLOCK : (j + 1) * BLOCK, :] = k_ref[pl.ds(starts[j], BLOCK), :]
            vcat[j * BLOCK : (j + 1) * BLOCK, :] = v_ref[pl.ds(starts[j], BLOCK), :]
        scores = masked_span(dot(kcat[...], qm, NT), row_id, limits)
        chance = jnp.exp(scores - l_ref[0, pl.ds(b, 1), :])
        grad_w = dot(vcat[...], gm, NT)
        mean = jnp.sum(chance * grad_w, axis=0, keepdims=True)
        grad_s = (chance * (grad_w - mean)).astype(jnp.bfloat16)
        dk_part = dot(grad_s, qm)
        dv_part = dot(chance.astype(jnp.bfloat16), gm)
        for j in range(LISTED):
            dst = pl.ds(starts[j], BLOCK)
            dk_sum[dst, :] += dk_part[j * BLOCK : (j + 1) * BLOCK]
            dv_sum[dst, :] += dv_part[j * BLOCK : (j + 1) * BLOCK]
        full = dot(grad_s, kcat[...], TN)
        dq_ref[rows, :] = (pick_heads(full, lane_head) * factor).astype(jnp.bfloat16)
        return carry

    lax.fori_loop(0, blocks, one_block, 0, unroll=UNROLL_B)

    def one_global(b, carry):
        is_whole, first, chunks, valid = layout.whole(b)

        @pl.when(is_whole)
        def _():
            rows = pl.ds(pl.multiple_of(b * BLOCK, BLOCK), BLOCK)
            qm = stack_heads(q_ref[rows, :], hm_ref[...])
            gm = stack_heads(g_ref[rows, :], hm_ref[...])
            log_total = l_ref[0, pl.ds(b, 1), :]
            both = (g_ref[rows, :].astype(jnp.float32) * o_ref[rows, :].astype(jnp.float32)).T
            mean = jnp.concatenate(
                [
                    jnp.sum(both[h * HEAD : (h + 1) * HEAD], axis=0, keepdims=True)
                    for h in range(QUAD)
                ],
                axis=1,
            )
            acc[...] = jnp.zeros_like(acc)

            def one_chunk(c, carry):
                src = pl.ds(pl.multiple_of(first + c * SHORT, BLOCK), SHORT)
                scores = dot(k_ref[src, :], qm, NT)
                scores = jnp.where(chunk_row < valid - c * SHORT, scores, MASKED)
                chance = jnp.exp(scores - log_total)
                grad_w = dot(v_ref[src, :], gm, NT)
                grad_s = (chance * (grad_w - mean)).astype(jnp.bfloat16)
                dk_sum[src, :] += dot(grad_s, qm)
                dv_sum[src, :] += dot(chance.astype(jnp.bfloat16), gm)
                acc[...] += dot(grad_s, k_ref[src, :], TN)
                return carry

            lax.fori_loop(0, chunks, one_chunk, 0)
            dq_ref[rows, :] = (pick_heads(acc[...], lane_head) * factor).astype(jnp.bfloat16)

        return carry

    lax.fori_loop(0, blocks, one_global, 0)
    dk_ref[...] = dk_sum[...].astype(jnp.bfloat16)
    dv_ref[...] = dv_sum[...].astype(jnp.bfloat16)


def attend_back(layout, queries, kv, grads, mixed, logs):
    rows, feat = queries.shape
    keys = kv.shape[0]
    quads = feat // WIDE
    blocks = rows // BLOCK
    pad_blocks = logs.shape[1]
    row_spec = pl.BlockSpec((rows, WIDE), lambda i: (0, i))
    key_spec = pl.BlockSpec((keys, WIDE), lambda i: (0, i))
    return pl.pallas_call(
        functools.partial(attend_back_kernel, blocks),
        grid=(quads,),
        out_shape=(
            jax.ShapeDtypeStruct((rows, feat), jnp.bfloat16),
            jax.ShapeDtypeStruct((keys, feat), jnp.bfloat16),
            jax.ShapeDtypeStruct((keys, feat), jnp.bfloat16),
        ),
        in_specs=[
            smem(),
            smem(),
            smem(),
            row_spec,
            key_spec,
            pl.BlockSpec((keys, WIDE), lambda i: (0, i + quads)),
            row_spec,
            row_spec,
            pl.BlockSpec((1, pad_blocks, WIDE), lambda i: (i, 0, 0)),
        ],
        out_specs=[row_spec, key_spec, key_spec],
        scratch_shapes=[
            pltpu.VMEM((SPAN, WIDE), jnp.bfloat16),
            pltpu.VMEM((SPAN, WIDE), jnp.bfloat16),
            pltpu.VMEM((keys, WIDE), jnp.float32),
            pltpu.VMEM((keys, WIDE), jnp.float32),
            pltpu.VMEM((WIDE, WIDE), jnp.float32),
            pltpu.VMEM((WIDE, WIDE), jnp.bfloat16),
        ],
        compiler_params=pltpu.CompilerParams(vmem_limit_bytes=56 * 2**20),
        name="attend_back",
    )(*layout, queries, kv, kv, grads, mixed, logs)


BLOCK8 = 8


def grid_place():
    batch, seq = lax.axis_index("batch"), lax.axis_index("seq")
    inner = lax.rem(batch, BLOCK8)
    base = batch - inner
    x, z = lax.rem(inner, 2), lax.div(inner, 2)
    core, y = lax.rem(seq, 2), lax.div(seq, 2)
    near, far = lax.rem(z, 2), lax.div(z, 2)

    def device(core=core, x=x, y=y, near=near, far=far):
        return (base + (far * 2 + near) * 2 + x, y * 2 + core)

    return core, x, y, near, far, device


class Copies:
    def __init__(self, send_sem, recv_sem, local_sem):
        self.send_sem, self.recv_sem, self.local_sem = send_sem, recv_sem, local_sem
        self.sent, self.held, self.started = 0, 0, []

    def send(self, src, dst, other, keep=True):
        copy = pltpu.make_async_remote_copy(
            src_ref=src,
            dst_ref=dst,
            send_sem=self.send_sem.at[self.sent],
            recv_sem=self.recv_sem.at[self.sent],
            device_id=other,
            device_id_type=pl.DeviceIdType.MESH,
        )
        self.sent += 1
        copy.start()
        if keep:
            self.started.append(copy)
        return copy

    def local(self, src, dst):
        copy = pltpu.make_async_copy(src, dst, self.local_sem.at[self.held])
        self.held += 1
        copy.start()
        return copy

    def finish(self):
        for copy in self.started:
            copy.wait_send()


def greet(partners):
    barrier = pltpu.get_barrier_semaphore()
    for other in partners:
        pl.semaphore_signal(barrier, inc=1, device_id=other, device_id_type=pl.DeviceIdType.MESH)
    pl.semaphore_wait(barrier, len(partners))


def add_rows(dst, src, step=64):
    count, lead = dst.shape[-2], dst.shape[:-2]
    step = step if count % step == 0 else step // 2

    def one(i, carry):
        at = pl.ds(pl.multiple_of(i * step, step), step)
        if len(lead) == 0:
            dst[at, :] = dst[at, :] + src[at, :]
        elif len(lead) == 1:
            for a in range(lead[0]):
                dst[a, at, :] = dst[a, at, :] + src[a, at, :]
        else:
            for a in range(lead[0]):
                for b in range(lead[1]):
                    dst[a, b, at, :] = dst[a, b, at, :] + src[a, b, at, :]
        return carry

    lax.fori_loop(0, count // step, one, 0)


def region(fixed, half):
    first = fixed["x"] if "x" in fixed else slice(None)
    second = fixed["y"] if "y" in fixed else slice(None)
    count, start = half, 0
    if "near" in fixed:
        count = half // 2
        start = fixed["near"] * count
    if "far" in fixed:
        start = start + fixed["far"] * (count // 2)
        count = count // 2
    rows = pl.ds(start if isinstance(start, int) else pl.multiple_of(start, count), count)
    return first, second, rows


def region_shape(names, half):
    lead = tuple(2 for name in ("x", "y") if name not in names)
    rows = half // (2 if "near" in names else 1) // (2 if "far" in names else 1)
    return lead + (rows,)


def step_shapes(half, plan, steps=4):
    return [
        region_shape(names[: s + 1], half) + (stop - start,)
        for names, start, stop in plan
        for s in range(steps)
    ]


class Loaded:
    def __init__(self, copy):
        self.copy = copy

    def wait_recv(self):
        self.copy.wait()


class Rings:
    def __init__(self, copies, half, plan, bits, device, got):
        self.copies, self.half, self.bits, self.device, self.got = copies, half, bits, device, got
        self.names = [names for names, start, stop in plan]
        self.columns = [pl.ds(start, stop - start) for names, start, stop in plan]

    def other(self, name):
        return self.device(**{name: 1 - self.bits[name]})

    def part(self, ref, fixed, p, offset=0):
        first, second, rows = region(fixed, self.half)
        if not isinstance(offset, int):
            start = rows.start + offset
            rows = pl.ds(pl.multiple_of(start, rows.size), rows.size)
        return ref.at[first, second, rows, self.columns[p]]

    def fixed(self, p, s, flip=False):
        names = self.names[p][: s + 1]
        result = {name: self.bits[name] for name in names}
        if flip:
            result[names[-1]] = 1 - result[names[-1]]
        return result

    def spread(self, out, p, s, offset):
        place = self.part(out, self.fixed(p, s), p, offset)
        return self.copies.send(place, place, self.other(self.names[p][s]))


def finish_kernel(
    plan, plan_q, order, work_hbm, *refs,
):
    early_got, refs = refs[: len(plan)], refs[len(plan) :]
    (w_out_ref, small_ref, dq_hbm, dk_hbm, dv_hbm,
     tok_hbm, w_hbm, pre_ref, out_ref, gtok_ref, sum_ref, work, got0, *rest) = refs
    steps_f, steps_q = 4 * len(plan), 4 * len(plan_q)
    got, got_q, rest = rest[:steps_f], rest[steps_f : steps_f + steps_q], rest[steps_f + steps_q :]
    (slabs, part, part_in, total_ref, small_in, dq_ref, dk_ref, dv_ref, tok_ref, w_ref,
     send_sem, recv_sem, local_sem) = rest
    core, x, y, near, far, device = grid_place()
    bits = {"x": x, "y": y, "near": near, "far": far}
    seq = lax.axis_index("seq")
    sibling = device(core=1 - core)
    others = {name: device(**{name: 1 - bits[name]}) for name in bits}
    copies = Copies(send_sem, recv_sem, local_sem)
    rows, feat = gtok_ref.shape
    half = rows // 2
    rings = Rings(copies, half, plan, bits, device, got)
    rings_q = Rings(copies, half, plan_q, bits, device, got_q)
    moves = {}
    early = []
    for k in range(2):
        early.append(copies.local(work_hbm.at[k], work.at[k]))
        for p, src in enumerate(early_got):
            moves[k, p, 0] = Loaded(copies.local(src.at[k], got[p * 4].at[k]))
    loads = {
        name: copies.local(src, dst)
        for name, src, dst in (
            ("w", w_hbm, w_ref), ("dk", dk_hbm, dk_ref), ("dv", dv_hbm, dv_ref),
            ("tok", tok_hbm, tok_ref), ("dq", dq_hbm, dq_ref), ("pre", pre_ref, total_ref),
        )
    }
    loaded = set()

    def need(*wanted):
        for name in wanted:
            if name not in loaded:
                loads[name].wait()
                loaded.add(name)

    greet([sibling] + list(others.values()))
    mine = pl.multiple_of(core * half, half)
    theirs = pl.multiple_of((1 - core) * half, half)

    def lane(k):
        return (rings, k) if k < 2 else (rings_q, 0)

    def reduce_send(k, p, s):
        ring, slot = lane(k)
        moves[k, p, s] = copies.send(
            ring.part(work.at[k], ring.fixed(p, s, True), p),
            ring.got[p * 4 + s].at[slot],
            others[ring.names[p][s]],
        )

    def reduce_step(k, p, s):
        ring, slot = lane(k)
        moves[k, p, s - 1].wait_recv()
        add_rows(ring.part(work.at[k], ring.fixed(p, s - 1), p), ring.got[p * 4 + s - 1].at[slot])
        if s < 4:
            reduce_send(k, p, s)

    def spread_start(k, p):
        reduce_step(k, p, 4)
        ring = lane(k)[0]
        src = ring.part(work.at[k], ring.fixed(p, 3), p)
        dst = ring.part(out_ref.at[k], ring.fixed(p, 3), p, mine)
        moves[k, p, "own"] = copies.local(src, dst)
        moves[k, p, 3] = copies.send(src, dst, others["far"])

    def spread_step(k, p, s):
        moves[k, p, s + 1].wait_recv()
        if s == 2:
            moves[k, p, "own"].wait()
        moves[k, p, s] = lane(k)[0].spread(out_ref.at[k], p, s, mine)

    def spread_cores(k, p):
        moves[k, p, 0].wait_recv()
        place = out_ref.at[k, :, :, pl.ds(mine, half), lane(k)[0].columns[p]]
        moves[k, p, "end"] = copies.send(place, place, sibling)

    small_partners = [sibling] + [others[name] for name in ("x", "y", "near", "far")]

    def small_step(s):
        moves["small"] = copies.send(
            sum_ref if s else small_ref, small_in.at[s], small_partners[s], False
        )

    def small_add(s):
        moves["small"].wait()
        sum_ref[...] = (sum_ref if s else small_ref)[...] + small_in[s]
        if s < 4:
            small_step(s + 1)

    def token_part(py, pc):
        need("w", "dk", "dv")
        at = pl.ds(pl.multiple_of((py * 2 + pc) * rows, rows), rows)
        return dot(dk_ref[at, :], w_ref[:, feat : 2 * feat], NT) + dot(
            dv_ref[at, :], w_ref[:, 2 * feat : 3 * feat], NT
        )

    def weights(n, columns):
        if n == 0:
            need("tok", "dq")
            at = pl.ds(pl.multiple_of(seq * rows, rows), rows)
            return dot(tok_ref[at, columns], dq_ref[...], TN).astype(jnp.bfloat16)
        need("tok", "dk" if n == 1 else "dv")
        return dot(
            tok_ref[:, columns], (dk_ref if n == 1 else dv_ref)[...], TN
        ).astype(jnp.bfloat16)

    away_columns, here_columns = pl.ds(theirs, half), pl.ds(mine, half)

    def weights_away(n):
        slabs[n] = weights(n, away_columns)
        moves["q", n] = copies.send(slabs.at[n], got0.at[n // 2, n % 2], sibling)

    def weights_here(n):
        if n == 3:
            out_here.wait()
        else:
            work[2, n // 2, n % 2] = weights(n, here_columns)
        moves["q", n].wait_recv()
        add_rows(work.at[2, n // 2, n % 2], got0.at[n // 2, n % 2])
        if n == 3:
            for p in range(len(plan_q)):
                reduce_send(2, p, 0)

    def tokens_far():
        part[0] = token_part(1 - y, 1 - core).astype(jnp.bfloat16)
        moves["far"] = copies.send(part.at[0], part_in.at[0], sibling)

    def tokens_near():
        part[1] = token_part(y, 1 - core).astype(jnp.bfloat16)
        moves["near"] = copies.send(part.at[1], part_in.at[1], sibling)

    def tokens_cross():
        part[2] = token_part(1 - y, core).astype(jnp.bfloat16)
        moves["far"].wait_recv()
        add_rows(part.at[2], part_in.at[0])
        moves["cross"] = copies.send(part.at[2], part_in.at[2], others["y"])

    def tokens_own():
        need("w", "pre", "dq")
        total_ref[...] = (
            total_ref[...] + dot(dq_ref[...], w_ref[:, 0:feat], NT) + token_part(y, core)
        )

    def tokens_end():
        moves["near"].wait_recv()
        moves["cross"].wait_recv()
        gtok_ref[...] = (
            total_ref[...] + part_in[1].astype(jnp.float32) + part_in[2].astype(jnp.float32)
        ).astype(jnp.bfloat16)

    moves["q", 3] = copies.send(w_out_ref.at[pl.ds(theirs, half), :], got0.at[1, 1], sibling)
    out_here = copies.local(w_out_ref.at[pl.ds(mine, half), :], work.at[2, 1, 1])
    small_step(0)
    for k in range(2):
        early[k].wait()
        for p in range(len(plan)):
            reduce_step(k, p, 1)
    steps = {
        "add": reduce_step, "top": spread_start, "out": spread_step, "end": spread_cores,
        "small": small_add, "away": weights_away, "here": weights_here, "far": tokens_far,
        "near": tokens_near, "cross": tokens_cross, "own": tokens_own, "last": tokens_end,
    }
    for name, *values in order:
        steps[name](*values)
    for k in range(3):
        for p in range(len(lane(k)[0].names)):
            moves[k, p, "end"].wait_recv()
    copies.finish()


PLAN = (
    (("near", "x", "y", "far"), 0, 256),
    (("y", "x", "near", "far"), 256, 512),
    (("x", "y", "near", "far"), 512, 768),
)
PLAN_Q = (
    (("y", "x", "near", "far"), 0, 256),
    (("near", "y", "x", "far"), 256, 512),
    (("x", "y", "near", "far"), 512, 768),
)
ORDER = (
    ("far",), ("small", 0), ("add", 0, 0, 2), ("cross",), ("add", 0, 1, 2), ("add", 0, 2, 2),
    ("add", 1, 2, 2), ("away", 0), ("add", 0, 0, 3), ("away", 1), ("add", 0, 1, 3),
    ("add", 0, 2, 3), ("away", 2), ("add", 1, 1, 2), ("add", 1, 2, 3), ("top", 0, 0),
    ("top", 0, 1), ("small", 1), ("here", 0), ("top", 0, 2), ("here", 1), ("add", 1, 1, 3),
    ("top", 1, 2), ("here", 2), ("add", 1, 0, 2), ("out", 0, 0, 2), ("out", 0, 1, 2),
    ("top", 1, 1), ("out", 0, 2, 2), ("here", 3), ("near",), ("small", 2), ("own",),
    ("out", 0, 0, 1), ("out", 0, 1, 1), ("out", 0, 2, 1), ("add", 1, 0, 3), ("last",),
    ("out", 1, 2, 2), ("add", 2, 2, 1), ("out", 1, 1, 2), ("add", 2, 0, 1), ("add", 2, 1, 1),
    ("out", 0, 0, 0), ("small", 3), ("top", 1, 0), ("out", 0, 2, 0), ("out", 1, 2, 1),
    ("add", 2, 2, 2), ("add", 2, 0, 2), ("out", 0, 1, 0), ("out", 1, 1, 1), ("add", 2, 1, 2),
    ("end", 0, 0), ("small", 4), ("out", 1, 2, 0), ("end", 0, 2), ("out", 1, 0, 2),
    ("add", 2, 2, 3), ("add", 2, 0, 3), ("out", 1, 1, 0), ("add", 2, 1, 3), ("top", 2, 2),
    ("end", 0, 1), ("top", 2, 0), ("out", 1, 0, 1), ("top", 2, 1), ("out", 2, 2, 2),
    ("end", 1, 2), ("out", 2, 0, 2), ("out", 2, 1, 2), ("out", 2, 2, 1), ("end", 1, 1),
    ("out", 1, 0, 0), ("out", 2, 0, 1), ("out", 2, 1, 1), ("out", 2, 2, 0), ("out", 2, 0, 0),
    ("out", 2, 1, 0), ("end", 1, 0), ("end", 2, 2), ("end", 2, 0), ("end", 2, 1),
)


def finish(work, early, w_out_grad, small, dq, dk, dv, group_tokens, w_qkv, grad_pre1):
    rows, feat = dq.shape
    half = rows // 2
    low = jnp.bfloat16
    vmem = pl.BlockSpec(memory_space=pltpu.VMEM)
    anywhere = pl.BlockSpec(memory_space=pl.ANY)
    return pl.pallas_call(
        functools.partial(finish_kernel, PLAN, PLAN_Q, ORDER),
        out_shape=(
            jax.ShapeDtypeStruct((3, 2, 2, rows, feat), low),
            jax.ShapeDtypeStruct((rows, feat), low),
            jax.ShapeDtypeStruct(small.shape, jnp.float32),
        ),
        in_specs=[anywhere] * (2 + len(PLAN)) + [vmem] + [anywhere] * 6,
        out_specs=(anywhere, vmem, vmem),
        scratch_shapes=[
            pltpu.VMEM((3, 2, 2, half, feat), low),
            pltpu.VMEM((2, 2, half, feat), low),
        ]
        + [pltpu.VMEM((2,) + shape, low) for shape in step_shapes(half, PLAN)]
        + [pltpu.VMEM((1,) + shape, low) for shape in step_shapes(half, PLAN_Q)]
        + [
            pltpu.VMEM((3, half, feat), low),
            pltpu.VMEM((3, rows, feat), low),
            pltpu.VMEM((3, rows, feat), low),
            pltpu.VMEM((rows, feat), jnp.float32),
            pltpu.VMEM((5,) + small.shape, jnp.float32),
            pltpu.VMEM(dq.shape, low),
            pltpu.VMEM(dk.shape, low),
            pltpu.VMEM(dv.shape, low),
            pltpu.VMEM(group_tokens.shape, low),
            pltpu.VMEM(w_qkv.shape, low),
            pltpu.SemaphoreType.DMA((128,)),
            pltpu.SemaphoreType.DMA((128,)),
            pltpu.SemaphoreType.DMA((32,)),
        ],
        compiler_params=pltpu.CompilerParams(
            collective_id=0, has_side_effects=True, vmem_limit_bytes=60 * 2**20
        ),
        name="finish",
    )(work, *early, w_out_grad, small, dq, dk, dv, group_tokens, w_qkv, grad_pre1)


def widen_kernel(in_ref, back_ref, last_ref, in_out, back_out, qkv_out, out_out):
    in_out[...] = in_ref[0, 0, 0].astype(jnp.float32)
    back_out[...] = back_ref[0, 0, 0].astype(jnp.float32)
    last = last_ref[0, 0, 0].astype(jnp.float32)

    @pl.when(pl.program_id(0) < 3)
    def _():
        qkv_out[...] = last

    @pl.when(pl.program_id(0) == 3)
    def _():
        out_out[...] = last


def widen(grads):
    rows, feat = grads.shape[-2:]
    step = rows // WIDEN_PARTS
    wide = jnp.float32

    def source(k):
        return pl.BlockSpec((1, 1, 1, step, feat), lambda n, i: (k, n // 2, n % 2, i, 0))

    return pl.pallas_call(
        widen_kernel,
        grid=(4, WIDEN_PARTS),
        out_shape=[
            jax.ShapeDtypeStruct((rows, 4 * feat), wide),
            jax.ShapeDtypeStruct((4 * rows, feat), wide),
            jax.ShapeDtypeStruct((rows, 3 * feat), wide),
            jax.ShapeDtypeStruct((rows, feat), wide),
        ],
        in_specs=[source(k) for k in range(3)],
        out_specs=[
            pl.BlockSpec((step, feat), lambda n, i: (i, n)),
            pl.BlockSpec((step, feat), lambda n, i: (n * WIDEN_PARTS + i, 0)),
            pl.BlockSpec(
                (step, feat),
                lambda n, i: (jnp.where(n < 3, i, WIDEN_PARTS - 1), jnp.minimum(n, 2)),
            ),
            pl.BlockSpec((step, feat), lambda n, i: (jnp.where(n < 3, 0, i), 0)),
        ],
        compiler_params=pltpu.CompilerParams(vmem_limit_bytes=56 * 2**20),
        name="widen",
    )(grads, grads, grads)


WIDEN_PARTS = 3


PIECES = 4


def front_kernel(
    tok_hbm, w_hbm, q_ref, kv_out, all_out, all_ref, kv_ref, w_ref, send_sem, recv_sem, local_sem
):
    core, x, y, near, far, device = grid_place()
    sibling, over_y = device(core=1 - core), device(y=1 - y)
    low = jnp.bfloat16
    rows, feat = q_ref.shape
    piece = rows // PIECES
    copies = Copies(send_sem, recv_sem, local_sem)

    def rows_of(py, pc, i=None):
        start = (py * 2 + pc) * rows
        if i is None:
            return pl.ds(pl.multiple_of(start, rows), rows)
        return pl.ds(pl.multiple_of(start + i * piece, piece), piece)

    own = rows_of(y, core)
    load = copies.local(tok_hbm, all_ref.at[own])
    load_w = copies.local(w_hbm, w_ref)
    greet([sibling, over_y])
    crossing = []
    for i in range(PIECES):
        src = tok_hbm.at[pl.ds(i * piece, piece)]
        crossing.append(copies.send(src, all_ref.at[rows_of(y, core, i)], over_y))
    beside = copies.send(tok_hbm, all_ref.at[own], sibling)
    stores = []

    def project(at):
        kv_ref[at, :] = dot(all_ref[at, :], w_ref[:, feat:]).astype(low)
        stores.append(copies.local(kv_ref.at[at], kv_out.at[at]))
        stores.append(copies.local(all_ref.at[at], all_out.at[at]))

    load.wait()
    load_w.wait()
    project(own)
    q_ref[...] = dot(all_ref[own, :], w_ref[:, 0:feat]).astype(low) * low(HEAD ** (-0.5))
    beside.wait_recv()
    project(rows_of(y, 1 - core))
    passed = []
    for i in range(PIECES):
        crossing[i].wait_recv()
        at = rows_of(1 - y, core, i)
        passed.append(copies.send(all_ref.at[at], all_ref.at[at], sibling))
        project(at)
        if i > 0:
            passed[i - 1].wait_recv()
            project(rows_of(1 - y, 1 - core, i - 1))
    passed[-1].wait_recv()
    project(rows_of(1 - y, 1 - core, PIECES - 1))
    for store in stores:
        store.wait()
    copies.finish()


def front(tokens, w_qkv, seq_parts):
    rows, feat = tokens.shape
    low = jnp.bfloat16
    keys = rows * seq_parts
    anywhere = pl.BlockSpec(memory_space=pl.ANY)
    count = 2 + 2 * PIECES
    return pl.pallas_call(
        front_kernel,
        out_shape=(
            jax.ShapeDtypeStruct((rows, feat), low),
            jax.ShapeDtypeStruct((keys, 2 * feat), low),
            jax.ShapeDtypeStruct((keys, feat), low),
        ),
        in_specs=[anywhere, anywhere],
        out_specs=(pl.BlockSpec(memory_space=pltpu.VMEM), anywhere, anywhere),
        scratch_shapes=[
            pltpu.VMEM((keys, feat), low),
            pltpu.VMEM((keys, 2 * feat), low),
            pltpu.VMEM(w_qkv.shape, low),
            pltpu.SemaphoreType.DMA((count,)),
            pltpu.SemaphoreType.DMA((count,)),
            pltpu.SemaphoreType.DMA((2 + 2 * count,)),
        ],
        compiler_params=pltpu.CompilerParams(
            collective_id=2, has_side_effects=True, vmem_limit_bytes=56 * 2**20
        ),
        name="front",
    )(tokens, w_qkv)


def gelu_parts(v):
    size = jnp.abs(v)
    fall = jnp.exp(-0.5 * v * v)
    t = 1.0 / (1.0 + (0.3275911 * 0.7071067811865476) * size)
    tail = 1.061405429 * t - 1.453152027
    tail = tail * t + 1.421413741
    tail = tail * t - 0.284496736
    tail = tail * t + 0.254829592
    half = 0.5 * tail * t * fall
    return jnp.where(v >= 0.0, 1.0 - half, half), fall


def row_mean(values):
    return jnp.sum(values, axis=-1, keepdims=True) * (1.0 / values.shape[-1])


def fold8(values):
    total = values[0:8]
    for i in range(1, values.shape[0] // 8):
        total = total + values[i * 8 : (i + 1) * 8]
    return total


STEP = 128
TILE = 64


def middle_kernel(
    plan, mixed_ref, tok_ref, cot_ref, *refs,
):
    vec_refs, bias_ref, refs = refs[:6], refs[6], refs[7:]
    (w_out_ref, w_in_hbm, w_back_hbm,
     out_ref, pre_ref, gmix_ref, gw_out_ref, small_ref, work_out, *refs) = refs
    away, refs = refs[: len(plan)], refs[len(plan) :]
    (w_in_ref, w_back_ref, unit, spread, hid, active, slope, acc, acc2, gsecond, gbranch,
     work, slabs, got0, send_sem, recv_sem, local_sem) = refs
    core, x, y, near, far, device = grid_place()
    sibling = device(core=1 - core)
    low = jnp.bfloat16
    rows, feat = tok_ref.shape
    half = rows // 2
    count = 4
    chunks = rows // STEP
    copies = Copies(send_sem, recv_sem, local_sem)
    load_in = copies.local(w_in_hbm, w_in_ref)
    load_back = copies.local(w_back_hbm, w_back_ref)
    greet([sibling])
    mine = pl.multiple_of(core * half, half)
    theirs = pl.multiple_of((1 - core) * half, half)

    def rows_at(i):
        return pl.ds(pl.multiple_of(i * STEP, STEP), STEP)

    def slab_at(n):
        return pl.ds(pl.multiple_of(n * feat, feat), feat)

    def vec(i):
        return vec_refs[i][...].reshape(1, feat)

    zero = jnp.zeros((8, feat), jnp.float32)

    def put(i, value):
        small_ref[i : i + 1, :] = jnp.sum(value, axis=0, keepdims=True)

    small_ref[...] = jnp.zeros_like(small_ref)

    acc[...] = dot(mixed_ref[...], w_out_ref[...])

    def norm_one(i, carry):
        at = rows_at(i)
        v = tok_ref[at, :].astype(jnp.float32) + (acc[at, :] + vec(0))
        v = v - row_mean(v)
        r = lax.rsqrt(row_mean(v * v) + NORM_EPS)
        u = v * r
        unit[at, :] = u
        spread[at, :] = jnp.broadcast_to(r, (STEP, 128))
        hid[at, :] = (u * vec(1) + vec(2)).astype(low)
        return carry

    lax.fori_loop(0, chunks, norm_one, 0)
    load_in.wait()

    acc2[...] = jnp.zeros_like(acc2)

    def forward_slab(n, carry):
        columns = slab_at(n)
        bias = bias_ref[columns].reshape(1, feat)
        inner = dot(hid[...], w_in_ref[:, columns])
        for i in range(rows // TILE):
            at = slice(i * TILE, (i + 1) * TILE)
            v = inner[at] + bias
            chance, fall = gelu_parts(v)
            active[n, at, :] = (v * chance).astype(low)
            slope[n, at, :] = (chance + v * fall * 0.3989422804014327).astype(low)

        @pl.when(n == 0)
        def _():
            load_back.wait()

        acc2[...] += dot(active[n], w_back_ref[columns, :])
        return carry

    lax.fori_loop(0, count, forward_slab, 0)

    def norm_two(i, sums):
        at = rows_at(i)
        v = (unit[at, :] * vec(1) + vec(2)) + (acc2[at, :] + vec(3))
        v = v - row_mean(v)
        r = lax.rsqrt(row_mean(v * v) + NORM_EPS)
        u = v * r
        out_ref[at, :] = (u * vec(4) + vec(5)).astype(low)
        c = cot_ref[at, :].astype(jnp.float32)
        a = c * vec(4)
        g = r * (a - row_mean(a) - u * row_mean(a * u))
        acc2[at, :] = g
        g_low = g.astype(low)
        gsecond[at, :] = g_low
        return (
            sums[0] + fold8(c * u), sums[1] + fold8(c), sums[2] + fold8(g_low.astype(jnp.float32)),
        )

    sums = lax.fori_loop(0, chunks, norm_two, (zero, zero, zero))
    put(4, sums[0])
    put(5, sums[1])
    put(3, sums[2])

    def exchange(k, n):
        return pltpu.make_async_remote_copy(
            src_ref=slabs.at[k, n],
            dst_ref=got0.at[k, n],
            send_sem=send_sem.at[k * 4 + n],
            recv_sem=recv_sem.at[k * 4 + n],
            device_id=sibling,
            device_id_type=pl.DeviceIdType.MESH,
        )

    def collect(k, n):
        exchange(k, n).wait_recv()
        add_rows(work.at[k, lax.div(n, 2), lax.rem(n, 2)], got0.at[k, n])
        exchange(k, n).wait_send()

    def back_slab(n, carry):
        columns = slab_at(n)
        slabs[1, n] = dot(active[n, :, pl.ds(theirs, half)], gsecond[...], TN).astype(low)
        exchange(1, n).start()
        work[1, lax.div(n, 2), lax.rem(n, 2)] = dot(active[n, :, pl.ds(mine, half)], gsecond[...], TN).astype(low)
        gactive = dot(gsecond[...], w_back_ref[columns, :], NT)
        total = zero
        for i in range(rows // TILE):
            at = slice(i * TILE, (i + 1) * TILE)
            g = (gactive[at] * slope[n, at, :].astype(jnp.float32)).astype(low)
            slope[n, at, :] = g
            total = total + fold8(g.astype(jnp.float32))

        small_ref[pl.ds(6 + n, 1), :] = jnp.sum(total, axis=0, keepdims=True)
        slabs[0, n] = dot(hid[:, pl.ds(theirs, half)], slope[n], TN).astype(low)
        exchange(0, n).start()
        collect(1, n)
        work[0, lax.div(n, 2), lax.rem(n, 2)] = dot(hid[:, pl.ds(mine, half)], slope[n], TN).astype(low)

        @pl.when(n > 0)
        def _():
            collect(0, n - 1)

        acc2[...] += dot(slope[n], w_in_ref[:, columns], NT)
        return carry

    lax.fori_loop(0, count, back_slab, 0)

    def norm_back(i, sums):
        at = rows_at(i)
        g = acc2[at, :]
        u = unit[at, :]
        r = spread[at, 0:1]
        a = g * vec(1)
        d = r * (a - row_mean(a) - u * row_mean(a * u))
        pre_ref[at, :] = d
        d_low = d.astype(low)
        gbranch[at, :] = d_low
        return (
            sums[0] + fold8(g * u), sums[1] + fold8(g), sums[2] + fold8(d_low.astype(jnp.float32)),
        )

    sums = lax.fori_loop(0, chunks, norm_back, (zero, zero, zero))
    put(1, sums[0])
    put(2, sums[1])
    put(0, sums[2])
    gmix_ref[...] = dot(gbranch[...], w_out_ref[...], NT).astype(low)
    gw_out_ref[...] = dot(mixed_ref[...], gbranch[...], TN).astype(low)

    collect(0, count - 1)
    stores = [copies.local(work, work_out)]
    bits = {"x": x, "y": y, "near": near, "far": far}
    rings = Rings(copies, half, plan, bits, device, None)
    for k in range(2):
        for p in range(len(plan)):
            stores.append(
                copies.local(rings.part(work.at[k], rings.fixed(p, 0, True), p), away[p].at[k])
            )
    for store in stores:
        store.wait()


def middle(mixed, tokens, cotangent, vectors, b_in, w_out, w_in, w_back):
    rows, feat = tokens.shape
    half = rows // 2
    low = jnp.bfloat16
    wide = jnp.float32
    vmem = pl.BlockSpec(memory_space=pltpu.VMEM)
    anywhere = pl.BlockSpec(memory_space=pl.ANY)
    full = jax.ShapeDtypeStruct((rows, feat), low)
    return pl.pallas_call(
        functools.partial(middle_kernel, PLAN),
        out_shape=(
            full,
            jax.ShapeDtypeStruct((rows, feat), wide),
            full,
            full,
            jax.ShapeDtypeStruct((16, feat), wide),
            jax.ShapeDtypeStruct((2, 2, 2, half, feat), low),
        )
        + tuple(jax.ShapeDtypeStruct((2,) + shape, low) for shape in step_shapes(half, PLAN, 1)),
        in_specs=[vmem] * 11 + [anywhere] * 2,
        out_specs=(vmem,) * 5 + (anywhere,) * (1 + len(PLAN)),
        scratch_shapes=[
            pltpu.VMEM(w_in.shape, low),
            pltpu.VMEM(w_back.shape, low),
            pltpu.VMEM((rows, feat), wide),
            pltpu.VMEM((rows, 128), wide),
            pltpu.VMEM((rows, feat), low),
            pltpu.VMEM((4, rows, feat), low),
            pltpu.VMEM((4, rows, feat), low),
            pltpu.VMEM((rows, feat), wide),
            pltpu.VMEM((rows, feat), wide),
            pltpu.VMEM((rows, feat), low),
            pltpu.VMEM((rows, feat), low),
            pltpu.VMEM((2, 2, 2, half, feat), low),
            pltpu.VMEM((2, 4, half, feat), low),
            pltpu.VMEM((2, 4, half, feat), low),
            pltpu.SemaphoreType.DMA((8,)),
            pltpu.SemaphoreType.DMA((8,)),
            pltpu.SemaphoreType.DMA((16,)),
        ],
        compiler_params=pltpu.CompilerParams(
            collective_id=1, has_side_effects=True, vmem_limit_bytes=60 * 2**20
        ),
        name="middle",
    )(mixed, tokens, cotangent, *vectors, b_in, w_out, w_in, w_back)


FLIPS = {"x": (1, 0), "y": (0, 2), "near": (2, 0)}


def trade(value, name):
    parts = lax.axis_size("seq")
    flip_b, flip_s = FLIPS[name]
    pairs = [
        (b * parts + s, (b ^ flip_b) * parts + (s ^ flip_s))
        for b in range(lax.axis_size("batch"))
        for s in range(parts)
    ]
    return lax.ppermute(value, ("batch", "seq"), pairs)


def per_device(
    tokens,
    group_bucket,
    lengths,
    random_blocks,
    w_qkv,
    w_out,
    b_out,
    norm1_gain,
    norm1_shift,
    w_in,
    b_in,
    w_back,
    b_back,
    norm2_gain,
    norm2_shift,
    cotangent,
):
    low = jnp.bfloat16
    seq_parts = lax.axis_size("seq")
    tok_rows, feat = tokens.shape
    layout = (group_bucket, lengths, random_blocks)
    queries, kv, group_tokens = front(tokens, w_qkv, seq_parts)
    mixed, logs = attend(layout, queries, kv)
    vectors = (b_out, norm1_gain, norm1_shift, b_back, norm2_gain, norm2_shift)
    layer_out, grad_pre1, grad_mixed, grad_w_out, small, work, *away = middle(
        mixed, tokens, cotangent, vectors, b_in, w_out, w_in, w_back
    )
    early = [trade(value, names[0]) for value, (names, _, _) in zip(away, PLAN)]
    dq, dk, dv = attend_back(layout, queries, kv, grad_mixed, mixed, logs)
    grads, grad_tokens, sums = finish(
        work,
        early,
        grad_w_out,
        small,
        dq,
        dk,
        dv,
        group_tokens,
        w_qkv,
        grad_pre1,
    )
    wide = jnp.float32
    outer = lax.axis_size("batch") // BLOCK8
    if outer > 1:
        groups = [[o * BLOCK8 + i for o in range(outer)] for i in range(BLOCK8)]
        grads = lax.psum(grads.astype(wide), "batch", axis_index_groups=groups)
        sums = lax.psum(sums, "batch", axis_index_groups=groups)
    if outer > 1:
        grads = grads.astype(low)
    full_in, full_back, full_qkv, full_out = widen(grads)
    return (
        layer_out,
        grad_tokens,
        full_qkv,
        full_out,
        sums[0],
        sums[1],
        sums[2],
        full_in,
        sums[6:10].reshape(b_in.shape),
        full_back,
        sums[3],
        sums[4],
        sums[5],
    )


def solution(mesh):
    rows = P(("batch", "seq"), None)
    whole = P()
    placed = (rows, P("batch"), P("batch", None), P("batch", None, None)) + (whole,) * 11 + (rows,)
    return jax.shard_map(
        per_device,
        mesh=mesh,
        in_specs=placed,
        out_specs=(rows, rows) + (whole,) * 11,
        check_vma=False,
    )
```

```python
import functools
import jax
import jax.numpy as jnp
from jax import lax
from jax.sharding import PartitionSpec as P
from jax.experimental import pallas as pl
from jax.experimental.pallas import tpu as pltpu

HEADS = 12
HEAD = 64
BLOCK = 64
SHORT = 1024
LISTED = 8
QUAD = 4
WIDE = QUAD * HEAD
SPAN = LISTED * BLOCK
MASKED = -1e30
NORM_EPS = 1e-06
NT = (((1,), (1,)), ((), ()))
TN = (((0,), (0,)), ((), ()))


def dot(a, b, dims=(((1,), (0,)), ((), ()))):
    return lax.dot_general(a, b, dims, preferred_element_type=jnp.float32)


def stack_heads(rows, head_mask):
    return jnp.concatenate([rows] * QUAD, axis=0) * head_mask


def pick_heads(full, lane_head):
    out = full[0:BLOCK]
    for h in range(1, QUAD):
        out = jnp.where(lane_head == h, full[h * BLOCK : (h + 1) * BLOCK], out)
    return out


def masked_span(scores, row_id, limits):
    parts = []
    for j in range(LISTED):
        parts.append(
            jnp.where(row_id < limits[j], scores[j * BLOCK : (j + 1) * BLOCK], MASKED)
        )
    return jnp.concatenate(parts, axis=0)


class Layout:
    def __init__(self, blocks, nblocks, bucket_ref, length_ref, random_ref):
        self.first_own = lax.axis_index("seq") * blocks
        self.nblocks, self.short = nblocks, SHORT // BLOCK
        self.is_long = bucket_ref[0] > 0
        self.length_ref, self.random_ref = length_ref, random_ref

    def sequence(self, b):
        own = self.first_own + b
        member = jnp.where(self.is_long, 0, own // self.short)
        first = member * self.short
        span = jnp.where(self.is_long, self.nblocks, self.short)
        return own, first, first + span - 1, self.length_ref[0, member]

    def listed(self, b):
        own, first, last, valid = self.sequence(b)
        starts, limits = [], []
        ids = [own - 1, own, own + 1]
        ids += [self.random_ref[0, own, j] for j in range(3)]
        ids += [first, last]
        for j, block in enumerate(ids):
            inside = (block >= first) & (block <= last)
            if j >= 6:
                inside = inside & (jnp.abs(block - own) > 1)
            limits.append(jnp.where(inside, valid - (block - first) * BLOCK, 0))
            block = jnp.minimum(jnp.maximum(block, 0), self.nblocks - 1)
            starts.append(pl.multiple_of(block * BLOCK, BLOCK))
        return starts, limits

    def whole(self, b):
        own, first, last, valid = self.sequence(b)
        chunks = jnp.where(self.is_long, self.nblocks // self.short, 1)
        return (own == first) | (own == last), first * BLOCK, chunks, valid


def fill_head_mask(hm_ref):
    r = lax.broadcasted_iota(jnp.int32, (WIDE, WIDE), 0) // HEAD
    c = lax.broadcasted_iota(jnp.int32, (WIDE, WIDE), 1) // HEAD
    hm_ref[...] = jnp.where(r == c, 1.0, 0.0).astype(jnp.bfloat16)


def attend_kernel(
    blocks, bucket_ref, length_ref, random_ref, q_ref, k_ref, v_ref, o_ref, l_ref, kcat, vcat, hm_ref,
):
    layout = Layout(blocks, k_ref.shape[0] // BLOCK, bucket_ref, length_ref, random_ref)
    fill_head_mask(hm_ref)
    row_id = lax.broadcasted_iota(jnp.int32, (BLOCK, WIDE), 0)
    lane_head = lax.broadcasted_iota(jnp.int32, (BLOCK, WIDE), 1) // HEAD
    chunk_row = lax.broadcasted_iota(jnp.int32, (SHORT, WIDE), 0)

    def one_block(b, carry):
        rows = pl.ds(pl.multiple_of(b * BLOCK, BLOCK), BLOCK)
        qm = stack_heads(q_ref[rows, :], hm_ref[...])
        starts, limits = layout.listed(b)
        for j in range(LISTED):
            src = pl.ds(starts[j], BLOCK)
            kcat[j * BLOCK : (j + 1) * BLOCK, :] = k_ref[src, :]
            vcat[j * BLOCK : (j + 1) * BLOCK, :] = v_ref[src, :]
        scores = masked_span(dot(kcat[...], qm, NT), row_id, limits)
        top = jnp.max(scores, axis=0, keepdims=True)
        grown = jnp.exp(scores - top)
        total = jnp.sum(grown, axis=0, keepdims=True)
        weights = (grown * (1.0 / total)).astype(jnp.bfloat16)
        full = dot(weights, vcat[...], TN)
        o_ref[rows, :] = pick_heads(full, lane_head).astype(jnp.bfloat16)
        l_ref[0, pl.ds(b, 1), :] = top + jnp.log(total)
        return carry

    lax.fori_loop(0, blocks, one_block, 0, unroll=UNROLL_F)

    def one_global(b, carry):
        is_whole, first, chunks, valid = layout.whole(b)

        @pl.when(is_whole)
        def _():
            rows = pl.ds(pl.multiple_of(b * BLOCK, BLOCK), BLOCK)
            qm = stack_heads(q_ref[rows, :], hm_ref[...])

            def attend_whole(count):
                spans = [
                    pl.ds(pl.multiple_of(first + c * SHORT, BLOCK), SHORT) for c in range(count)
                ]
                scores = [
                    jnp.where(chunk_row < valid - c * SHORT, dot(k_ref[spans[c], :], qm, NT), MASKED)
                    for c in range(count)
                ]
                top = functools.reduce(
                    jnp.maximum, [jnp.max(value, axis=0, keepdims=True) for value in scores]
                )
                total, full = 0.0, 0.0
                for c in range(count):
                    grown = jnp.exp(scores[c] - top)
                    total = total + jnp.sum(grown, axis=0, keepdims=True)
                    full = full + dot(v_ref[spans[c], :], grown.astype(jnp.bfloat16), TN)
                full = (full * (1.0 / total)).T
                o_ref[rows, :] = pick_heads(full, lane_head).astype(jnp.bfloat16)
                l_ref[0, pl.ds(b, 1), :] = top + jnp.log(total)

            pl.when(layout.is_long)(lambda: attend_whole(layout.nblocks // layout.short))
            pl.when(jnp.logical_not(layout.is_long))(lambda: attend_whole(1))

        return carry

    lax.fori_loop(0, blocks, one_global, 0)

UNROLL_F = 12
UNROLL_B = 6

def smem():
    return pl.BlockSpec(memory_space=pltpu.SMEM)


def attend(layout, queries, kv):
    rows, feat = queries.shape
    keys = kv.shape[0]
    quads = feat // WIDE
    blocks = rows // BLOCK
    pad_blocks = -(-blocks // 8) * 8
    return pl.pallas_call(
        functools.partial(attend_kernel, blocks),
        grid=(quads,),
        out_shape=(
            jax.ShapeDtypeStruct((rows, feat), jnp.bfloat16),
            jax.ShapeDtypeStruct((quads, pad_blocks, WIDE), jnp.float32),
        ),
        in_specs=[
            smem(),
            smem(),
            smem(),
            pl.BlockSpec((rows, WIDE), lambda i: (0, i)),
            pl.BlockSpec((keys, WIDE), lambda i: (0, i)),
            pl.BlockSpec((keys, WIDE), lambda i: (0, i + quads)),
        ],
        out_specs=[
            pl.BlockSpec((rows, WIDE), lambda i: (0, i)),
            pl.BlockSpec((1, pad_blocks, WIDE), lambda i: (i, 0, 0)),
        ],
        scratch_shapes=[
            pltpu.VMEM((SPAN, WIDE), jnp.bfloat16),
            pltpu.VMEM((SPAN, WIDE), jnp.bfloat16),
            pltpu.VMEM((WIDE, WIDE), jnp.bfloat16),
        ],
        compiler_params=pltpu.CompilerParams(vmem_limit_bytes=56 * 2**20),
        name="attend",
    )(*layout, queries, kv, kv)


def attend_back_kernel(
    blocks, bucket_ref, length_ref, random_ref, q_ref, k_ref, v_ref, g_ref, o_ref, l_ref,
    dq_ref, dk_ref, dv_ref, kcat, vcat, dk_sum, dv_sum, acc, hm_ref,
):
    layout = Layout(blocks, k_ref.shape[0] // BLOCK, bucket_ref, length_ref, random_ref)
    fill_head_mask(hm_ref)
    row_id = lax.broadcasted_iota(jnp.int32, (BLOCK, WIDE), 0)
    lane_head = lax.broadcasted_iota(jnp.int32, (BLOCK, WIDE), 1) // HEAD
    chunk_row = lax.broadcasted_iota(jnp.int32, (SHORT, WIDE), 0)
    dk_sum[...] = jnp.zeros_like(dk_sum)
    dv_sum[...] = jnp.zeros_like(dv_sum)
    factor = HEAD ** (-0.5)

    def one_block(b, carry):
        rows = pl.ds(pl.multiple_of(b * BLOCK, BLOCK), BLOCK)
        keep = jnp.where(layout.whole(b)[0], 0.0, 1.0).astype(jnp.bfloat16)
        qm = stack_heads(q_ref[rows, :], hm_ref[...])
        gm = stack_heads(g_ref[rows, :] * keep, hm_ref[...])
        starts, limits = layout.listed(b)
        for j in range(LISTED):
            kcat[j * BLOCK : (j + 1) * BLOCK, :] = k_ref[pl.ds(starts[j], BLOCK), :]
            vcat[j * BLOCK : (j + 1) * BLOCK, :] = v_ref[pl.ds(starts[j], BLOCK), :]
        scores = masked_span(dot(kcat[...], qm, NT), row_id, limits)
        chance = jnp.exp(scores - l_ref[0, pl.ds(b, 1), :])
        grad_w = dot(vcat[...], gm, NT)
        mean = jnp.sum(chance * grad_w, axis=0, keepdims=True)
        grad_s = (chance * (grad_w - mean)).astype(jnp.bfloat16)
        dk_part = dot(grad_s, qm)
        dv_part = dot(chance.astype(jnp.bfloat16), gm)
        for j in range(LISTED):
            dst = pl.ds(starts[j], BLOCK)
            dk_sum[dst, :] += dk_part[j * BLOCK : (j + 1) * BLOCK]
            dv_sum[dst, :] += dv_part[j * BLOCK : (j + 1) * BLOCK]
        full = dot(grad_s, kcat[...], TN)
        dq_ref[rows, :] = (pick_heads(full, lane_head) * factor).astype(jnp.bfloat16)
        return carry

    lax.fori_loop(0, blocks, one_block, 0, unroll=UNROLL_B)

    def one_global(b, carry):
        is_whole, first, chunks, valid = layout.whole(b)

        @pl.when(is_whole)
        def _():
            rows = pl.ds(pl.multiple_of(b * BLOCK, BLOCK), BLOCK)
            qm = stack_heads(q_ref[rows, :], hm_ref[...])
            gm = stack_heads(g_ref[rows, :], hm_ref[...])
            log_total = l_ref[0, pl.ds(b, 1), :]
            both = (g_ref[rows, :].astype(jnp.float32) * o_ref[rows, :].astype(jnp.float32)).T
            mean = jnp.concatenate(
                [
                    jnp.sum(both[h * HEAD : (h + 1) * HEAD], axis=0, keepdims=True)
                    for h in range(QUAD)
                ],
                axis=1,
            )
            acc[...] = jnp.zeros_like(acc)

            def one_chunk(c, carry):
                src = pl.ds(pl.multiple_of(first + c * SHORT, BLOCK), SHORT)
                scores = dot(k_ref[src, :], qm, NT)
                scores = jnp.where(chunk_row < valid - c * SHORT, scores, MASKED)
                chance = jnp.exp(scores - log_total)
                grad_w = dot(v_ref[src, :], gm, NT)
                grad_s = (chance * (grad_w - mean)).astype(jnp.bfloat16)
                dk_sum[src, :] += dot(grad_s, qm)
                dv_sum[src, :] += dot(chance.astype(jnp.bfloat16), gm)
                acc[...] += dot(grad_s, k_ref[src, :], TN)
                return carry

            lax.fori_loop(0, chunks, one_chunk, 0)
            dq_ref[rows, :] = (pick_heads(acc[...], lane_head) * factor).astype(jnp.bfloat16)

        return carry

    lax.fori_loop(0, blocks, one_global, 0)
    dk_ref[...] = dk_sum[...].astype(jnp.bfloat16)
    dv_ref[...] = dv_sum[...].astype(jnp.bfloat16)


def attend_back(layout, queries, kv, grads, mixed, logs):
    rows, feat = queries.shape
    keys = kv.shape[0]
    quads = feat // WIDE
    blocks = rows // BLOCK
    pad_blocks = logs.shape[1]
    row_spec = pl.BlockSpec((rows, WIDE), lambda i: (0, i))
    key_spec = pl.BlockSpec((keys, WIDE), lambda i: (0, i))
    return pl.pallas_call(
        functools.partial(attend_back_kernel, blocks),
        grid=(quads,),
        out_shape=(
            jax.ShapeDtypeStruct((rows, feat), jnp.bfloat16),
            jax.ShapeDtypeStruct((keys, feat), jnp.bfloat16),
            jax.ShapeDtypeStruct((keys, feat), jnp.bfloat16),
        ),
        in_specs=[
            smem(),
            smem(),
            smem(),
            row_spec,
            key_spec,
            pl.BlockSpec((keys, WIDE), lambda i: (0, i + quads)),
            row_spec,
            row_spec,
            pl.BlockSpec((1, pad_blocks, WIDE), lambda i: (i, 0, 0)),
        ],
        out_specs=[row_spec, key_spec, key_spec],
        scratch_shapes=[
            pltpu.VMEM((SPAN, WIDE), jnp.bfloat16),
            pltpu.VMEM((SPAN, WIDE), jnp.bfloat16),
            pltpu.VMEM((keys, WIDE), jnp.float32),
            pltpu.VMEM((keys, WIDE), jnp.float32),
            pltpu.VMEM((WIDE, WIDE), jnp.float32),
            pltpu.VMEM((WIDE, WIDE), jnp.bfloat16),
        ],
        compiler_params=pltpu.CompilerParams(vmem_limit_bytes=56 * 2**20),
        name="attend_back",
    )(*layout, queries, kv, kv, grads, mixed, logs)


BLOCK8 = 8


def grid_place():
    batch, seq = lax.axis_index("batch"), lax.axis_index("seq")
    inner = lax.rem(batch, BLOCK8)
    base = batch - inner
    x, z = lax.rem(inner, 2), lax.div(inner, 2)
    core, y = lax.rem(seq, 2), lax.div(seq, 2)
    near, far = lax.rem(z, 2), lax.div(z, 2)

    def device(core=core, x=x, y=y, near=near, far=far):
        return (base + (far * 2 + near) * 2 + x, y * 2 + core)

    return core, x, y, near, far, device


class Copies:
    def __init__(self, send_sem, recv_sem, local_sem):
        self.send_sem, self.recv_sem, self.local_sem = send_sem, recv_sem, local_sem
        self.sent, self.held, self.started = 0, 0, []

    def send(self, src, dst, other, keep=True):
        copy = pltpu.make_async_remote_copy(
            src_ref=src,
            dst_ref=dst,
            send_sem=self.send_sem.at[self.sent],
            recv_sem=self.recv_sem.at[self.sent],
            device_id=other,
            device_id_type=pl.DeviceIdType.MESH,
        )
        self.sent += 1
        copy.start()
        if keep:
            self.started.append(copy)
        return copy

    def local(self, src, dst):
        copy = pltpu.make_async_copy(src, dst, self.local_sem.at[self.held])
        self.held += 1
        copy.start()
        return copy

    def finish(self):
        for copy in self.started:
            copy.wait_send()


def greet(partners):
    barrier = pltpu.get_barrier_semaphore()
    for other in partners:
        pl.semaphore_signal(barrier, inc=1, device_id=other, device_id_type=pl.DeviceIdType.MESH)
    pl.semaphore_wait(barrier, len(partners))


def add_rows(dst, src, step=64):
    count, lead = dst.shape[-2], dst.shape[:-2]
    step = step if count % step == 0 else step // 2

    def one(i, carry):
        at = pl.ds(pl.multiple_of(i * step, step), step)
        if len(lead) == 0:
            dst[at, :] = dst[at, :] + src[at, :]
        elif len(lead) == 1:
            for a in range(lead[0]):
                dst[a, at, :] = dst[a, at, :] + src[a, at, :]
        else:
            for a in range(lead[0]):
                for b in range(lead[1]):
                    dst[a, b, at, :] = dst[a, b, at, :] + src[a, b, at, :]
        return carry

    lax.fori_loop(0, count // step, one, 0)


def region(fixed, half):
    first = fixed["x"] if "x" in fixed else slice(None)
    second = fixed["y"] if "y" in fixed else slice(None)
    count, start = half, 0
    if "near" in fixed:
        count = half // 2
        start = fixed["near"] * count
    if "far" in fixed:
        start = start + fixed["far"] * (count // 2)
        count = count // 2
    rows = pl.ds(start if isinstance(start, int) else pl.multiple_of(start, count), count)
    return first, second, rows


def region_shape(names, half):
    lead = tuple(2 for name in ("x", "y") if name not in names)
    rows = half // (2 if "near" in names else 1) // (2 if "far" in names else 1)
    return lead + (rows,)


def step_shapes(half, plan, steps=4):
    return [
        region_shape(names[: s + 1], half) + (stop - start,)
        for names, start, stop in plan
        for s in range(steps)
    ]


class Loaded:
    def __init__(self, copy):
        self.copy = copy

    def wait_recv(self):
        self.copy.wait()


class Rings:
    def __init__(self, copies, half, plan, bits, device, got):
        self.copies, self.half, self.bits, self.device, self.got = copies, half, bits, device, got
        self.names = [names for names, start, stop in plan]
        self.columns = [pl.ds(start, stop - start) for names, start, stop in plan]

    def other(self, name):
        return self.device(**{name: 1 - self.bits[name]})

    def part(self, ref, fixed, p, offset=0):
        first, second, rows = region(fixed, self.half)
        if not isinstance(offset, int):
            start = rows.start + offset
            rows = pl.ds(pl.multiple_of(start, rows.size), rows.size)
        return ref.at[first, second, rows, self.columns[p]]

    def fixed(self, p, s, flip=False):
        names = self.names[p][: s + 1]
        result = {name: self.bits[name] for name in names}
        if flip:
            result[names[-1]] = 1 - result[names[-1]]
        return result

    def spread(self, out, p, s, offset):
        place = self.part(out, self.fixed(p, s), p, offset)
        return self.copies.send(place, place, self.other(self.names[p][s]))


def finish_kernel(
    plan, plan_q, order, work_hbm, *refs,
):
    early_got, refs = refs[: len(plan)], refs[len(plan) :]
    (w_out_ref, small_ref, dq_hbm, dk_hbm, dv_hbm,
     tok_hbm, w_hbm, pre_ref, out_ref, gtok_ref, sum_ref, work, got0, *rest) = refs
    steps_f, steps_q = 4 * len(plan), 4 * len(plan_q)
    got, got_q, rest = rest[:steps_f], rest[steps_f : steps_f + steps_q], rest[steps_f + steps_q :]
    (slabs, part, part_in, total_ref, small_in, dq_ref, dk_ref, dv_ref, tok_ref, w_ref,
     send_sem, recv_sem, local_sem) = rest
    core, x, y, near, far, device = grid_place()
    bits = {"x": x, "y": y, "near": near, "far": far}
    seq = lax.axis_index("seq")
    sibling = device(core=1 - core)
    others = {name: device(**{name: 1 - bits[name]}) for name in bits}
    copies = Copies(send_sem, recv_sem, local_sem)
    rows, feat = gtok_ref.shape
    half = rows // 2
    rings = Rings(copies, half, plan, bits, device, got)
    rings_q = Rings(copies, half, plan_q, bits, device, got_q)
    moves = {}
    early = []
    for k in range(2):
        early.append(copies.local(work_hbm.at[k], work.at[k]))
        for p, src in enumerate(early_got):
            moves[k, p, 0] = Loaded(copies.local(src.at[k], got[p * 4].at[k]))
    loads = {
        name: copies.local(src, dst)
        for name, src, dst in (
            ("w", w_hbm, w_ref), ("dk", dk_hbm, dk_ref), ("dv", dv_hbm, dv_ref),
            ("tok", tok_hbm, tok_ref), ("dq", dq_hbm, dq_ref), ("pre", pre_ref, total_ref),
        )
    }
    loaded = set()

    def need(*wanted):
        for name in wanted:
            if name not in loaded:
                loads[name].wait()
                loaded.add(name)

    greet([sibling] + list(others.values()))
    mine = pl.multiple_of(core * half, half)
    theirs = pl.multiple_of((1 - core) * half, half)

    def lane(k):
        return (rings, k) if k < 2 else (rings_q, 0)

    def reduce_send(k, p, s):
        ring, slot = lane(k)
        moves[k, p, s] = copies.send(
            ring.part(work.at[k], ring.fixed(p, s, True), p),
            ring.got[p * 4 + s].at[slot],
            others[ring.names[p][s]],
        )

    def reduce_step(k, p, s):
        ring, slot = lane(k)
        moves[k, p, s - 1].wait_recv()
        add_rows(ring.part(work.at[k], ring.fixed(p, s - 1), p), ring.got[p * 4 + s - 1].at[slot])
        if s < 4:
            reduce_send(k, p, s)

    def spread_start(k, p):
        reduce_step(k, p, 4)
        ring = lane(k)[0]
        src = ring.part(work.at[k], ring.fixed(p, 3), p)
        dst = ring.part(out_ref.at[k], ring.fixed(p, 3), p, mine)
        moves[k, p, "own"] = copies.local(src, dst)
        moves[k, p, 3] = copies.send(src, dst, others["far"])

    def spread_step(k, p, s):
        moves[k, p, s + 1].wait_recv()
        if s == 2:
            moves[k, p, "own"].wait()
        moves[k, p, s] = lane(k)[0].spread(out_ref.at[k], p, s, mine)

    def spread_cores(k, p):
        moves[k, p, 0].wait_recv()
        place = out_ref.at[k, :, :, pl.ds(mine, half), lane(k)[0].columns[p]]
        moves[k, p, "end"] = copies.send(place, place, sibling)

    small_partners = [sibling] + [others[name] for name in ("x", "y", "near", "far")]

    def small_step(s):
        moves["small"] = copies.send(
            sum_ref if s else small_ref, small_in.at[s], small_partners[s], False
        )

    def small_add(s):
        moves["small"].wait()
        sum_ref[...] = (sum_ref if s else small_ref)[...] + small_in[s]
        if s < 4:
            small_step(s + 1)

    def token_part(py, pc):
        need("w", "dk", "dv")
        at = pl.ds(pl.multiple_of((py * 2 + pc) * rows, rows), rows)
        return dot(dk_ref[at, :], w_ref[:, feat : 2 * feat], NT) + dot(
            dv_ref[at, :], w_ref[:, 2 * feat : 3 * feat], NT
        )

    def weights(n, at, columns):
        if n == 0:
            need("tok", "dq")
            own_tokens = pl.ds(pl.multiple_of(seq * rows, rows), rows)
            value = dot(tok_ref[at, own_tokens], dq_ref[:, columns])
        else:
            need("tok", "dk" if n == 1 else "dv")
            value = dot(tok_ref[at, :], (dk_ref if n == 1 else dv_ref)[:, columns])
        return value.astype(jnp.bfloat16)

    def weights_away(p):
        columns = rings_q.columns[p]
        for n in range(3):
            slabs[n, :, columns] = weights(n, pl.ds(theirs, half), columns)
        moves["q", p] = copies.send(slabs.at[:, :, columns], got0.at[0:3, :, columns], sibling)

    def weights_here(p):
        columns = rings_q.columns[p]
        for n in range(3):
            work[2, n // 2, n % 2, :, columns] = weights(n, pl.ds(mine, half), columns)
        if "out" in moves:
            out_here.wait()
            moves.pop("out").wait_recv()
        moves["q", p].wait_recv()
        for n in range(4):
            add_rows(work.at[2, n // 2, n % 2, :, columns], got0.at[n, :, columns])
        reduce_send(2, p, 0)

    def tokens_far():
        part[0] = token_part(1 - y, 1 - core).astype(jnp.bfloat16)
        moves["far"] = copies.send(part.at[0], part_in.at[0], sibling)

    def tokens_near():
        part[1] = token_part(y, 1 - core).astype(jnp.bfloat16)
        moves["near"] = copies.send(part.at[1], part_in.at[1], sibling)

    def tokens_cross():
        part[2] = token_part(1 - y, core).astype(jnp.bfloat16)
        moves["far"].wait_recv()
        add_rows(part.at[2], part_in.at[0])
        moves["cross"] = copies.send(part.at[2], part_in.at[2], others["y"])

    def tokens_own():
        need("w", "pre", "dq")
        total_ref[...] = (
            total_ref[...] + dot(dq_ref[...], w_ref[:, 0:feat], NT) + token_part(y, core)
        )

    def tokens_end():
        moves["near"].wait_recv()
        moves["cross"].wait_recv()
        gtok_ref[...] = (
            total_ref[...] + part_in[1].astype(jnp.float32) + part_in[2].astype(jnp.float32)
        ).astype(jnp.bfloat16)

    moves["out"] = copies.send(w_out_ref.at[pl.ds(theirs, half), :], got0.at[3], sibling)
    out_here = copies.local(w_out_ref.at[pl.ds(mine, half), :], work.at[2, 1, 1])
    small_step(0)
    for k in range(2):
        early[k].wait()
        for p in range(len(plan)):
            reduce_step(k, p, 1)
    steps = {
        "add": reduce_step, "top": spread_start, "out": spread_step, "end": spread_cores,
        "small": small_add, "wa": weights_away, "wh": weights_here, "far": tokens_far,
        "near": tokens_near, "cross": tokens_cross, "own": tokens_own, "last": tokens_end,
    }
    for name, *values in order:
        steps[name](*values)
    for k in range(3):
        for p in range(len(lane(k)[0].names)):
            moves[k, p, "end"].wait_recv()
    copies.finish()


PLAN = (
    (("near", "x", "y", "far"), 0, 256),
    (("y", "near", "x", "far"), 256, 512),
    (("x", "y", "near", "far"), 512, 768),
)
PLAN_Q = (
    (("near", "x", "y", "far"), 0, 256),
    (("x", "near", "y", "far"), 256, 512),
    (("near", "y", "x", "far"), 512, 640),
    (("y", "x", "near", "far"), 640, 768),
)
ORDER = (
    ("far",), ("small", 0), ("wa", 0), ("add", 0, 0, 2), ("add", 0, 1, 2), ("add", 0, 2, 2),
    ("wh", 0), ("add", 1, 0, 2), ("add", 1, 1, 2), ("small", 1), ("cross",), ("add", 1, 2, 2),
    ("wa", 1), ("add", 0, 0, 3), ("add", 0, 1, 3), ("add", 0, 2, 3), ("small", 2), ("wh", 1),
    ("add", 2, 0, 1), ("add", 1, 0, 3), ("add", 1, 1, 3), ("add", 1, 2, 3), ("wa", 2),
    ("top", 0, 0), ("wh", 2), ("top", 0, 1), ("top", 0, 2), ("small", 3), ("wa", 3),
    ("top", 1, 0), ("wh", 3), ("add", 2, 1, 1), ("top", 1, 1), ("top", 1, 2), ("near",),
    ("add", 2, 0, 2), ("add", 2, 2, 1), ("out", 0, 1, 2), ("own",), ("add", 2, 1, 2),
    ("out", 0, 2, 2), ("out", 0, 1, 1), ("small", 4), ("last",), ("out", 0, 0, 2),
    ("add", 2, 3, 1), ("out", 1, 1, 2), ("out", 1, 0, 2), ("add", 2, 0, 3), ("out", 1, 2, 2),
    ("out", 0, 2, 1), ("add", 2, 2, 2), ("add", 2, 3, 2), ("add", 2, 1, 3), ("out", 0, 1, 0),
    ("out", 1, 1, 1), ("out", 0, 0, 1), ("add", 2, 2, 3), ("top", 2, 0), ("out", 1, 0, 1),
    ("add", 2, 3, 3), ("top", 2, 1), ("out", 0, 2, 0), ("out", 1, 2, 1), ("out", 0, 0, 0),
    ("top", 2, 2), ("out", 2, 0, 2), ("top", 2, 3), ("out", 2, 1, 2), ("out", 1, 0, 0),
    ("end", 0, 1), ("out", 1, 1, 0), ("out", 1, 2, 0), ("end", 0, 2), ("end", 0, 0),
    ("out", 2, 0, 1), ("out", 2, 2, 2), ("out", 2, 3, 2), ("out", 2, 1, 1), ("end", 1, 0),
    ("end", 1, 2), ("out", 2, 3, 1), ("end", 1, 1), ("out", 2, 0, 0), ("out", 2, 1, 0),
    ("out", 2, 2, 1), ("out", 2, 3, 0), ("out", 2, 2, 0), ("end", 2, 3), ("end", 2, 0),
    ("end", 2, 1), ("end", 2, 2),
)


def finish(work, early, w_out_grad, small, dq, dk, dv, flipped_tokens, w_qkv, grad_pre1):
    rows, feat = dq.shape
    half = rows // 2
    low = jnp.bfloat16
    vmem = pl.BlockSpec(memory_space=pltpu.VMEM)
    anywhere = pl.BlockSpec(memory_space=pl.ANY)
    return pl.pallas_call(
        functools.partial(finish_kernel, PLAN, PLAN_Q, ORDER),
        out_shape=(
            jax.ShapeDtypeStruct((3, 2, 2, rows, feat), low),
            jax.ShapeDtypeStruct((rows, feat), low),
            jax.ShapeDtypeStruct(small.shape, jnp.float32),
        ),
        in_specs=[anywhere] * (2 + len(PLAN)) + [vmem] + [anywhere] * 6,
        out_specs=(anywhere, vmem, vmem),
        scratch_shapes=[
            pltpu.VMEM((3, 2, 2, half, feat), low),
            pltpu.VMEM((4, half, feat), low),
        ]
        + [pltpu.VMEM((2,) + shape, low) for shape in step_shapes(half, PLAN)]
        + [pltpu.VMEM((1,) + shape, low) for shape in step_shapes(half, PLAN_Q)]
        + [
            pltpu.VMEM((3, half, feat), low),
            pltpu.VMEM((3, rows, feat), low),
            pltpu.VMEM((3, rows, feat), low),
            pltpu.VMEM((rows, feat), jnp.float32),
            pltpu.VMEM((5,) + small.shape, jnp.float32),
            pltpu.VMEM(dq.shape, low),
            pltpu.VMEM(dk.shape, low),
            pltpu.VMEM(dv.shape, low),
            pltpu.VMEM(flipped_tokens.shape, low),
            pltpu.VMEM(w_qkv.shape, low),
            pltpu.SemaphoreType.DMA((128,)),
            pltpu.SemaphoreType.DMA((128,)),
            pltpu.SemaphoreType.DMA((32,)),
        ],
        compiler_params=pltpu.CompilerParams(
            collective_id=0, has_side_effects=True, vmem_limit_bytes=60 * 2**20
        ),
        name="finish",
    )(work, *early, w_out_grad, small, dq, dk, dv, flipped_tokens, w_qkv, grad_pre1)


def widen_kernel(in_ref, back_ref, last_ref, in_out, back_out, qkv_out, out_out):
    in_out[...] = in_ref[0, 0, 0].astype(jnp.float32)
    back_out[...] = back_ref[0, 0, 0].astype(jnp.float32)
    last = last_ref[0, 0, 0].astype(jnp.float32)

    @pl.when(pl.program_id(0) < 3)
    def _():
        qkv_out[...] = last

    @pl.when(pl.program_id(0) == 3)
    def _():
        out_out[...] = last


def widen(grads):
    rows, feat = grads.shape[-2:]
    step = rows // WIDEN_PARTS
    wide = jnp.float32

    def source(k):
        return pl.BlockSpec((1, 1, 1, step, feat), lambda n, i: (k, n // 2, n % 2, i, 0))

    return pl.pallas_call(
        widen_kernel,
        grid=(4, WIDEN_PARTS),
        out_shape=[
            jax.ShapeDtypeStruct((rows, 4 * feat), wide),
            jax.ShapeDtypeStruct((4 * rows, feat), wide),
            jax.ShapeDtypeStruct((rows, 3 * feat), wide),
            jax.ShapeDtypeStruct((rows, feat), wide),
        ],
        in_specs=[source(k) for k in range(3)],
        out_specs=[
            pl.BlockSpec((step, feat), lambda n, i: (i, n)),
            pl.BlockSpec((step, feat), lambda n, i: (n * WIDEN_PARTS + i, 0)),
            pl.BlockSpec(
                (step, feat),
                lambda n, i: (jnp.where(n < 3, i, WIDEN_PARTS - 1), jnp.minimum(n, 2)),
            ),
            pl.BlockSpec((step, feat), lambda n, i: (jnp.where(n < 3, 0, i), 0)),
        ],
        compiler_params=pltpu.CompilerParams(vmem_limit_bytes=56 * 2**20),
        name="widen",
    )(grads, grads, grads)


WIDEN_PARTS = 1


PIECES = 6


def front_kernel(
    tok_hbm, w_hbm, q_ref, kv_out, flip_out, all_ref, kv_ref, flip_ref, w_ref, send_sem, recv_sem, local_sem
):
    core, x, y, near, far, device = grid_place()
    sibling, over_y = device(core=1 - core), device(y=1 - y)
    low = jnp.bfloat16
    rows, feat = q_ref.shape
    piece = rows // PIECES
    copies = Copies(send_sem, recv_sem, local_sem)

    def rows_of(py, pc, i=None):
        start = (py * 2 + pc) * rows
        if i is None:
            return pl.ds(pl.multiple_of(start, rows), rows)
        return pl.ds(pl.multiple_of(start + i * piece, piece), piece)

    own = rows_of(y, core)
    load = copies.local(tok_hbm, all_ref.at[own])
    load_w = copies.local(w_hbm, w_ref)
    greet([sibling, over_y])
    crossing = []
    for i in range(PIECES):
        src = tok_hbm.at[pl.ds(i * piece, piece)]
        crossing.append(copies.send(src, all_ref.at[rows_of(y, core, i)], over_y))
    beside = copies.send(tok_hbm, all_ref.at[own], sibling)
    stores = []

    def project(at):
        kv_ref[at, :] = dot(all_ref[at, :], w_ref[:, feat:]).astype(low)
        stores.append(copies.local(kv_ref.at[at], kv_out.at[at]))
        flip_ref[:, at] = all_ref[at, :].T
        stores.append(copies.local(flip_ref.at[:, at], flip_out.at[:, at]))

    load.wait()
    load_w.wait()
    project(own)
    q_ref[...] = dot(all_ref[own, :], w_ref[:, 0:feat]).astype(low) * low(HEAD ** (-0.5))
    beside.wait_recv()
    project(rows_of(y, 1 - core))
    passed = []
    for i in range(PIECES):
        crossing[i].wait_recv()
        at = rows_of(1 - y, core, i)
        passed.append(copies.send(all_ref.at[at], all_ref.at[at], sibling))
        project(at)
        if i > 0:
            passed[i - 1].wait_recv()
            project(rows_of(1 - y, 1 - core, i - 1))
    passed[-1].wait_recv()
    project(rows_of(1 - y, 1 - core, PIECES - 1))
    for store in stores:
        store.wait()
    copies.finish()


def front(tokens, w_qkv, seq_parts):
    rows, feat = tokens.shape
    low = jnp.bfloat16
    keys = rows * seq_parts
    anywhere = pl.BlockSpec(memory_space=pl.ANY)
    count = 2 + 2 * PIECES
    return pl.pallas_call(
        front_kernel,
        out_shape=(
            jax.ShapeDtypeStruct((rows, feat), low),
            jax.ShapeDtypeStruct((keys, 2 * feat), low),
            jax.ShapeDtypeStruct((feat, keys), low),
        ),
        in_specs=[anywhere, anywhere],
        out_specs=(pl.BlockSpec(memory_space=pltpu.VMEM), anywhere, anywhere),
        scratch_shapes=[
            pltpu.VMEM((keys, feat), low),
            pltpu.VMEM((keys, 2 * feat), low),
            pltpu.VMEM((feat, keys), low),
            pltpu.VMEM(w_qkv.shape, low),
            pltpu.SemaphoreType.DMA((count,)),
            pltpu.SemaphoreType.DMA((count,)),
            pltpu.SemaphoreType.DMA((2 + 2 * count,)),
        ],
        compiler_params=pltpu.CompilerParams(
            collective_id=2, has_side_effects=True, vmem_limit_bytes=56 * 2**20
        ),
        name="front",
    )(tokens, w_qkv)


def gelu_parts(v):
    size = jnp.abs(v)
    fall = jnp.exp(-0.5 * v * v)
    t = 1.0 / (1.0 + (0.3275911 * 0.7071067811865476) * size)
    tail = 1.061405429 * t - 1.453152027
    tail = tail * t + 1.421413741
    tail = tail * t - 0.284496736
    tail = tail * t + 0.254829592
    half = 0.5 * tail * t * fall
    return jnp.where(v >= 0.0, 1.0 - half, half), fall


def row_mean(values):
    return jnp.sum(values, axis=-1, keepdims=True) * (1.0 / values.shape[-1])


def fold8(values):
    total = values[0:8]
    for i in range(1, values.shape[0] // 8):
        total = total + values[i * 8 : (i + 1) * 8]
    return total


STEP = 128
TILE = 64


def middle_kernel(
    plan, mixed_ref, tok_ref, cot_ref, *refs,
):
    vec_refs, bias_ref, refs = refs[:6], refs[6], refs[7:]
    (w_out_ref, w_in_hbm, w_back_hbm,
     out_ref, pre_ref, gmix_ref, gw_out_ref, small_ref, work_out, *refs) = refs
    away, refs = refs[: len(plan)], refs[len(plan) :]
    (w_in_ref, w_back_ref, unit, spread, hid, active, slope, acc, acc2, gsecond, gbranch,
     work, slabs, got0, send_sem, recv_sem, local_sem) = refs
    core, x, y, near, far, device = grid_place()
    sibling = device(core=1 - core)
    low = jnp.bfloat16
    rows, feat = tok_ref.shape
    half = rows // 2
    count = 4
    chunks = rows // STEP
    copies = Copies(send_sem, recv_sem, local_sem)
    load_in = copies.local(w_in_hbm, w_in_ref)
    load_back = copies.local(w_back_hbm, w_back_ref)
    greet([sibling])
    mine = pl.multiple_of(core * half, half)
    theirs = pl.multiple_of((1 - core) * half, half)

    def rows_at(i):
        return pl.ds(pl.multiple_of(i * STEP, STEP), STEP)

    def slab_at(n):
        return pl.ds(pl.multiple_of(n * feat, feat), feat)

    def vec(i):
        return vec_refs[i][...].reshape(1, feat)

    zero = jnp.zeros((8, feat), jnp.float32)

    def put(i, value):
        small_ref[i : i + 1, :] = jnp.sum(value, axis=0, keepdims=True)

    small_ref[...] = jnp.zeros_like(small_ref)

    acc[...] = dot(mixed_ref[...], w_out_ref[...])

    def norm_one(i, carry):
        at = rows_at(i)
        v = tok_ref[at, :].astype(jnp.float32) + (acc[at, :] + vec(0))
        v = v - row_mean(v)
        r = lax.rsqrt(row_mean(v * v) + NORM_EPS)
        u = v * r
        unit[at, :] = u
        spread[at, :] = jnp.broadcast_to(r, (STEP, 128))
        hid[at, :] = (u * vec(1) + vec(2)).astype(low)
        return carry

    lax.fori_loop(0, chunks, norm_one, 0)
    load_in.wait()

    group = rows // 6

    def inner_of(n, i):
        return dot(hid[i * group : (i + 1) * group, :], w_in_ref[:, n * feat : (n + 1) * feat])

    inner = [inner_of(0, i) for i in range(6)]
    load_back.wait()
    for n in range(count):
        bias = bias_ref[n * feat : (n + 1) * feat].reshape(1, feat)
        following = []
        for i in range(6):
            if n + 1 < count:
                following.append(inner_of(n + 1, i))
            for j in range(group // TILE):
                at = slice(i * group + j * TILE, i * group + (j + 1) * TILE)
                v = inner[i][j * TILE : (j + 1) * TILE] + bias
                chance, fall = gelu_parts(v)
                active[n, at, :] = (v * chance).astype(low)
                slope[n, at, :] = (chance + (v * 0.3989422804014327) * fall).astype(low)
            at = slice(i * group, (i + 1) * group)
            second = dot(active[n, at, :], w_back_ref[n * feat : (n + 1) * feat, :])
            acc2[at, :] = second if n == 0 else acc2[at, :] + second
        inner = following

    def norm_two(i, sums):
        at = rows_at(i)
        v = (unit[at, :] * vec(1) + vec(2)) + (acc2[at, :] + vec(3))
        v = v - row_mean(v)
        r = lax.rsqrt(row_mean(v * v) + NORM_EPS)
        u = v * r
        out_ref[at, :] = (u * vec(4) + vec(5)).astype(low)
        c = cot_ref[at, :].astype(jnp.float32)
        a = c * vec(4)
        g = r * (a - row_mean(a) - u * row_mean(a * u))
        acc2[at, :] = g
        g_low = g.astype(low)
        gsecond[at, :] = g_low
        return (
            sums[0] + fold8(c * u), sums[1] + fold8(c), sums[2] + fold8(g_low.astype(jnp.float32)),
        )

    sums = lax.fori_loop(0, chunks, norm_two, (zero, zero, zero))
    put(4, sums[0])
    put(5, sums[1])
    put(3, sums[2])

    def exchange(k, n):
        return pltpu.make_async_remote_copy(
            src_ref=slabs.at[k, n],
            dst_ref=got0.at[k, n],
            send_sem=send_sem.at[k * 4 + n],
            recv_sem=recv_sem.at[k * 4 + n],
            device_id=sibling,
            device_id_type=pl.DeviceIdType.MESH,
        )

    def collect(k, n):
        exchange(k, n).wait_recv()
        add_rows(work.at[k, lax.div(n, 2), lax.rem(n, 2)], got0.at[k, n])
        exchange(k, n).wait_send()

    def back_slab(n, carry):
        columns = slab_at(n)
        slabs[1, n] = dot(active[n, :, pl.ds(theirs, half)], gsecond[...], TN).astype(low)
        exchange(1, n).start()
        work[1, lax.div(n, 2), lax.rem(n, 2)] = dot(active[n, :, pl.ds(mine, half)], gsecond[...], TN).astype(low)
        gactive = dot(gsecond[...], w_back_ref[columns, :], NT)
        total = zero
        for i in range(rows // TILE):
            at = slice(i * TILE, (i + 1) * TILE)
            g = (gactive[at] * slope[n, at, :].astype(jnp.float32)).astype(low)
            slope[n, at, :] = g
            total = total + fold8(g.astype(jnp.float32))

        small_ref[pl.ds(6 + n, 1), :] = jnp.sum(total, axis=0, keepdims=True)
        slabs[0, n] = dot(hid[:, pl.ds(theirs, half)], slope[n], TN).astype(low)
        exchange(0, n).start()

        @pl.when(n > 0)
        def _():
            collect(1, n - 1)
            collect(0, n - 1)

        work[0, lax.div(n, 2), lax.rem(n, 2)] = dot(hid[:, pl.ds(mine, half)], slope[n], TN).astype(low)

        acc2[...] += dot(slope[n], w_in_ref[:, columns], NT)
        return carry

    lax.fori_loop(0, count, back_slab, 0)

    def norm_back(i, sums):
        at = rows_at(i)
        g = acc2[at, :]
        u = unit[at, :]
        r = spread[at, 0:1]
        a = g * vec(1)
        d = r * (a - row_mean(a) - u * row_mean(a * u))
        pre_ref[at, :] = d
        d_low = d.astype(low)
        gbranch[at, :] = d_low
        return (
            sums[0] + fold8(g * u), sums[1] + fold8(g), sums[2] + fold8(d_low.astype(jnp.float32)),
        )

    sums = lax.fori_loop(0, chunks, norm_back, (zero, zero, zero))
    put(1, sums[0])
    put(2, sums[1])
    put(0, sums[2])
    gmix_ref[...] = dot(gbranch[...], w_out_ref[...], NT).astype(low)
    gw_out_ref[...] = dot(mixed_ref[...], gbranch[...], TN).astype(low)

    collect(1, count - 1)
    collect(0, count - 1)
    stores = [copies.local(work, work_out)]
    bits = {"x": x, "y": y, "near": near, "far": far}
    rings = Rings(copies, half, plan, bits, device, None)
    for k in range(2):
        for p in range(len(plan)):
            stores.append(
                copies.local(rings.part(work.at[k], rings.fixed(p, 0, True), p), away[p].at[k])
            )
    for store in stores:
        store.wait()


def middle(mixed, tokens, cotangent, vectors, b_in, w_out, w_in, w_back):
    rows, feat = tokens.shape
    half = rows // 2
    low = jnp.bfloat16
    wide = jnp.float32
    vmem = pl.BlockSpec(memory_space=pltpu.VMEM)
    anywhere = pl.BlockSpec(memory_space=pl.ANY)
    full = jax.ShapeDtypeStruct((rows, feat), low)
    return pl.pallas_call(
        functools.partial(middle_kernel, PLAN),
        out_shape=(
            full,
            jax.ShapeDtypeStruct((rows, feat), wide),
            full,
            full,
            jax.ShapeDtypeStruct((16, feat), wide),
            jax.ShapeDtypeStruct((2, 2, 2, half, feat), low),
        )
        + tuple(jax.ShapeDtypeStruct((2,) + shape, low) for shape in step_shapes(half, PLAN, 1)),
        in_specs=[vmem] * 11 + [anywhere] * 2,
        out_specs=(vmem,) * 5 + (anywhere,) * (1 + len(PLAN)),
        scratch_shapes=[
            pltpu.VMEM(w_in.shape, low),
            pltpu.VMEM(w_back.shape, low),
            pltpu.VMEM((rows, feat), wide),
            pltpu.VMEM((rows, 128), wide),
            pltpu.VMEM((rows, feat), low),
            pltpu.VMEM((4, rows, feat), low),
            pltpu.VMEM((4, rows, feat), low),
            pltpu.VMEM((rows, feat), wide),
            pltpu.VMEM((rows, feat), wide),
            pltpu.VMEM((rows, feat), low),
            pltpu.VMEM((rows, feat), low),
            pltpu.VMEM((2, 2, 2, half, feat), low),
            pltpu.VMEM((2, 4, half, feat), low),
            pltpu.VMEM((2, 4, half, feat), low),
            pltpu.SemaphoreType.DMA((8,)),
            pltpu.SemaphoreType.DMA((8,)),
            pltpu.SemaphoreType.DMA((16,)),
        ],
        compiler_params=pltpu.CompilerParams(
            collective_id=1, has_side_effects=True, vmem_limit_bytes=60 * 2**20
        ),
        name="middle",
    )(mixed, tokens, cotangent, *vectors, b_in, w_out, w_in, w_back)


FLIPS = {"x": (1, 0), "y": (0, 2), "near": (2, 0)}


def trade(value, name):
    parts = lax.axis_size("seq")
    flip_b, flip_s = FLIPS[name]
    pairs = [
        (b * parts + s, (b ^ flip_b) * parts + (s ^ flip_s))
        for b in range(lax.axis_size("batch"))
        for s in range(parts)
    ]
    return lax.ppermute(value, ("batch", "seq"), pairs)


def per_device(
    tokens,
    group_bucket,
    lengths,
    random_blocks,
    w_qkv,
    w_out,
    b_out,
    norm1_gain,
    norm1_shift,
    w_in,
    b_in,
    w_back,
    b_back,
    norm2_gain,
    norm2_shift,
    cotangent,
):
    low = jnp.bfloat16
    seq_parts = lax.axis_size("seq")
    tok_rows, feat = tokens.shape
    layout = (group_bucket, lengths, random_blocks)
    queries, kv, flipped_tokens = front(tokens, w_qkv, seq_parts)
    mixed, logs = attend(layout, queries, kv)
    vectors = (b_out, norm1_gain, norm1_shift, b_back, norm2_gain, norm2_shift)
    layer_out, grad_pre1, grad_mixed, grad_w_out, small, work, *away = middle(
        mixed, tokens, cotangent, vectors, b_in, w_out, w_in, w_back
    )
    early = [trade(value, names[0]) for value, (names, _, _) in zip(away, PLAN)]
    dq, dk, dv = attend_back(layout, queries, kv, grad_mixed, mixed, logs)
    grads, grad_tokens, sums = finish(
        work,
        early,
        grad_w_out,
        small,
        dq,
        dk,
        dv,
        flipped_tokens,
        w_qkv,
        grad_pre1,
    )
    wide = jnp.float32
    outer = lax.axis_size("batch") // BLOCK8
    if outer > 1:
        groups = [[o * BLOCK8 + i for o in range(outer)] for i in range(BLOCK8)]
        grads = lax.psum(grads.astype(wide), "batch", axis_index_groups=groups)
        sums = lax.psum(sums, "batch", axis_index_groups=groups)
    if outer > 1:
        grads = grads.astype(low)
    full_in, full_back, full_qkv, full_out = widen(grads)
    return (
        layer_out,
        grad_tokens,
        full_qkv,
        full_out,
        sums[0],
        sums[1],
        sums[2],
        full_in,
        sums[6:10].reshape(b_in.shape),
        full_back,
        sums[3],
        sums[4],
        sums[5],
    )


def solution(mesh):
    rows = P(("batch", "seq"), None)
    whole = P()
    placed = (rows, P("batch"), P("batch", None), P("batch", None, None)) + (whole,) * 11 + (rows,)
    return jax.shard_map(
        per_device,
        mesh=mesh,
        in_specs=placed,
        out_specs=(rows, rows) + (whole,) * 11,
        check_vma=False,
    )
```

```python
import functools
import jax
import jax.numpy as jnp
from jax import lax
from jax.sharding import PartitionSpec as P
from jax.experimental import pallas as pl
from jax.experimental.pallas import tpu as pltpu

HEADS = 12
HEAD = 64
BLOCK = 64
SHORT = 1024
LISTED = 8
QUAD = 4
WIDE = QUAD * HEAD
SPAN = LISTED * BLOCK
MASKED = -1e30
NORM_EPS = 1e-06
NT = (((1,), (1,)), ((), ()))
TN = (((0,), (0,)), ((), ()))


def dot(a, b, dims=(((1,), (0,)), ((), ()))):
    return lax.dot_general(a, b, dims, preferred_element_type=jnp.float32)


def stack_heads(rows, head_mask):
    return jnp.concatenate([rows] * QUAD, axis=0) * head_mask


def pick_heads(full, lane_head):
    out = full[0:BLOCK]
    for h in range(1, QUAD):
        out = jnp.where(lane_head == h, full[h * BLOCK : (h + 1) * BLOCK], out)
    return out


def masked_span(scores, row_id, limits):
    parts = []
    for j in range(LISTED):
        parts.append(
            jnp.where(row_id < limits[j], scores[j * BLOCK : (j + 1) * BLOCK], MASKED)
        )
    return jnp.concatenate(parts, axis=0)


class Layout:
    def __init__(self, blocks, nblocks, bucket_ref, length_ref, random_ref):
        self.first_own = lax.axis_index("seq") * blocks
        self.nblocks, self.short = nblocks, SHORT // BLOCK
        self.is_long = bucket_ref[0] > 0
        self.length_ref, self.random_ref = length_ref, random_ref

    def sequence(self, b):
        own = self.first_own + b
        member = jnp.where(self.is_long, 0, own // self.short)
        first = member * self.short
        span = jnp.where(self.is_long, self.nblocks, self.short)
        return own, first, first + span - 1, self.length_ref[0, member]

    def listed(self, b):
        own, first, last, valid = self.sequence(b)
        starts, limits = [], []
        ids = [own - 1, own, own + 1]
        ids += [self.random_ref[0, own, j] for j in range(3)]
        ids += [first, last]
        for j, block in enumerate(ids):
            inside = (block >= first) & (block <= last)
            if j >= 6:
                inside = inside & (jnp.abs(block - own) > 1)
            limits.append(jnp.where(inside, valid - (block - first) * BLOCK, 0))
            block = jnp.minimum(jnp.maximum(block, 0), self.nblocks - 1)
            starts.append(pl.multiple_of(block * BLOCK, BLOCK))
        return starts, limits

    def whole(self, b):
        own, first, last, valid = self.sequence(b)
        chunks = jnp.where(self.is_long, self.nblocks // self.short, 1)
        return (own == first) | (own == last), first * BLOCK, chunks, valid


def split_blocks(layout, blocks, sparse_ref):
    count = jnp.int32(0)
    for b in range(blocks):
        is_whole = layout.whole(b)[0]

        @pl.when(jnp.logical_not(is_whole))
        def _():
            sparse_ref[count] = b

        count = count + jnp.where(is_whole, 0, 1)
    return count


def fill_head_mask(hm_ref):
    r = lax.broadcasted_iota(jnp.int32, (WIDE, WIDE), 0) // HEAD
    c = lax.broadcasted_iota(jnp.int32, (WIDE, WIDE), 1) // HEAD
    hm_ref[...] = jnp.where(r == c, 1.0, 0.0).astype(jnp.bfloat16)


def attend_kernel(
    blocks, bucket_ref, length_ref, random_ref, q_ref, k_ref, v_ref, o_ref, l_ref, kcat, vcat, hm_ref,
):
    layout = Layout(blocks, k_ref.shape[0] // BLOCK, bucket_ref, length_ref, random_ref)
    fill_head_mask(hm_ref)
    row_id = lax.broadcasted_iota(jnp.int32, (BLOCK, WIDE), 0)
    lane_head = lax.broadcasted_iota(jnp.int32, (BLOCK, WIDE), 1) // HEAD
    chunk_row = lax.broadcasted_iota(jnp.int32, (SHORT, WIDE), 0)

    def one_block(b, carry):
        rows = pl.ds(pl.multiple_of(b * BLOCK, BLOCK), BLOCK)
        qm = stack_heads(q_ref[rows, :], hm_ref[...])
        starts, limits = layout.listed(b)
        for j in range(LISTED):
            src = pl.ds(starts[j], BLOCK)
            kcat[j * BLOCK : (j + 1) * BLOCK, :] = k_ref[src, :]
            vcat[j * BLOCK : (j + 1) * BLOCK, :] = v_ref[src, :]
        scores = masked_span(dot(kcat[...], qm, NT), row_id, limits)
        top = jnp.max(scores, axis=0, keepdims=True)
        grown = jnp.exp(scores - top)
        total = jnp.sum(grown, axis=0, keepdims=True)
        weights = (grown * (1.0 / total)).astype(jnp.bfloat16)
        full = dot(weights, vcat[...], TN)
        o_ref[rows, :] = pick_heads(full, lane_head).astype(jnp.bfloat16)
        l_ref[0, pl.ds(b, 1), :] = top + jnp.log(total)
        return carry

    lax.fori_loop(0, blocks, one_block, 0, unroll=UNROLL_F)

    def one_global(b, carry):
        is_whole, first, chunks, valid = layout.whole(b)

        @pl.when(is_whole)
        def _():
            rows = pl.ds(pl.multiple_of(b * BLOCK, BLOCK), BLOCK)
            qm = stack_heads(q_ref[rows, :], hm_ref[...])

            def attend_whole(count):
                spans = [
                    pl.ds(pl.multiple_of(first + c * SHORT, BLOCK), SHORT) for c in range(count)
                ]
                scores = [
                    jnp.where(chunk_row < valid - c * SHORT, dot(k_ref[spans[c], :], qm, NT), MASKED)
                    for c in range(count)
                ]
                top = functools.reduce(
                    jnp.maximum, [jnp.max(value, axis=0, keepdims=True) for value in scores]
                )
                total, full = 0.0, 0.0
                for c in range(count):
                    grown = jnp.exp(scores[c] - top)
                    total = total + jnp.sum(grown, axis=0, keepdims=True)
                    full = full + dot(v_ref[spans[c], :], grown.astype(jnp.bfloat16), TN)
                full = (full * (1.0 / total)).T
                o_ref[rows, :] = pick_heads(full, lane_head).astype(jnp.bfloat16)
                l_ref[0, pl.ds(b, 1), :] = top + jnp.log(total)

            pl.when(layout.is_long)(lambda: attend_whole(layout.nblocks // layout.short))
            pl.when(jnp.logical_not(layout.is_long))(lambda: attend_whole(1))

        return carry

    lax.fori_loop(0, blocks, one_global, 0)

UNROLL_F = 12
UNROLL_B = 10

def smem():
    return pl.BlockSpec(memory_space=pltpu.SMEM)


def attend(layout, queries, kv):
    rows, feat = queries.shape
    keys = kv.shape[0]
    quads = feat // WIDE
    blocks = rows // BLOCK
    pad_blocks = -(-blocks // 8) * 8
    return pl.pallas_call(
        functools.partial(attend_kernel, blocks),
        grid=(quads,),
        out_shape=(
            jax.ShapeDtypeStruct((rows, feat), jnp.bfloat16),
            jax.ShapeDtypeStruct((quads, pad_blocks, WIDE), jnp.float32),
        ),
        in_specs=[
            smem(),
            smem(),
            smem(),
            pl.BlockSpec((rows, WIDE), lambda i: (0, i)),
            pl.BlockSpec((keys, WIDE), lambda i: (0, i)),
            pl.BlockSpec((keys, WIDE), lambda i: (0, i + quads)),
        ],
        out_specs=[
            pl.BlockSpec((rows, WIDE), lambda i: (0, i)),
            pl.BlockSpec((1, pad_blocks, WIDE), lambda i: (i, 0, 0)),
        ],
        scratch_shapes=[
            pltpu.VMEM((SPAN, WIDE), jnp.bfloat16),
            pltpu.VMEM((SPAN, WIDE), jnp.bfloat16),
            pltpu.VMEM((WIDE, WIDE), jnp.bfloat16),
        ],
        compiler_params=pltpu.CompilerParams(vmem_limit_bytes=56 * 2**20),
        name="attend",
    )(*layout, queries, kv, kv)


def attend_back_kernel(
    blocks, bucket_ref, length_ref, random_ref, q_ref, k_ref, v_ref, g_ref, l_ref,
    dq_ref, dk_ref, dv_ref, kcat, vcat, dk_sum, dv_sum, hm_ref, sparse_ref,
):
    layout = Layout(blocks, k_ref.shape[0] // BLOCK, bucket_ref, length_ref, random_ref)
    fill_head_mask(hm_ref)
    count = split_blocks(layout, blocks, sparse_ref)
    row_id = lax.broadcasted_iota(jnp.int32, (BLOCK, WIDE), 0)
    lane_head = lax.broadcasted_iota(jnp.int32, (BLOCK, WIDE), 1) // HEAD
    chunk_row = lax.broadcasted_iota(jnp.int32, (SHORT, WIDE), 0)
    dk_sum[...] = jnp.zeros_like(dk_sum)
    dv_sum[...] = jnp.zeros_like(dv_sum)
    factor = HEAD ** (-0.5)

    def one_block(t, carry):
        b = sparse_ref[t]
        rows = pl.ds(pl.multiple_of(b * BLOCK, BLOCK), BLOCK)
        qm = stack_heads(q_ref[rows, :], hm_ref[...])
        gm = stack_heads(g_ref[rows, :], hm_ref[...])
        starts, limits = layout.listed(b)
        for j in range(LISTED):
            kcat[j * BLOCK : (j + 1) * BLOCK, :] = k_ref[pl.ds(starts[j], BLOCK), :]
            vcat[j * BLOCK : (j + 1) * BLOCK, :] = v_ref[pl.ds(starts[j], BLOCK), :]
        scores = masked_span(dot(kcat[...], qm, NT), row_id, limits)
        chance = jnp.exp(scores - l_ref[0, pl.ds(b, 1), :])
        grad_w = dot(vcat[...], gm, NT)
        mean = jnp.sum(chance * grad_w, axis=0, keepdims=True)
        grad_s = (chance * (grad_w - mean)).astype(jnp.bfloat16)
        dk_part = dot(grad_s, qm)
        dv_part = dot(chance.astype(jnp.bfloat16), gm)
        for j in range(LISTED):
            dst = pl.ds(starts[j], BLOCK)
            dk_sum[dst, :] += dk_part[j * BLOCK : (j + 1) * BLOCK]
            dv_sum[dst, :] += dv_part[j * BLOCK : (j + 1) * BLOCK]
        full = dot(grad_s, kcat[...], TN)
        dq_ref[rows, :] = (pick_heads(full, lane_head) * factor).astype(jnp.bfloat16)
        return carry

    lax.fori_loop(0, blocks - 2, one_block, 0, unroll=UNROLL_B)
    lax.fori_loop(blocks - 2, count, one_block, 0)

    def one_global(b, carry):
        is_whole, first, chunks, valid = layout.whole(b)

        @pl.when(is_whole)
        def _():
            rows = pl.ds(pl.multiple_of(b * BLOCK, BLOCK), BLOCK)
            qm = stack_heads(q_ref[rows, :], hm_ref[...])
            gm = stack_heads(g_ref[rows, :], hm_ref[...])
            log_total = l_ref[0, pl.ds(b, 1), :]

            def back_whole(count):
                spans = [
                    pl.ds(pl.multiple_of(first + c * SHORT, BLOCK), SHORT) for c in range(count)
                ]
                chances, grads, mean = [], [], 0.0
                for c in range(count):
                    scores = dot(k_ref[spans[c], :], qm, NT)
                    scores = jnp.where(chunk_row < valid - c * SHORT, scores, MASKED)
                    chances.append(jnp.exp(scores - log_total))
                    grads.append(dot(v_ref[spans[c], :], gm, NT))
                    mean = mean + jnp.sum(chances[c] * grads[c], axis=0, keepdims=True)
                full = 0.0
                for c in range(count):
                    grad_s = (chances[c] * (grads[c] - mean)).astype(jnp.bfloat16)
                    dk_sum[spans[c], :] += dot(grad_s, qm)
                    dv_sum[spans[c], :] += dot(chances[c].astype(jnp.bfloat16), gm)
                    full = full + dot(grad_s, k_ref[spans[c], :], TN)
                dq_ref[rows, :] = (pick_heads(full, lane_head) * factor).astype(jnp.bfloat16)

            pl.when(layout.is_long)(lambda: back_whole(layout.nblocks // layout.short))
            pl.when(jnp.logical_not(layout.is_long))(lambda: back_whole(1))

        return carry

    lax.fori_loop(0, blocks, one_global, 0)
    dk_ref[...] = dk_sum[...].astype(jnp.bfloat16)
    dv_ref[...] = dv_sum[...].astype(jnp.bfloat16)


def attend_back(layout, queries, kv, grads, logs):
    rows, feat = queries.shape
    keys = kv.shape[0]
    quads = feat // WIDE
    blocks = rows // BLOCK
    pad_blocks = logs.shape[1]
    row_spec = pl.BlockSpec((rows, WIDE), lambda i: (0, i))
    key_spec = pl.BlockSpec((keys, WIDE), lambda i: (0, i))
    return pl.pallas_call(
        functools.partial(attend_back_kernel, blocks),
        grid=(quads,),
        out_shape=(
            jax.ShapeDtypeStruct((rows, feat), jnp.bfloat16),
            jax.ShapeDtypeStruct((keys, feat), jnp.bfloat16),
            jax.ShapeDtypeStruct((keys, feat), jnp.bfloat16),
        ),
        in_specs=[
            smem(),
            smem(),
            smem(),
            row_spec,
            key_spec,
            pl.BlockSpec((keys, WIDE), lambda i: (0, i + quads)),
            row_spec,
            pl.BlockSpec((1, pad_blocks, WIDE), lambda i: (i, 0, 0)),
        ],
        out_specs=[row_spec, key_spec, key_spec],
        scratch_shapes=[
            pltpu.VMEM((SPAN, WIDE), jnp.bfloat16),
            pltpu.VMEM((SPAN, WIDE), jnp.bfloat16),
            pltpu.VMEM((keys, WIDE), jnp.float32),
            pltpu.VMEM((keys, WIDE), jnp.float32),
            pltpu.VMEM((WIDE, WIDE), jnp.bfloat16),
            pltpu.SMEM((blocks,), jnp.int32),
        ],
        compiler_params=pltpu.CompilerParams(vmem_limit_bytes=56 * 2**20),
        name="attend_back",
    )(*layout, queries, kv, kv, grads, logs)


BLOCK8 = 8


def grid_place():
    batch, seq = lax.axis_index("batch"), lax.axis_index("seq")
    inner = lax.rem(batch, BLOCK8)
    base = batch - inner
    x, z = lax.rem(inner, 2), lax.div(inner, 2)
    core, y = lax.rem(seq, 2), lax.div(seq, 2)
    near, far = lax.rem(z, 2), lax.div(z, 2)

    def device(core=core, x=x, y=y, near=near, far=far):
        return (base + (far * 2 + near) * 2 + x, y * 2 + core)

    return core, x, y, near, far, device


class Copies:
    def __init__(self, send_sem, recv_sem, local_sem):
        self.send_sem, self.recv_sem, self.local_sem = send_sem, recv_sem, local_sem
        self.sent, self.held, self.started = 0, 0, []

    def send(self, src, dst, other, keep=True):
        copy = pltpu.make_async_remote_copy(
            src_ref=src,
            dst_ref=dst,
            send_sem=self.send_sem.at[self.sent],
            recv_sem=self.recv_sem.at[self.sent],
            device_id=other,
            device_id_type=pl.DeviceIdType.MESH,
        )
        self.sent += 1
        copy.start()
        if keep:
            self.started.append(copy)
        return copy

    def local(self, src, dst):
        copy = pltpu.make_async_copy(src, dst, self.local_sem.at[self.held])
        self.held += 1
        copy.start()
        return copy

    def finish(self):
        for copy in self.started:
            copy.wait_send()


def greet(partners):
    barrier = pltpu.get_barrier_semaphore()
    for other in partners:
        pl.semaphore_signal(barrier, inc=1, device_id=other, device_id_type=pl.DeviceIdType.MESH)
    pl.semaphore_wait(barrier, len(partners))


def add_rows(dst, src, step=64):
    count, lead = dst.shape[-2], dst.shape[:-2]
    step = step if count % step == 0 else step // 2

    def one(i, carry):
        at = pl.ds(pl.multiple_of(i * step, step), step)
        if len(lead) == 0:
            dst[at, :] = dst[at, :] + src[at, :]
        elif len(lead) == 1:
            for a in range(lead[0]):
                dst[a, at, :] = dst[a, at, :] + src[a, at, :]
        else:
            for a in range(lead[0]):
                for b in range(lead[1]):
                    dst[a, b, at, :] = dst[a, b, at, :] + src[a, b, at, :]
        return carry

    lax.fori_loop(0, count // step, one, 0)


def region(fixed, half):
    first = fixed["x"] if "x" in fixed else slice(None)
    second = fixed["y"] if "y" in fixed else slice(None)
    count, start = half, 0
    if "near" in fixed:
        count = half // 2
        start = fixed["near"] * count
    if "far" in fixed:
        start = start + fixed["far"] * (count // 2)
        count = count // 2
    rows = pl.ds(start if isinstance(start, int) else pl.multiple_of(start, count), count)
    return first, second, rows


def region_shape(names, half):
    lead = tuple(2 for name in ("x", "y") if name not in names)
    rows = half // (2 if "near" in names else 1) // (2 if "far" in names else 1)
    return lead + (rows,)


def step_shapes(half, plan, steps=4):
    return [
        region_shape(names[: s + 1], half) + (stop - start,)
        for names, start, stop in plan
        for s in range(steps)
    ]


class Loaded:
    def __init__(self, copy):
        self.copy = copy

    def wait_recv(self):
        self.copy.wait()


class Rings:
    def __init__(self, copies, half, plan, bits, device, got):
        self.copies, self.half, self.bits, self.device, self.got = copies, half, bits, device, got
        self.names = [names for names, start, stop in plan]
        self.columns = [pl.ds(start, stop - start) for names, start, stop in plan]

    def other(self, name):
        return self.device(**{name: 1 - self.bits[name]})

    def part(self, ref, fixed, p, offset=0):
        first, second, rows = region(fixed, self.half)
        if not isinstance(offset, int):
            start = rows.start + offset
            rows = pl.ds(pl.multiple_of(start, rows.size), rows.size)
        return ref.at[first, second, rows, self.columns[p]]

    def fixed(self, p, s, flip=False):
        names = self.names[p][: s + 1]
        result = {name: self.bits[name] for name in names}
        if flip:
            result[names[-1]] = 1 - result[names[-1]]
        return result

    def spread(self, out, p, s, offset):
        place = self.part(out, self.fixed(p, s), p, offset)
        return self.copies.send(place, place, self.other(self.names[p][s]))


def finish_kernel(
    plan, plan_q, order, work_hbm, *refs,
):
    early_got, refs = refs[: len(plan)], refs[len(plan) :]
    (w_out_ref, small_ref, dq_hbm, dk_hbm, dv_hbm,
     tok_hbm, w_hbm, pre_ref, out_ref, gtok_ref, sum_ref, work, got0, *rest) = refs
    steps_f, steps_q = 4 * len(plan), 4 * len(plan_q)
    got, got_q, rest = rest[:steps_f], rest[steps_f : steps_f + steps_q], rest[steps_f + steps_q :]
    (slabs, part, part_in, total_ref, small_in, dq_ref, dk_ref, dv_ref, tok_ref, w_ref,
     send_sem, recv_sem, local_sem) = rest
    core, x, y, near, far, device = grid_place()
    bits = {"x": x, "y": y, "near": near, "far": far}
    seq = lax.axis_index("seq")
    sibling = device(core=1 - core)
    others = {name: device(**{name: 1 - bits[name]}) for name in bits}
    copies = Copies(send_sem, recv_sem, local_sem)
    rows, feat = gtok_ref.shape
    half = rows // 2
    rings = Rings(copies, half, plan, bits, device, got)
    rings_q = Rings(copies, half, plan_q, bits, device, got_q)
    moves = {}
    early = []
    for k in range(2):
        early.append(copies.local(work_hbm.at[k], work.at[k]))
        for p, src in enumerate(early_got):
            moves[k, p, 0] = Loaded(copies.local(src.at[k], got[p * 4].at[k]))
    loads = {
        name: copies.local(src, dst)
        for name, src, dst in (
            ("w", w_hbm, w_ref), ("dk", dk_hbm, dk_ref), ("dv", dv_hbm, dv_ref),
            ("tok", tok_hbm, tok_ref), ("dq", dq_hbm, dq_ref), ("pre", pre_ref, total_ref),
        )
    }
    loaded = set()

    def need(*wanted):
        for name in wanted:
            if name not in loaded:
                loads[name].wait()
                loaded.add(name)

    greet([sibling] + list(others.values()))
    mine = pl.multiple_of(core * half, half)
    theirs = pl.multiple_of((1 - core) * half, half)

    def lane(k):
        return (rings, k) if k < 2 else (rings_q, 0)

    def reduce_send(k, p, s):
        ring, slot = lane(k)
        moves[k, p, s] = copies.send(
            ring.part(work.at[k], ring.fixed(p, s, True), p),
            ring.got[p * 4 + s].at[slot],
            others[ring.names[p][s]],
        )

    def reduce_step(k, p, s):
        ring, slot = lane(k)
        moves[k, p, s - 1].wait_recv()
        add_rows(ring.part(work.at[k], ring.fixed(p, s - 1), p), ring.got[p * 4 + s - 1].at[slot])
        if s < 4:
            reduce_send(k, p, s)

    def spread_start(k, p):
        reduce_step(k, p, 4)
        ring = lane(k)[0]
        src = ring.part(work.at[k], ring.fixed(p, 3), p)
        dst = ring.part(out_ref.at[k], ring.fixed(p, 3), p, mine)
        moves[k, p, "own"] = copies.local(src, dst)
        moves[k, p, 3] = copies.send(src, dst, others["far"])

    def spread_step(k, p, s):
        moves[k, p, s + 1].wait_recv()
        if s == 2:
            moves[k, p, "own"].wait()
        moves[k, p, s] = lane(k)[0].spread(out_ref.at[k], p, s, mine)

    def spread_cores(k, p):
        moves[k, p, 0].wait_recv()
        place = out_ref.at[k, :, :, pl.ds(mine, half), lane(k)[0].columns[p]]
        moves[k, p, "end"] = copies.send(place, place, sibling)

    small_partners = [sibling] + [others[name] for name in ("x", "y", "near", "far")]

    def small_step(s):
        moves["small"] = copies.send(
            sum_ref if s else small_ref, small_in.at[s], small_partners[s], False
        )

    def small_add(s):
        moves["small"].wait()
        sum_ref[...] = (sum_ref if s else small_ref)[...] + small_in[s]
        if s < 4:
            small_step(s + 1)

    def token_part(py, pc):
        need("w", "dk", "dv")
        at = pl.ds(pl.multiple_of((py * 2 + pc) * rows, rows), rows)
        return dot(dk_ref[at, :], w_ref[:, feat : 2 * feat], NT) + dot(
            dv_ref[at, :], w_ref[:, 2 * feat : 3 * feat], NT
        )

    def weights(n, at, columns):
        if n == 0:
            need("tok", "dq")
            own_tokens = pl.ds(pl.multiple_of(seq * rows, rows), rows)
            value = dot(tok_ref[at, own_tokens], dq_ref[:, columns])
        else:
            need("tok", "dk" if n == 1 else "dv")
            value = dot(tok_ref[at, :], (dk_ref if n == 1 else dv_ref)[:, columns])
        return value.astype(jnp.bfloat16)

    def weights_away(p):
        columns = rings_q.columns[p]
        for n in range(3):
            slabs[n, :, columns] = weights(n, pl.ds(theirs, half), columns)
        moves["q", p] = copies.send(slabs.at[:, :, columns], got0.at[0:3, :, columns], sibling)

    def weights_here(p):
        columns = rings_q.columns[p]
        for n in range(3):
            work[2, n // 2, n % 2, :, columns] = weights(n, pl.ds(mine, half), columns)
        if "out" in moves:
            out_here.wait()
            moves.pop("out").wait_recv()
        moves["q", p].wait_recv()
        for n in range(4):
            add_rows(work.at[2, n // 2, n % 2, :, columns], got0.at[n, :, columns])
        reduce_send(2, p, 0)

    def tokens_far():
        part[0] = token_part(1 - y, 1 - core).astype(jnp.bfloat16)
        moves["far"] = copies.send(part.at[0], part_in.at[0], sibling)

    def tokens_near():
        part[1] = token_part(y, 1 - core).astype(jnp.bfloat16)
        moves["near"] = copies.send(part.at[1], part_in.at[1], sibling)

    def tokens_cross():
        part[2] = token_part(1 - y, core).astype(jnp.bfloat16)
        moves["far"].wait_recv()
        add_rows(part.at[2], part_in.at[0])
        moves["cross"] = copies.send(part.at[2], part_in.at[2], others["y"])

    def tokens_own():
        need("w", "pre", "dq")
        total_ref[...] = (
            total_ref[...] + dot(dq_ref[...], w_ref[:, 0:feat], NT) + token_part(y, core)
        )

    def tokens_end():
        moves["near"].wait_recv()
        moves["cross"].wait_recv()
        gtok_ref[...] = (
            total_ref[...] + part_in[1].astype(jnp.float32) + part_in[2].astype(jnp.float32)
        ).astype(jnp.bfloat16)

    moves["out"] = copies.send(w_out_ref.at[pl.ds(theirs, half), :], got0.at[3], sibling)
    out_here = copies.local(w_out_ref.at[pl.ds(mine, half), :], work.at[2, 1, 1])
    small_step(0)
    for k in range(2):
        early[k].wait()
        for p in range(len(plan)):
            reduce_step(k, p, 1)
    steps = {
        "add": reduce_step, "top": spread_start, "out": spread_step, "end": spread_cores,
        "small": small_add, "wa": weights_away, "wh": weights_here, "far": tokens_far,
        "near": tokens_near, "cross": tokens_cross, "own": tokens_own, "last": tokens_end,
    }
    for name, *values in order:
        steps[name](*values)
    for k in range(3):
        for p in range(len(lane(k)[0].names)):
            moves[k, p, "end"].wait_recv()
    copies.finish()


PLAN = (
    (("near", "x", "y", "far"), 0, 256),
    (("y", "near", "x", "far"), 256, 512),
    (("x", "y", "near", "far"), 512, 768),
)
PLAN_Q = (
    (("near", "x", "y", "far"), 0, 256),
    (("x", "near", "y", "far"), 256, 512),
    (("near", "y", "x", "far"), 512, 640),
    (("y", "x", "near", "far"), 640, 768),
)
ORDER = (
    ("far",), ("small", 0), ("wa", 0), ("add", 0, 0, 2), ("add", 0, 1, 2), ("add", 0, 2, 2),
    ("wh", 0), ("add", 1, 0, 2), ("add", 1, 1, 2), ("small", 1), ("cross",), ("add", 1, 2, 2),
    ("wa", 1), ("add", 0, 0, 3), ("add", 0, 1, 3), ("add", 0, 2, 3), ("small", 2), ("wh", 1),
    ("add", 2, 0, 1), ("add", 1, 0, 3), ("add", 1, 1, 3), ("add", 1, 2, 3), ("wa", 2),
    ("top", 0, 0), ("wh", 2), ("top", 0, 1), ("top", 0, 2), ("small", 3), ("wa", 3),
    ("top", 1, 0), ("wh", 3), ("add", 2, 1, 1), ("top", 1, 1), ("top", 1, 2), ("near",),
    ("add", 2, 0, 2), ("add", 2, 2, 1), ("out", 0, 1, 2), ("own",), ("add", 2, 1, 2),
    ("out", 0, 2, 2), ("out", 0, 1, 1), ("small", 4), ("last",), ("out", 0, 0, 2),
    ("add", 2, 3, 1), ("out", 1, 1, 2), ("out", 1, 0, 2), ("add", 2, 0, 3), ("out", 1, 2, 2),
    ("out", 0, 2, 1), ("add", 2, 2, 2), ("add", 2, 3, 2), ("add", 2, 1, 3), ("out", 0, 1, 0),
    ("out", 1, 1, 1), ("out", 0, 0, 1), ("add", 2, 2, 3), ("top", 2, 0), ("out", 1, 0, 1),
    ("add", 2, 3, 3), ("top", 2, 1), ("out", 0, 2, 0), ("out", 1, 2, 1), ("out", 0, 0, 0),
    ("top", 2, 2), ("out", 2, 0, 2), ("top", 2, 3), ("out", 2, 1, 2), ("out", 1, 0, 0),
    ("end", 0, 1), ("out", 1, 1, 0), ("out", 1, 2, 0), ("end", 0, 2), ("end", 0, 0),
    ("out", 2, 0, 1), ("out", 2, 2, 2), ("out", 2, 3, 2), ("out", 2, 1, 1), ("end", 1, 0),
    ("end", 1, 2), ("out", 2, 3, 1), ("end", 1, 1), ("out", 2, 0, 0), ("out", 2, 1, 0),
    ("out", 2, 2, 1), ("out", 2, 3, 0), ("out", 2, 2, 0), ("end", 2, 3), ("end", 2, 0),
    ("end", 2, 1), ("end", 2, 2),
)


def finish(work, early, w_out_grad, small, dq, dk, dv, flipped_tokens, w_qkv, grad_pre1):
    rows, feat = dq.shape
    half = rows // 2
    low = jnp.bfloat16
    vmem = pl.BlockSpec(memory_space=pltpu.VMEM)
    anywhere = pl.BlockSpec(memory_space=pl.ANY)
    return pl.pallas_call(
        functools.partial(finish_kernel, PLAN, PLAN_Q, ORDER),
        out_shape=(
            jax.ShapeDtypeStruct((3, 2, 2, rows, feat), low),
            jax.ShapeDtypeStruct((rows, feat), low),
            jax.ShapeDtypeStruct(small.shape, jnp.float32),
        ),
        in_specs=[anywhere] * (2 + len(PLAN)) + [vmem] + [anywhere] * 6,
        out_specs=(anywhere, vmem, vmem),
        scratch_shapes=[
            pltpu.VMEM((3, 2, 2, half, feat), low),
            pltpu.VMEM((4, half, feat), low),
        ]
        + [pltpu.VMEM((2,) + shape, low) for shape in step_shapes(half, PLAN)]
        + [pltpu.VMEM((1,) + shape, low) for shape in step_shapes(half, PLAN_Q)]
        + [
            pltpu.VMEM((3, half, feat), low),
            pltpu.VMEM((3, rows, feat), low),
            pltpu.VMEM((3, rows, feat), low),
            pltpu.VMEM((rows, feat), jnp.float32),
            pltpu.VMEM((5,) + small.shape, jnp.float32),
            pltpu.VMEM(dq.shape, low),
            pltpu.VMEM(dk.shape, low),
            pltpu.VMEM(dv.shape, low),
            pltpu.VMEM(flipped_tokens.shape, low),
            pltpu.VMEM(w_qkv.shape, low),
            pltpu.SemaphoreType.DMA((128,)),
            pltpu.SemaphoreType.DMA((128,)),
            pltpu.SemaphoreType.DMA((32,)),
        ],
        compiler_params=pltpu.CompilerParams(
            collective_id=0, has_side_effects=True, vmem_limit_bytes=60 * 2**20
        ),
        name="finish",
    )(work, *early, w_out_grad, small, dq, dk, dv, flipped_tokens, w_qkv, grad_pre1)


def widen_kernel(
    in_ref, back_ref, last_ref, sum_ref, one_ref, two_ref,
    in_out, back_out, qkv_out, out_out, one_out, two_out, bias_out, *vec_outs,
):
    in_out[...] = in_ref[0, 0, 0].astype(jnp.float32)
    back_out[...] = back_ref[0, 0, 0].astype(jnp.float32)
    one_out[...] = one_ref[...]
    two_out[...] = two_ref[...]
    last = last_ref[0, 0, 0].astype(jnp.float32)
    feat = sum_ref.shape[1]

    @pl.when(pl.program_id(0) < 3)
    def _():
        qkv_out[...] = last

    @pl.when(pl.program_id(0) == 3)
    def _():
        out_out[...] = last
        for i, vec_out in enumerate(vec_outs):
            vec_out[...] = sum_ref[i]
        for i in range(4):
            bias_out[pl.ds(i * feat, feat)] = sum_ref[6 + i]


def widen(grads, sums, layer_out, grad_tokens):
    rows, feat = grads.shape[-2:]
    wide = jnp.float32
    quarter = rows // 4

    def source(k):
        return pl.BlockSpec((1, 1, 1, rows, feat), lambda n: (k, n // 2, n % 2, 0, 0))

    part = pl.BlockSpec((quarter, feat), lambda n: (n, 0))
    vector = jax.ShapeDtypeStruct((feat,), wide)
    return pl.pallas_call(
        widen_kernel,
        grid=(4,),
        out_shape=[
            jax.ShapeDtypeStruct((rows, 4 * feat), wide),
            jax.ShapeDtypeStruct((4 * rows, feat), wide),
            jax.ShapeDtypeStruct((rows, 3 * feat), wide),
            jax.ShapeDtypeStruct((rows, feat), wide),
            jax.ShapeDtypeStruct((rows, feat), layer_out.dtype),
            jax.ShapeDtypeStruct((rows, feat), layer_out.dtype),
            jax.ShapeDtypeStruct((4 * feat,), wide),
        ]
        + [vector] * 6,
        in_specs=[source(k) for k in range(3)]
        + [pl.BlockSpec(sums.shape, lambda n: (0, 0)), part, part],
        out_specs=[
            pl.BlockSpec((rows, feat), lambda n: (0, n)),
            pl.BlockSpec((rows, feat), lambda n: (n, 0)),
            pl.BlockSpec((rows, feat), lambda n: (0, jnp.minimum(n, 2))),
            pl.BlockSpec((rows, feat), lambda n: (0, 0)),
            part,
            part,
            pl.BlockSpec((4 * feat,), lambda n: (0,)),
        ]
        + [pl.BlockSpec((feat,), lambda n: (0,))] * 6,
        compiler_params=pltpu.CompilerParams(vmem_limit_bytes=56 * 2**20),
        name="widen",
    )(grads, grads, grads, sums, layer_out, grad_tokens)


PIECES = 6


def front_kernel(
    tok_hbm, w_hbm, q_ref, kv_out, flip_out, all_ref, kv_ref, flip_ref, w_ref, send_sem, recv_sem, local_sem
):
    core, x, y, near, far, device = grid_place()
    sibling, over_y = device(core=1 - core), device(y=1 - y)
    low = jnp.bfloat16
    rows, feat = q_ref.shape
    piece = rows // PIECES
    copies = Copies(send_sem, recv_sem, local_sem)

    def rows_of(py, pc, i=None):
        start = (py * 2 + pc) * rows
        if i is None:
            return pl.ds(pl.multiple_of(start, rows), rows)
        return pl.ds(pl.multiple_of(start + i * piece, piece), piece)

    own = rows_of(y, core)
    load = copies.local(tok_hbm, all_ref.at[own])
    load_w = copies.local(w_hbm, w_ref)
    greet([sibling, over_y])
    crossing = []
    for i in range(PIECES):
        src = tok_hbm.at[pl.ds(i * piece, piece)]
        crossing.append(copies.send(src, all_ref.at[rows_of(y, core, i)], over_y))
    beside = copies.send(tok_hbm, all_ref.at[own], sibling)
    stores = []

    def project(at):
        kv_ref[at, :] = dot(all_ref[at, :], w_ref[:, feat:]).astype(low)
        stores.append(copies.local(kv_ref.at[at], kv_out.at[at]))
        flip_ref[:, at] = all_ref[at, :].T
        stores.append(copies.local(flip_ref.at[:, at], flip_out.at[:, at]))

    load.wait()
    load_w.wait()
    project(own)
    q_ref[...] = dot(all_ref[own, :], w_ref[:, 0:feat]).astype(low) * low(HEAD ** (-0.5))
    beside.wait_recv()
    project(rows_of(y, 1 - core))
    passed = []
    for i in range(PIECES):
        crossing[i].wait_recv()
        at = rows_of(1 - y, core, i)
        passed.append(copies.send(all_ref.at[at], all_ref.at[at], sibling))
        project(at)
        if i > 0:
            passed[i - 1].wait_recv()
            project(rows_of(1 - y, 1 - core, i - 1))
    passed[-1].wait_recv()
    project(rows_of(1 - y, 1 - core, PIECES - 1))
    for store in stores:
        store.wait()
    copies.finish()


def front(tokens, w_qkv, seq_parts):
    rows, feat = tokens.shape
    low = jnp.bfloat16
    keys = rows * seq_parts
    anywhere = pl.BlockSpec(memory_space=pl.ANY)
    count = 2 + 2 * PIECES
    return pl.pallas_call(
        front_kernel,
        out_shape=(
            jax.ShapeDtypeStruct((rows, feat), low),
            jax.ShapeDtypeStruct((keys, 2 * feat), low),
            jax.ShapeDtypeStruct((feat, keys), low),
        ),
        in_specs=[anywhere, anywhere],
        out_specs=(pl.BlockSpec(memory_space=pltpu.VMEM), anywhere, anywhere),
        scratch_shapes=[
            pltpu.VMEM((keys, feat), low),
            pltpu.VMEM((keys, 2 * feat), low),
            pltpu.VMEM((feat, keys), low),
            pltpu.VMEM(w_qkv.shape, low),
            pltpu.SemaphoreType.DMA((count,)),
            pltpu.SemaphoreType.DMA((count,)),
            pltpu.SemaphoreType.DMA((2 + 2 * count,)),
        ],
        compiler_params=pltpu.CompilerParams(
            collective_id=2, has_side_effects=True, vmem_limit_bytes=56 * 2**20
        ),
        name="front",
    )(tokens, w_qkv)


def gelu_parts(v):
    size = jnp.abs(v)
    fall = jnp.exp(-0.5 * v * v)
    t = 1.0 / (1.0 + (0.3275911 * 0.7071067811865476) * size)
    tail = 1.061405429 * t - 1.453152027
    tail = tail * t + 1.421413741
    tail = tail * t - 0.284496736
    tail = tail * t + 0.254829592
    half = 0.5 * tail * t * fall
    return jnp.where(v >= 0.0, 1.0 - half, half), fall


def row_mean(values):
    return jnp.sum(values, axis=-1, keepdims=True) * (1.0 / values.shape[-1])


def fold8(values):
    total = values[0:8]
    for i in range(1, values.shape[0] // 8):
        total = total + values[i * 8 : (i + 1) * 8]
    return total


STEP = 128
TILE = 64


def middle_kernel(
    plan, mixed_ref, tok_ref, cot_ref, *refs,
):
    vec_refs, bias_ref, refs = refs[:6], refs[6], refs[7:]
    (w_out_ref, w_in_hbm, w_back_hbm,
     out_ref, pre_ref, gmix_ref, gw_out_ref, small_ref, work_out, *refs) = refs
    away, refs = refs[: len(plan)], refs[len(plan) :]
    (w_in_ref, w_back_ref, unit, spread, hid, active, slope, acc, acc2, gsecond, gbranch,
     work, slabs, got0, send_sem, recv_sem, local_sem) = refs
    core, x, y, near, far, device = grid_place()
    sibling = device(core=1 - core)
    low = jnp.bfloat16
    rows, feat = tok_ref.shape
    half = rows // 2
    count = 4
    chunks = rows // STEP
    copies = Copies(send_sem, recv_sem, local_sem)
    load_in = copies.local(w_in_hbm, w_in_ref)
    load_back = copies.local(w_back_hbm, w_back_ref)
    greet([sibling])
    mine = pl.multiple_of(core * half, half)
    theirs = pl.multiple_of((1 - core) * half, half)

    def rows_at(i):
        return pl.ds(pl.multiple_of(i * STEP, STEP), STEP)

    def slab_at(n):
        return pl.ds(pl.multiple_of(n * feat, feat), feat)

    def vec(i):
        return vec_refs[i][...].reshape(1, feat)

    zero = jnp.zeros((8, feat), jnp.float32)

    def put(i, value):
        small_ref[i : i + 1, :] = jnp.sum(value, axis=0, keepdims=True)

    small_ref[...] = jnp.zeros_like(small_ref)

    acc[...] = dot(mixed_ref[...], w_out_ref[...])

    def norm_one(i, carry):
        at = rows_at(i)
        v = tok_ref[at, :].astype(jnp.float32) + (acc[at, :] + vec(0))
        v = v - row_mean(v)
        r = lax.rsqrt(row_mean(v * v) + NORM_EPS)
        u = v * r
        unit[at, :] = u
        spread[at, :] = jnp.broadcast_to(r, (STEP, 128))
        hid[at, :] = (u * vec(1) + vec(2)).astype(low)
        return carry

    lax.fori_loop(0, chunks, norm_one, 0)
    load_in.wait()

    group = rows // 6

    def inner_of(n, i):
        return dot(hid[i * group : (i + 1) * group, :], w_in_ref[:, n * feat : (n + 1) * feat])

    inner = [inner_of(0, i) for i in range(6)]
    load_back.wait()
    for n in range(count):
        bias = bias_ref[n * feat : (n + 1) * feat].reshape(1, feat)
        following = []
        for i in range(6):
            if n + 1 < count:
                following.append(inner_of(n + 1, i))
            for j in range(group // TILE):
                at = slice(i * group + j * TILE, i * group + (j + 1) * TILE)
                v = inner[i][j * TILE : (j + 1) * TILE] + bias
                chance, fall = gelu_parts(v)
                active[n, at, :] = (v * chance).astype(low)
                slope[n, at, :] = (chance + (v * 0.3989422804014327) * fall).astype(low)
            at = slice(i * group, (i + 1) * group)
            second = dot(active[n, at, :], w_back_ref[n * feat : (n + 1) * feat, :])
            acc2[at, :] = second if n == 0 else acc2[at, :] + second
        inner = following

    def norm_two(i, sums):
        at = rows_at(i)
        v = (unit[at, :] * vec(1) + vec(2)) + (acc2[at, :] + vec(3))
        v = v - row_mean(v)
        r = lax.rsqrt(row_mean(v * v) + NORM_EPS)
        u = v * r
        out_ref[at, :] = (u * vec(4) + vec(5)).astype(low)
        c = cot_ref[at, :].astype(jnp.float32)
        a = c * vec(4)
        g = r * (a - row_mean(a) - u * row_mean(a * u))
        acc2[at, :] = g
        g_low = g.astype(low)
        gsecond[at, :] = g_low
        return (
            sums[0] + fold8(c * u), sums[1] + fold8(c), sums[2] + fold8(g_low.astype(jnp.float32)),
        )

    sums = lax.fori_loop(0, chunks, norm_two, (zero, zero, zero))
    put(4, sums[0])
    put(5, sums[1])
    put(3, sums[2])

    def exchange(k, n):
        return pltpu.make_async_remote_copy(
            src_ref=slabs.at[k, n],
            dst_ref=got0.at[k, n],
            send_sem=send_sem.at[k * 4 + n],
            recv_sem=recv_sem.at[k * 4 + n],
            device_id=sibling,
            device_id_type=pl.DeviceIdType.MESH,
        )

    def collect(k, n):
        exchange(k, n).wait_recv()
        add_rows(work.at[k, lax.div(n, 2), lax.rem(n, 2)], got0.at[k, n])
        exchange(k, n).wait_send()

    def back_slab(n, carry):
        columns = slab_at(n)
        slabs[1, n] = dot(active[n, :, pl.ds(theirs, half)], gsecond[...], TN).astype(low)
        exchange(1, n).start()
        work[1, lax.div(n, 2), lax.rem(n, 2)] = dot(active[n, :, pl.ds(mine, half)], gsecond[...], TN).astype(low)
        gactive = dot(gsecond[...], w_back_ref[columns, :], NT)
        total = zero
        for i in range(rows // TILE):
            at = slice(i * TILE, (i + 1) * TILE)
            g = (gactive[at] * slope[n, at, :].astype(jnp.float32)).astype(low)
            slope[n, at, :] = g
            total = total + fold8(g.astype(jnp.float32))

        small_ref[pl.ds(6 + n, 1), :] = jnp.sum(total, axis=0, keepdims=True)
        slabs[0, n] = dot(hid[:, pl.ds(theirs, half)], slope[n], TN).astype(low)
        exchange(0, n).start()

        @pl.when(n > 0)
        def _():
            collect(1, n - 1)
            collect(0, n - 1)

        work[0, lax.div(n, 2), lax.rem(n, 2)] = dot(hid[:, pl.ds(mine, half)], slope[n], TN).astype(low)

        acc2[...] += dot(slope[n], w_in_ref[:, columns], NT)
        return carry

    lax.fori_loop(0, count, back_slab, 0)

    def norm_back(i, sums):
        at = rows_at(i)
        g = acc2[at, :]
        u = unit[at, :]
        r = spread[at, 0:1]
        a = g * vec(1)
        d = r * (a - row_mean(a) - u * row_mean(a * u))
        pre_ref[at, :] = d
        d_low = d.astype(low)
        gbranch[at, :] = d_low
        return (
            sums[0] + fold8(g * u), sums[1] + fold8(g), sums[2] + fold8(d_low.astype(jnp.float32)),
        )

    sums = lax.fori_loop(0, chunks, norm_back, (zero, zero, zero))
    put(1, sums[0])
    put(2, sums[1])
    put(0, sums[2])
    gmix_ref[...] = dot(gbranch[...], w_out_ref[...], NT).astype(low)
    gw_out_ref[...] = dot(mixed_ref[...], gbranch[...], TN).astype(low)

    collect(1, count - 1)
    collect(0, count - 1)
    stores = [copies.local(work, work_out)]
    bits = {"x": x, "y": y, "near": near, "far": far}
    rings = Rings(copies, half, plan, bits, device, None)
    for k in range(2):
        for p in range(len(plan)):
            stores.append(
                copies.local(rings.part(work.at[k], rings.fixed(p, 0, True), p), away[p].at[k])
            )
    for store in stores:
        store.wait()


def middle(mixed, tokens, cotangent, vectors, b_in, w_out, w_in, w_back):
    rows, feat = tokens.shape
    half = rows // 2
    low = jnp.bfloat16
    wide = jnp.float32
    vmem = pl.BlockSpec(memory_space=pltpu.VMEM)
    anywhere = pl.BlockSpec(memory_space=pl.ANY)
    full = jax.ShapeDtypeStruct((rows, feat), low)
    return pl.pallas_call(
        functools.partial(middle_kernel, PLAN),
        out_shape=(
            full,
            jax.ShapeDtypeStruct((rows, feat), wide),
            full,
            full,
            jax.ShapeDtypeStruct((16, feat), wide),
            jax.ShapeDtypeStruct((2, 2, 2, half, feat), low),
        )
        + tuple(jax.ShapeDtypeStruct((2,) + shape, low) for shape in step_shapes(half, PLAN, 1)),
        in_specs=[vmem] * 11 + [anywhere] * 2,
        out_specs=(vmem,) * 5 + (anywhere,) * (1 + len(PLAN)),
        scratch_shapes=[
            pltpu.VMEM(w_in.shape, low),
            pltpu.VMEM(w_back.shape, low),
            pltpu.VMEM((rows, feat), wide),
            pltpu.VMEM((rows, 128), wide),
            pltpu.VMEM((rows, feat), low),
            pltpu.VMEM((4, rows, feat), low),
            pltpu.VMEM((4, rows, feat), low),
            pltpu.VMEM((rows, feat), wide),
            pltpu.VMEM((rows, feat), wide),
            pltpu.VMEM((rows, feat), low),
            pltpu.VMEM((rows, feat), low),
            pltpu.VMEM((2, 2, 2, half, feat), low),
            pltpu.VMEM((2, 4, half, feat), low),
            pltpu.VMEM((2, 4, half, feat), low),
            pltpu.SemaphoreType.DMA((8,)),
            pltpu.SemaphoreType.DMA((8,)),
            pltpu.SemaphoreType.DMA((16,)),
        ],
        compiler_params=pltpu.CompilerParams(
            collective_id=1, has_side_effects=True, vmem_limit_bytes=60 * 2**20
        ),
        name="middle",
    )(mixed, tokens, cotangent, *vectors, b_in, w_out, w_in, w_back)


FLIPS = {"x": (1, 0), "y": (0, 2), "near": (2, 0)}


def trade(value, name):
    parts = lax.axis_size("seq")
    flip_b, flip_s = FLIPS[name]
    pairs = [
        (b * parts + s, (b ^ flip_b) * parts + (s ^ flip_s))
        for b in range(lax.axis_size("batch"))
        for s in range(parts)
    ]
    return lax.ppermute(value, ("batch", "seq"), pairs)


def per_device(
    tokens,
    group_bucket,
    lengths,
    random_blocks,
    w_qkv,
    w_out,
    b_out,
    norm1_gain,
    norm1_shift,
    w_in,
    b_in,
    w_back,
    b_back,
    norm2_gain,
    norm2_shift,
    cotangent,
):
    low = jnp.bfloat16
    seq_parts = lax.axis_size("seq")
    tok_rows, feat = tokens.shape
    layout = (group_bucket, lengths, random_blocks)
    queries, kv, flipped_tokens = front(tokens, w_qkv, seq_parts)
    mixed, logs = attend(layout, queries, kv)
    vectors = (b_out, norm1_gain, norm1_shift, b_back, norm2_gain, norm2_shift)
    layer_out, grad_pre1, grad_mixed, grad_w_out, small, work, *away = middle(
        mixed, tokens, cotangent, vectors, b_in, w_out, w_in, w_back
    )
    early = [trade(value, names[0]) for value, (names, _, _) in zip(away, PLAN)]
    dq, dk, dv = attend_back(layout, queries, kv, grad_mixed, logs)
    grads, grad_tokens, sums = finish(
        work,
        early,
        grad_w_out,
        small,
        dq,
        dk,
        dv,
        flipped_tokens,
        w_qkv,
        grad_pre1,
    )
    wide = jnp.float32
    outer = lax.axis_size("batch") // BLOCK8
    if outer > 1:
        groups = [[o * BLOCK8 + i for o in range(outer)] for i in range(BLOCK8)]
        grads = lax.psum(grads.astype(wide), "batch", axis_index_groups=groups)
        sums = lax.psum(sums, "batch", axis_index_groups=groups)
    if outer > 1:
        grads = grads.astype(low)
    full_in, full_back, full_qkv, full_out, layer_out, grad_tokens, grad_b_in, *vectors = widen(
        grads, sums, layer_out, grad_tokens
    )
    return (
        layer_out,
        grad_tokens,
        full_qkv,
        full_out,
        *vectors[0:3],
        full_in,
        grad_b_in,
        full_back,
        *vectors[3:6],
    )


def solution(mesh):
    rows = P(("batch", "seq"), None)
    whole = P()
    placed = (rows, P("batch"), P("batch", None), P("batch", None, None)) + (whole,) * 11 + (rows,)
    return jax.shard_map(
        per_device,
        mesh=mesh,
        in_specs=placed,
        out_specs=(rows, rows) + (whole,) * 11,
        check_vma=False,
    )
```

```python
import functools
import jax
import jax.numpy as jnp
from jax import lax
from jax.sharding import PartitionSpec as P
from jax.experimental import pallas as pl
from jax.experimental.pallas import tpu as pltpu

HEADS = 12
HEAD = 64
BLOCK = 64
SHORT = 1024
LISTED = 8
QUAD = 4
WIDE = QUAD * HEAD
SPAN = LISTED * BLOCK
MASKED = -1e30
NORM_EPS = 1e-06
NT = (((1,), (1,)), ((), ()))
TN = (((0,), (0,)), ((), ()))


def dot(a, b, dims=(((1,), (0,)), ((), ()))):
    return lax.dot_general(a, b, dims, preferred_element_type=jnp.float32)


def stack_heads(rows, head_mask):
    return jnp.concatenate([rows] * QUAD, axis=0) * head_mask


def pick_heads(full, lane_head):
    out = full[0:BLOCK]
    for h in range(1, QUAD):
        out = jnp.where(lane_head == h, full[h * BLOCK : (h + 1) * BLOCK], out)
    return out


def masked_span(scores, row_id, limits):
    parts = []
    for j in range(LISTED):
        parts.append(
            jnp.where(row_id < limits[j], scores[j * BLOCK : (j + 1) * BLOCK], MASKED)
        )
    return jnp.concatenate(parts, axis=0)


class Layout:
    def __init__(self, blocks, nblocks, bucket_ref, length_ref, random_ref):
        self.first_own = lax.axis_index("seq") * blocks
        self.nblocks, self.short = nblocks, SHORT // BLOCK
        self.is_long = bucket_ref[0] > 0
        self.length_ref, self.random_ref = length_ref, random_ref

    def sequence(self, b):
        own = self.first_own + b
        member = jnp.where(self.is_long, 0, own // self.short)
        first = member * self.short
        span = jnp.where(self.is_long, self.nblocks, self.short)
        return own, first, first + span - 1, self.length_ref[0, member]

    def listed(self, b):
        own, first, last, valid = self.sequence(b)
        starts, limits = [], []
        ids = [own - 1, own, own + 1]
        ids += [self.random_ref[0, own, j] for j in range(3)]
        ids += [first, last]
        for j, block in enumerate(ids):
            inside = (block >= first) & (block <= last)
            if j >= 6:
                inside = inside & (jnp.abs(block - own) > 1)
            limits.append(jnp.where(inside, valid - (block - first) * BLOCK, 0))
            block = jnp.minimum(jnp.maximum(block, 0), self.nblocks - 1)
            starts.append(pl.multiple_of(block * BLOCK, BLOCK))
        return starts, limits

    def whole(self, b):
        own, first, last, valid = self.sequence(b)
        chunks = jnp.where(self.is_long, self.nblocks // self.short, 1)
        return (own == first) | (own == last), first * BLOCK, chunks, valid


def split_blocks(layout, blocks, sparse_ref):
    count = jnp.int32(0)
    for b in range(blocks):
        is_whole = layout.whole(b)[0]

        @pl.when(jnp.logical_not(is_whole))
        def _():
            sparse_ref[count] = b

        count = count + jnp.where(is_whole, 0, 1)
    return count


def fill_head_mask(hm_ref):
    r = lax.broadcasted_iota(jnp.int32, (WIDE, WIDE), 0) // HEAD
    c = lax.broadcasted_iota(jnp.int32, (WIDE, WIDE), 1) // HEAD
    hm_ref[...] = jnp.where(r == c, 1.0, 0.0).astype(jnp.bfloat16)


def attend_kernel(
    blocks, bucket_ref, length_ref, random_ref, q_ref, k_ref, v_ref, o_ref, l_ref, kcat, vcat, hm_ref,
):
    layout = Layout(blocks, k_ref.shape[0] // BLOCK, bucket_ref, length_ref, random_ref)
    fill_head_mask(hm_ref)
    row_id = lax.broadcasted_iota(jnp.int32, (BLOCK, WIDE), 0)
    lane_head = lax.broadcasted_iota(jnp.int32, (BLOCK, WIDE), 1) // HEAD
    chunk_row = lax.broadcasted_iota(jnp.int32, (SHORT, WIDE), 0)

    def one_block(b, carry):
        rows = pl.ds(pl.multiple_of(b * BLOCK, BLOCK), BLOCK)
        qm = stack_heads(q_ref[rows, :], hm_ref[...])
        starts, limits = layout.listed(b)
        for j in range(LISTED):
            src = pl.ds(starts[j], BLOCK)
            kcat[j * BLOCK : (j + 1) * BLOCK, :] = k_ref[src, :]
            vcat[j * BLOCK : (j + 1) * BLOCK, :] = v_ref[src, :]
        scores = masked_span(dot(kcat[...], qm, NT), row_id, limits)
        top = jnp.max(scores, axis=0, keepdims=True)
        grown = jnp.exp(scores - top)
        total = jnp.sum(grown, axis=0, keepdims=True)
        weights = (grown * (1.0 / total)).astype(jnp.bfloat16)
        full = dot(weights, vcat[...], TN)
        o_ref[rows, :] = pick_heads(full, lane_head).astype(jnp.bfloat16)
        l_ref[0, pl.ds(b, 1), :] = top + jnp.log(total)
        return carry

    lax.fori_loop(0, blocks, one_block, 0, unroll=UNROLL_F)

    def one_global(b, carry):
        is_whole, first, chunks, valid = layout.whole(b)

        @pl.when(is_whole)
        def _():
            rows = pl.ds(pl.multiple_of(b * BLOCK, BLOCK), BLOCK)
            qm = stack_heads(q_ref[rows, :], hm_ref[...])

            def attend_whole(count):
                spans = [
                    pl.ds(pl.multiple_of(first + c * SHORT, BLOCK), SHORT) for c in range(count)
                ]
                scores = [
                    jnp.where(chunk_row < valid - c * SHORT, dot(k_ref[spans[c], :], qm, NT), MASKED)
                    for c in range(count)
                ]
                top = functools.reduce(
                    jnp.maximum, [jnp.max(value, axis=0, keepdims=True) for value in scores]
                )
                total, full = 0.0, 0.0
                for c in range(count):
                    grown = jnp.exp(scores[c] - top)
                    total = total + jnp.sum(grown, axis=0, keepdims=True)
                    full = full + dot(v_ref[spans[c], :], grown.astype(jnp.bfloat16), TN)
                full = (full * (1.0 / total)).T
                o_ref[rows, :] = pick_heads(full, lane_head).astype(jnp.bfloat16)
                l_ref[0, pl.ds(b, 1), :] = top + jnp.log(total)

            pl.when(layout.is_long)(lambda: attend_whole(layout.nblocks // layout.short))
            pl.when(jnp.logical_not(layout.is_long))(lambda: attend_whole(1))

        return carry

    lax.fori_loop(0, blocks, one_global, 0)

UNROLL_F = 12
UNROLL_B = 10

def smem():
    return pl.BlockSpec(memory_space=pltpu.SMEM)


def attend(layout, queries, kv):
    rows, feat = queries.shape
    keys = kv.shape[0]
    quads = feat // WIDE
    blocks = rows // BLOCK
    pad_blocks = -(-blocks // 8) * 8
    return pl.pallas_call(
        functools.partial(attend_kernel, blocks),
        grid=(quads,),
        out_shape=(
            jax.ShapeDtypeStruct((rows, feat), jnp.bfloat16),
            jax.ShapeDtypeStruct((quads, pad_blocks, WIDE), jnp.float32),
        ),
        in_specs=[
            smem(),
            smem(),
            smem(),
            pl.BlockSpec((rows, WIDE), lambda i: (0, i)),
            pl.BlockSpec((keys, WIDE), lambda i: (0, i)),
            pl.BlockSpec((keys, WIDE), lambda i: (0, i + quads)),
        ],
        out_specs=[
            pl.BlockSpec((rows, WIDE), lambda i: (0, i)),
            pl.BlockSpec((1, pad_blocks, WIDE), lambda i: (i, 0, 0)),
        ],
        scratch_shapes=[
            pltpu.VMEM((SPAN, WIDE), jnp.bfloat16),
            pltpu.VMEM((SPAN, WIDE), jnp.bfloat16),
            pltpu.VMEM((WIDE, WIDE), jnp.bfloat16),
        ],
        compiler_params=pltpu.CompilerParams(vmem_limit_bytes=56 * 2**20),
        name="attend",
    )(*layout, queries, kv, kv)


def attend_back_kernel(
    blocks, bucket_ref, length_ref, random_ref, q_ref, k_ref, v_ref, g_ref, l_ref,
    dq_ref, dk_ref, dv_ref, kcat, vcat, dk_sum, dv_sum, hm_ref, sparse_ref,
):
    layout = Layout(blocks, k_ref.shape[0] // BLOCK, bucket_ref, length_ref, random_ref)
    fill_head_mask(hm_ref)
    count = split_blocks(layout, blocks, sparse_ref)
    row_id = lax.broadcasted_iota(jnp.int32, (BLOCK, WIDE), 0)
    lane_head = lax.broadcasted_iota(jnp.int32, (BLOCK, WIDE), 1) // HEAD
    chunk_row = lax.broadcasted_iota(jnp.int32, (SHORT, WIDE), 0)
    dk_sum[...] = jnp.zeros_like(dk_sum)
    dv_sum[...] = jnp.zeros_like(dv_sum)
    factor = HEAD ** (-0.5)

    def one_block(t, carry):
        b = sparse_ref[t]
        rows = pl.ds(pl.multiple_of(b * BLOCK, BLOCK), BLOCK)
        qm = stack_heads(q_ref[rows, :], hm_ref[...])
        gm = stack_heads(g_ref[rows, :], hm_ref[...])
        starts, limits = layout.listed(b)
        for j in range(LISTED):
            kcat[j * BLOCK : (j + 1) * BLOCK, :] = k_ref[pl.ds(starts[j], BLOCK), :]
            vcat[j * BLOCK : (j + 1) * BLOCK, :] = v_ref[pl.ds(starts[j], BLOCK), :]
        scores = masked_span(dot(kcat[...], qm, NT), row_id, limits)
        chance = jnp.exp(scores - l_ref[0, pl.ds(b, 1), :])
        grad_w = dot(vcat[...], gm, NT)
        mean = jnp.sum(chance * grad_w, axis=0, keepdims=True)
        grad_s = (chance * (grad_w - mean)).astype(jnp.bfloat16)
        dk_part = dot(grad_s, qm)
        dv_part = dot(chance.astype(jnp.bfloat16), gm)
        for j in range(LISTED):
            dst = pl.ds(starts[j], BLOCK)
            dk_sum[dst, :] += dk_part[j * BLOCK : (j + 1) * BLOCK]
            dv_sum[dst, :] += dv_part[j * BLOCK : (j + 1) * BLOCK]
        full = dot(grad_s, kcat[...], TN)
        dq_ref[rows, :] = (pick_heads(full, lane_head) * factor).astype(jnp.bfloat16)
        return carry

    lax.fori_loop(0, blocks - 2, one_block, 0, unroll=UNROLL_B)
    lax.fori_loop(blocks - 2, count, one_block, 0)

    def one_global(b, carry):
        is_whole, first, chunks, valid = layout.whole(b)

        @pl.when(is_whole)
        def _():
            rows = pl.ds(pl.multiple_of(b * BLOCK, BLOCK), BLOCK)
            qm = stack_heads(q_ref[rows, :], hm_ref[...])
            gm = stack_heads(g_ref[rows, :], hm_ref[...])
            log_total = l_ref[0, pl.ds(b, 1), :]

            def back_whole(count):
                spans = [
                    pl.ds(pl.multiple_of(first + c * SHORT, BLOCK), SHORT) for c in range(count)
                ]
                chances, grads, mean = [], [], 0.0
                for c in range(count):
                    scores = dot(k_ref[spans[c], :], qm, NT)
                    scores = jnp.where(chunk_row < valid - c * SHORT, scores, MASKED)
                    chances.append(jnp.exp(scores - log_total))
                    grads.append(dot(v_ref[spans[c], :], gm, NT))
                    mean = mean + jnp.sum(chances[c] * grads[c], axis=0, keepdims=True)
                full = 0.0
                for c in range(count):
                    grad_s = (chances[c] * (grads[c] - mean)).astype(jnp.bfloat16)
                    dk_sum[spans[c], :] += dot(grad_s, qm)
                    dv_sum[spans[c], :] += dot(chances[c].astype(jnp.bfloat16), gm)
                    full = full + dot(grad_s, k_ref[spans[c], :], TN)
                dq_ref[rows, :] = (pick_heads(full, lane_head) * factor).astype(jnp.bfloat16)

            pl.when(layout.is_long)(lambda: back_whole(layout.nblocks // layout.short))
            pl.when(jnp.logical_not(layout.is_long))(lambda: back_whole(1))

        return carry

    lax.fori_loop(0, blocks, one_global, 0)
    dk_ref[...] = dk_sum[...].astype(jnp.bfloat16)
    dv_ref[...] = dv_sum[...].astype(jnp.bfloat16)


def attend_back(layout, queries, kv, grads, logs):
    rows, feat = queries.shape
    keys = kv.shape[0]
    quads = feat // WIDE
    blocks = rows // BLOCK
    pad_blocks = logs.shape[1]
    row_spec = pl.BlockSpec((rows, WIDE), lambda i: (0, i))
    key_spec = pl.BlockSpec((keys, WIDE), lambda i: (0, i))
    return pl.pallas_call(
        functools.partial(attend_back_kernel, blocks),
        grid=(quads,),
        out_shape=(
            jax.ShapeDtypeStruct((rows, feat), jnp.bfloat16),
            jax.ShapeDtypeStruct((keys, feat), jnp.bfloat16),
            jax.ShapeDtypeStruct((keys, feat), jnp.bfloat16),
        ),
        in_specs=[
            smem(),
            smem(),
            smem(),
            row_spec,
            key_spec,
            pl.BlockSpec((keys, WIDE), lambda i: (0, i + quads)),
            row_spec,
            pl.BlockSpec((1, pad_blocks, WIDE), lambda i: (i, 0, 0)),
        ],
        out_specs=[row_spec, key_spec, key_spec],
        scratch_shapes=[
            pltpu.VMEM((SPAN, WIDE), jnp.bfloat16),
            pltpu.VMEM((SPAN, WIDE), jnp.bfloat16),
            pltpu.VMEM((keys, WIDE), jnp.float32),
            pltpu.VMEM((keys, WIDE), jnp.float32),
            pltpu.VMEM((WIDE, WIDE), jnp.bfloat16),
            pltpu.SMEM((blocks,), jnp.int32),
        ],
        compiler_params=pltpu.CompilerParams(vmem_limit_bytes=56 * 2**20),
        name="attend_back",
    )(*layout, queries, kv, kv, grads, logs)


BLOCK8 = 8


def grid_place():
    batch, seq = lax.axis_index("batch"), lax.axis_index("seq")
    inner = lax.rem(batch, BLOCK8)
    base = batch - inner
    x, z = lax.rem(inner, 2), lax.div(inner, 2)
    core, y = lax.rem(seq, 2), lax.div(seq, 2)
    near, far = lax.rem(z, 2), lax.div(z, 2)

    def device(core=core, x=x, y=y, near=near, far=far):
        return (base + (far * 2 + near) * 2 + x, y * 2 + core)

    return core, x, y, near, far, device


class Copies:
    def __init__(self, send_sem, recv_sem, local_sem):
        self.send_sem, self.recv_sem, self.local_sem = send_sem, recv_sem, local_sem
        self.sent, self.held, self.started = 0, 0, []

    def send(self, src, dst, other, keep=True):
        copy = pltpu.make_async_remote_copy(
            src_ref=src,
            dst_ref=dst,
            send_sem=self.send_sem.at[self.sent],
            recv_sem=self.recv_sem.at[self.sent],
            device_id=other,
            device_id_type=pl.DeviceIdType.MESH,
        )
        self.sent += 1
        copy.start()
        if keep:
            self.started.append(copy)
        return copy

    def local(self, src, dst):
        copy = pltpu.make_async_copy(src, dst, self.local_sem.at[self.held])
        self.held += 1
        copy.start()
        return copy

    def finish(self):
        for copy in self.started:
            copy.wait_send()


def greet(partners):
    barrier = pltpu.get_barrier_semaphore()
    for other in partners:
        pl.semaphore_signal(barrier, inc=1, device_id=other, device_id_type=pl.DeviceIdType.MESH)
    pl.semaphore_wait(barrier, len(partners))


def add_rows(dst, src, step=64):
    count, lead = dst.shape[-2], dst.shape[:-2]
    step = step if count % step == 0 else step // 2

    def one(i, carry):
        at = pl.ds(pl.multiple_of(i * step, step), step)
        if len(lead) == 0:
            dst[at, :] = dst[at, :] + src[at, :]
        elif len(lead) == 1:
            for a in range(lead[0]):
                dst[a, at, :] = dst[a, at, :] + src[a, at, :]
        else:
            for a in range(lead[0]):
                for b in range(lead[1]):
                    dst[a, b, at, :] = dst[a, b, at, :] + src[a, b, at, :]
        return carry

    lax.fori_loop(0, count // step, one, 0)


def region(fixed, half):
    first = fixed["x"] if "x" in fixed else slice(None)
    second = fixed["y"] if "y" in fixed else slice(None)
    count, start = half, 0
    if "near" in fixed:
        count = half // 2
        start = fixed["near"] * count
    if "far" in fixed:
        start = start + fixed["far"] * (count // 2)
        count = count // 2
    rows = pl.ds(start if isinstance(start, int) else pl.multiple_of(start, count), count)
    return first, second, rows


def region_shape(names, half):
    lead = tuple(2 for name in ("x", "y") if name not in names)
    rows = half // (2 if "near" in names else 1) // (2 if "far" in names else 1)
    return lead + (rows,)


def step_shapes(half, plan, first=0, last=4):
    return [
        region_shape(names[: s + 1], half) + (stop - start,)
        for names, start, stop in plan
        for s in range(first, last)
    ]


class Rings:
    def __init__(self, copies, half, plan, bits, device, got):
        self.copies, self.half, self.bits, self.device, self.got = copies, half, bits, device, got
        self.names = [names for names, start, stop in plan]
        self.columns = [pl.ds(start, stop - start) for names, start, stop in plan]

    def other(self, name):
        return self.device(**{name: 1 - self.bits[name]})

    def part(self, ref, fixed, p, offset=0):
        first, second, rows = region(fixed, self.half)
        if not isinstance(offset, int):
            start = rows.start + offset
            rows = pl.ds(pl.multiple_of(start, rows.size), rows.size)
        return ref.at[first, second, rows, self.columns[p]]

    def fixed(self, p, s, flip=False):
        names = self.names[p][: s + 1]
        result = {name: self.bits[name] for name in names}
        if flip:
            result[names[-1]] = 1 - result[names[-1]]
        return result

    def spread(self, out, p, s, offset):
        place = self.part(out, self.fixed(p, s), p, offset)
        return self.copies.send(place, place, self.other(self.names[p][s]))


def finish_kernel(
    plan, plan_q, order, work_hbm, *refs,
):
    early_got, refs = refs[: len(plan)], refs[len(plan) :]
    (w_out_ref, small_ref, dq_hbm, dk_hbm, dv_hbm,
     tok_hbm, w_hbm, pre_ref, out_ref, gtok_ref, sum_ref, work, got0, *rest) = refs
    steps_f, steps_q = 3 * len(plan), 4 * len(plan_q)
    got_f, got_q, rest = rest[:steps_f], rest[steps_f : steps_f + steps_q], rest[steps_f + steps_q :]
    got = []
    for p in range(len(plan)):
        got += [early_got[p], *got_f[3 * p : 3 * p + 3]]
    (slabs, part, part_in, total_ref, small_in, dq_ref, dk_ref, dv_ref, tok_ref, w_ref,
     send_sem, recv_sem, local_sem) = rest
    core, x, y, near, far, device = grid_place()
    bits = {"x": x, "y": y, "near": near, "far": far}
    seq = lax.axis_index("seq")
    sibling = device(core=1 - core)
    others = {name: device(**{name: 1 - bits[name]}) for name in bits}
    copies = Copies(send_sem, recv_sem, local_sem)
    rows, feat = gtok_ref.shape
    half = rows // 2
    rings = Rings(copies, half, plan, bits, device, got)
    rings_q = Rings(copies, half, plan_q, bits, device, got_q)
    moves = {}
    early = []
    for k in range(2):
        early.append(copies.local(work_hbm.at[k], work.at[k]))
    loads = {
        name: copies.local(src, dst)
        for name, src, dst in (
            ("w", w_hbm, w_ref), ("dk", dk_hbm, dk_ref), ("dv", dv_hbm, dv_ref),
            ("tok", tok_hbm, tok_ref), ("dq", dq_hbm, dq_ref), ("pre", pre_ref, total_ref),
        )
    }
    loaded = set()

    def need(*wanted):
        for name in wanted:
            if name not in loaded:
                loads[name].wait()
                loaded.add(name)

    greet([sibling] + list(others.values()))
    mine = pl.multiple_of(core * half, half)
    theirs = pl.multiple_of((1 - core) * half, half)

    def lane(k):
        return (rings, k) if k < 2 else (rings_q, 0)

    def reduce_send(k, p, s):
        ring, slot = lane(k)
        moves[k, p, s] = copies.send(
            ring.part(work.at[k], ring.fixed(p, s, True), p),
            ring.got[p * 4 + s].at[slot],
            others[ring.names[p][s]],
        )

    def reduce_step(k, p, s):
        ring, slot = lane(k)
        if (k, p, s - 1) in moves:
            moves[k, p, s - 1].wait_recv()
        add_rows(ring.part(work.at[k], ring.fixed(p, s - 1), p), ring.got[p * 4 + s - 1].at[slot])
        if s < 4:
            reduce_send(k, p, s)

    def spread_start(k, p):
        reduce_step(k, p, 4)
        ring = lane(k)[0]
        src = ring.part(work.at[k], ring.fixed(p, 3), p)
        dst = ring.part(out_ref.at[k], ring.fixed(p, 3), p, mine)
        moves[k, p, "own"] = copies.local(src, dst)
        moves[k, p, 3] = copies.send(src, dst, others["far"])

    def spread_step(k, p, s):
        moves[k, p, s + 1].wait_recv()
        if s == 2:
            moves[k, p, "own"].wait()
        moves[k, p, s] = lane(k)[0].spread(out_ref.at[k], p, s, mine)

    def spread_cores(k, p):
        moves[k, p, 0].wait_recv()
        place = out_ref.at[k, :, :, pl.ds(mine, half), lane(k)[0].columns[p]]
        moves[k, p, "end"] = copies.send(place, place, sibling)

    small_partners = [sibling] + [others[name] for name in ("x", "y", "near", "far")]

    def small_step(s):
        moves["small"] = copies.send(
            sum_ref if s else small_ref, small_in.at[s], small_partners[s], False
        )

    def small_add(s):
        moves["small"].wait()
        sum_ref[...] = (sum_ref if s else small_ref)[...] + small_in[s]
        if s < 4:
            small_step(s + 1)

    def token_part(py, pc):
        need("w", "dk", "dv")
        at = pl.ds(pl.multiple_of((py * 2 + pc) * rows, rows), rows)
        return dot(dk_ref[at, :], w_ref[:, feat : 2 * feat], NT) + dot(
            dv_ref[at, :], w_ref[:, 2 * feat : 3 * feat], NT
        )

    def weights(n, at, columns):
        if n == 0:
            need("tok", "dq")
            own_tokens = pl.ds(pl.multiple_of(seq * rows, rows), rows)
            value = dot(tok_ref[at, own_tokens], dq_ref[:, columns])
        else:
            need("tok", "dk" if n == 1 else "dv")
            value = dot(tok_ref[at, :], (dk_ref if n == 1 else dv_ref)[:, columns])
        return value.astype(jnp.bfloat16)

    def weights_away(p):
        columns = rings_q.columns[p]
        for n in range(3):
            slabs[n, :, columns] = weights(n, pl.ds(theirs, half), columns)
        moves["q", p] = copies.send(slabs.at[:, :, columns], got0.at[0:3, :, columns], sibling)

    def weights_here(p):
        columns = rings_q.columns[p]
        for n in range(3):
            work[2, n // 2, n % 2, :, columns] = weights(n, pl.ds(mine, half), columns)
        if "out" in moves:
            out_here.wait()
            moves.pop("out").wait_recv()
        moves["q", p].wait_recv()
        for n in range(4):
            add_rows(work.at[2, n // 2, n % 2, :, columns], got0.at[n, :, columns])
        reduce_send(2, p, 0)

    def tokens_far():
        part[0] = token_part(1 - y, 1 - core).astype(jnp.bfloat16)
        moves["far"] = copies.send(part.at[0], part_in.at[0], sibling)

    def tokens_near():
        part[1] = token_part(y, 1 - core).astype(jnp.bfloat16)
        moves["near"] = copies.send(part.at[1], part_in.at[1], sibling)

    def tokens_cross():
        part[2] = token_part(1 - y, core).astype(jnp.bfloat16)
        moves["far"].wait_recv()
        add_rows(part.at[2], part_in.at[0])
        moves["cross"] = copies.send(part.at[2], part_in.at[2], others["y"])

    def tokens_own():
        need("w", "pre", "dq")
        total_ref[...] = (
            total_ref[...] + dot(dq_ref[...], w_ref[:, 0:feat], NT) + token_part(y, core)
        )

    def tokens_end():
        moves["near"].wait_recv()
        moves["cross"].wait_recv()
        gtok_ref[...] = (
            total_ref[...] + part_in[1].astype(jnp.float32) + part_in[2].astype(jnp.float32)
        ).astype(jnp.bfloat16)

    moves["out"] = copies.send(w_out_ref.at[pl.ds(theirs, half), :], got0.at[3], sibling)
    out_here = copies.local(w_out_ref.at[pl.ds(mine, half), :], work.at[2, 1, 1])
    small_step(0)
    for k in range(2):
        early[k].wait()
        for p in range(len(plan)):
            reduce_step(k, p, 1)
    steps = {
        "add": reduce_step, "top": spread_start, "out": spread_step, "end": spread_cores,
        "small": small_add, "wa": weights_away, "wh": weights_here, "far": tokens_far,
        "near": tokens_near, "cross": tokens_cross, "own": tokens_own, "last": tokens_end,
    }
    for name, *values in order:
        steps[name](*values)
    for k in range(3):
        for p in range(len(lane(k)[0].names)):
            moves[k, p, "end"].wait_recv()
    copies.finish()


PLAN = (
    (("near", "x", "y", "far"), 0, 256),
    (("y", "near", "x", "far"), 256, 512),
    (("x", "y", "near", "far"), 512, 768),
)
PLAN_Q = (
    (("near", "x", "y", "far"), 0, 256),
    (("x", "near", "y", "far"), 256, 512),
    (("near", "y", "x", "far"), 512, 640),
    (("y", "x", "near", "far"), 640, 768),
)
ORDER = (
    ("far",), ("small", 0), ("wa", 0), ("add", 0, 0, 2), ("add", 0, 1, 2), ("add", 0, 2, 2),
    ("wh", 0), ("add", 1, 0, 2), ("add", 1, 1, 2), ("small", 1), ("cross",), ("add", 1, 2, 2),
    ("wa", 1), ("add", 0, 0, 3), ("add", 0, 1, 3), ("add", 0, 2, 3), ("small", 2), ("wh", 1),
    ("add", 2, 0, 1), ("add", 1, 0, 3), ("add", 1, 1, 3), ("add", 1, 2, 3), ("wa", 2),
    ("top", 0, 0), ("wh", 2), ("top", 0, 1), ("top", 0, 2), ("small", 3), ("wa", 3),
    ("top", 1, 0), ("wh", 3), ("add", 2, 1, 1), ("top", 1, 1), ("top", 1, 2), ("near",),
    ("add", 2, 0, 2), ("add", 2, 2, 1), ("out", 0, 1, 2), ("own",), ("add", 2, 1, 2),
    ("out", 0, 2, 2), ("out", 0, 1, 1), ("small", 4), ("last",), ("out", 0, 0, 2),
    ("add", 2, 3, 1), ("out", 1, 1, 2), ("out", 1, 0, 2), ("add", 2, 0, 3), ("out", 1, 2, 2),
    ("out", 0, 2, 1), ("add", 2, 2, 2), ("add", 2, 3, 2), ("add", 2, 1, 3), ("out", 0, 1, 0),
    ("out", 1, 1, 1), ("out", 0, 0, 1), ("add", 2, 2, 3), ("top", 2, 0), ("out", 1, 0, 1),
    ("add", 2, 3, 3), ("top", 2, 1), ("out", 0, 2, 0), ("out", 1, 2, 1), ("out", 0, 0, 0),
    ("top", 2, 2), ("out", 2, 0, 2), ("top", 2, 3), ("out", 2, 1, 2), ("out", 1, 0, 0),
    ("end", 0, 1), ("out", 1, 1, 0), ("out", 1, 2, 0), ("end", 0, 2), ("end", 0, 0),
    ("out", 2, 0, 1), ("out", 2, 2, 2), ("out", 2, 3, 2), ("out", 2, 1, 1), ("end", 1, 0),
    ("end", 1, 2), ("out", 2, 3, 1), ("end", 1, 1), ("out", 2, 0, 0), ("out", 2, 1, 0),
    ("out", 2, 2, 1), ("out", 2, 3, 0), ("out", 2, 2, 0), ("end", 2, 3), ("end", 2, 0),
    ("end", 2, 1), ("end", 2, 2),
)


def finish(work, early, w_out_grad, small, dq, dk, dv, flipped_tokens, w_qkv, grad_pre1):
    rows, feat = dq.shape
    half = rows // 2
    low = jnp.bfloat16
    vmem = pl.BlockSpec(memory_space=pltpu.VMEM)
    anywhere = pl.BlockSpec(memory_space=pl.ANY)
    return pl.pallas_call(
        functools.partial(finish_kernel, PLAN, PLAN_Q, ORDER),
        out_shape=(
            jax.ShapeDtypeStruct((3, 2, 2, rows, feat), low),
            jax.ShapeDtypeStruct((rows, feat), low),
            jax.ShapeDtypeStruct(small.shape, jnp.float32),
        ),
        in_specs=[anywhere] + [vmem] * len(PLAN) + [anywhere, vmem] + [anywhere] * 6,
        out_specs=(anywhere, vmem, vmem),
        scratch_shapes=[
            pltpu.VMEM((3, 2, 2, half, feat), low),
            pltpu.VMEM((4, half, feat), low),
        ]
        + [pltpu.VMEM((2,) + shape, low) for shape in step_shapes(half, PLAN, 1)]
        + [pltpu.VMEM((1,) + shape, low) for shape in step_shapes(half, PLAN_Q)]
        + [
            pltpu.VMEM((3, half, feat), low),
            pltpu.VMEM((3, rows, feat), low),
            pltpu.VMEM((3, rows, feat), low),
            pltpu.VMEM((rows, feat), jnp.float32),
            pltpu.VMEM((5,) + small.shape, jnp.float32),
            pltpu.VMEM(dq.shape, low),
            pltpu.VMEM(dk.shape, low),
            pltpu.VMEM(dv.shape, low),
            pltpu.VMEM(flipped_tokens.shape, low),
            pltpu.VMEM(w_qkv.shape, low),
            pltpu.SemaphoreType.DMA((128,)),
            pltpu.SemaphoreType.DMA((128,)),
            pltpu.SemaphoreType.DMA((32,)),
        ],
        compiler_params=pltpu.CompilerParams(
            collective_id=0, has_side_effects=True, vmem_limit_bytes=60 * 2**20
        ),
        name="finish",
    )(work, *early, w_out_grad, small, dq, dk, dv, flipped_tokens, w_qkv, grad_pre1)


def widen_kernel(
    in_ref, back_ref, last_ref, sum_ref, one_ref, two_ref,
    in_out, back_out, qkv_out, out_out, one_out, two_out, bias_out, *vec_outs,
):
    in_out[...] = in_ref[0, 0, 0].astype(jnp.float32)
    back_out[...] = back_ref[0, 0, 0].astype(jnp.float32)
    one_out[...] = one_ref[...]
    two_out[...] = two_ref[...]
    last = last_ref[0, 0, 0].astype(jnp.float32)
    feat = sum_ref.shape[1]

    @pl.when(pl.program_id(0) < 3)
    def _():
        qkv_out[...] = last

    @pl.when(pl.program_id(0) == 3)
    def _():
        out_out[...] = last
        for i, vec_out in enumerate(vec_outs):
            vec_out[...] = sum_ref[i]
        for i in range(4):
            bias_out[pl.ds(i * feat, feat)] = sum_ref[6 + i]


def widen(grads, sums, layer_out, grad_tokens):
    rows, feat = grads.shape[-2:]
    wide = jnp.float32
    quarter = rows // 4

    def source(k):
        return pl.BlockSpec((1, 1, 1, rows, feat), lambda n: (k, n // 2, n % 2, 0, 0))

    part = pl.BlockSpec((quarter, feat), lambda n: (n, 0))
    vector = jax.ShapeDtypeStruct((feat,), wide)
    return pl.pallas_call(
        widen_kernel,
        grid=(4,),
        out_shape=[
            jax.ShapeDtypeStruct((rows, 4 * feat), wide),
            jax.ShapeDtypeStruct((4 * rows, feat), wide),
            jax.ShapeDtypeStruct((rows, 3 * feat), wide),
            jax.ShapeDtypeStruct((rows, feat), wide),
            jax.ShapeDtypeStruct((rows, feat), layer_out.dtype),
            jax.ShapeDtypeStruct((rows, feat), layer_out.dtype),
            jax.ShapeDtypeStruct((4 * feat,), wide),
        ]
        + [vector] * 6,
        in_specs=[source(k) for k in range(3)]
        + [pl.BlockSpec(sums.shape, lambda n: (0, 0)), part, part],
        out_specs=[
            pl.BlockSpec((rows, feat), lambda n: (0, n)),
            pl.BlockSpec((rows, feat), lambda n: (n, 0)),
            pl.BlockSpec((rows, feat), lambda n: (0, jnp.minimum(n, 2))),
            pl.BlockSpec((rows, feat), lambda n: (0, 0)),
            part,
            part,
            pl.BlockSpec((4 * feat,), lambda n: (0,)),
        ]
        + [pl.BlockSpec((feat,), lambda n: (0,))] * 6,
        compiler_params=pltpu.CompilerParams(vmem_limit_bytes=56 * 2**20),
        name="widen",
    )(grads, grads, grads, sums, layer_out, grad_tokens)


PIECES = 6


def front_kernel(
    tok_hbm, w_hbm, q_ref, kv_out, flip_out, all_ref, kv_ref, flip_ref, w_ref, send_sem, recv_sem, local_sem
):
    core, x, y, near, far, device = grid_place()
    sibling, over_y = device(core=1 - core), device(y=1 - y)
    low = jnp.bfloat16
    rows, feat = q_ref.shape
    piece = rows // PIECES
    copies = Copies(send_sem, recv_sem, local_sem)

    def rows_of(py, pc, i=None):
        start = (py * 2 + pc) * rows
        if i is None:
            return pl.ds(pl.multiple_of(start, rows), rows)
        return pl.ds(pl.multiple_of(start + i * piece, piece), piece)

    own = rows_of(y, core)
    load = copies.local(tok_hbm, all_ref.at[own])
    load_w = copies.local(w_hbm, w_ref)
    greet([sibling, over_y])
    crossing = []
    for i in range(PIECES):
        src = tok_hbm.at[pl.ds(i * piece, piece)]
        crossing.append(copies.send(src, all_ref.at[rows_of(y, core, i)], over_y))
    beside = copies.send(tok_hbm, all_ref.at[own], sibling)
    stores = []

    def project(at):
        kv_ref[at, :] = dot(all_ref[at, :], w_ref[:, feat:]).astype(low)
        stores.append(copies.local(kv_ref.at[at], kv_out.at[at]))
        flip_ref[:, at] = all_ref[at, :].T
        stores.append(copies.local(flip_ref.at[:, at], flip_out.at[:, at]))

    load.wait()
    load_w.wait()
    project(own)
    q_ref[...] = dot(all_ref[own, :], w_ref[:, 0:feat]).astype(low) * low(HEAD ** (-0.5))
    beside.wait_recv()
    project(rows_of(y, 1 - core))
    passed = []
    for i in range(PIECES):
        crossing[i].wait_recv()
        at = rows_of(1 - y, core, i)
        passed.append(copies.send(all_ref.at[at], all_ref.at[at], sibling))
        project(at)
        if i > 0:
            passed[i - 1].wait_recv()
            project(rows_of(1 - y, 1 - core, i - 1))
    passed[-1].wait_recv()
    project(rows_of(1 - y, 1 - core, PIECES - 1))
    for store in stores:
        store.wait()
    copies.finish()


def front(tokens, w_qkv, seq_parts):
    rows, feat = tokens.shape
    low = jnp.bfloat16
    keys = rows * seq_parts
    anywhere = pl.BlockSpec(memory_space=pl.ANY)
    count = 2 + 2 * PIECES
    return pl.pallas_call(
        front_kernel,
        out_shape=(
            jax.ShapeDtypeStruct((rows, feat), low),
            jax.ShapeDtypeStruct((keys, 2 * feat), low),
            jax.ShapeDtypeStruct((feat, keys), low),
        ),
        in_specs=[anywhere, anywhere],
        out_specs=(pl.BlockSpec(memory_space=pltpu.VMEM), anywhere, anywhere),
        scratch_shapes=[
            pltpu.VMEM((keys, feat), low),
            pltpu.VMEM((keys, 2 * feat), low),
            pltpu.VMEM((feat, keys), low),
            pltpu.VMEM(w_qkv.shape, low),
            pltpu.SemaphoreType.DMA((count,)),
            pltpu.SemaphoreType.DMA((count,)),
            pltpu.SemaphoreType.DMA((2 + 2 * count,)),
        ],
        compiler_params=pltpu.CompilerParams(
            collective_id=2, has_side_effects=True, vmem_limit_bytes=56 * 2**20
        ),
        name="front",
    )(tokens, w_qkv)


def gelu_parts(v):
    size = jnp.abs(v)
    fall = jnp.exp(-0.5 * v * v)
    t = 1.0 / (1.0 + (0.3275911 * 0.7071067811865476) * size)
    tail = 1.061405429 * t - 1.453152027
    tail = tail * t + 1.421413741
    tail = tail * t - 0.284496736
    tail = tail * t + 0.254829592
    half = 0.5 * tail * t * fall
    return jnp.where(v >= 0.0, 1.0 - half, half), fall


def row_mean(values):
    return jnp.sum(values, axis=-1, keepdims=True) * (1.0 / values.shape[-1])


def fold8(values):
    total = values[0:8]
    for i in range(1, values.shape[0] // 8):
        total = total + values[i * 8 : (i + 1) * 8]
    return total


STEP = 256
TILE = 64


def middle_kernel(
    plan, mixed_ref, tok_ref, cot_ref, *refs,
):
    vec_refs, bias_ref, refs = refs[:6], refs[6], refs[7:]
    (w_out_ref, w_in_hbm, w_back_hbm,
     out_ref, pre_ref, gmix_ref, gw_out_ref, small_ref, work_out, *refs) = refs
    away, refs = refs[: len(plan)], refs[len(plan) :]
    (w_in_ref, w_back_ref, unit, spread, hid, active, slope, acc, acc2, gsecond, gbranch,
     work, slabs, got0, send_sem, recv_sem, local_sem) = refs
    core, x, y, near, far, device = grid_place()
    sibling = device(core=1 - core)
    low = jnp.bfloat16
    rows, feat = tok_ref.shape
    half = rows // 2
    count = 4
    chunks = rows // STEP
    copies = Copies(send_sem, recv_sem, local_sem)
    load_in = copies.local(w_in_hbm, w_in_ref)
    load_back = copies.local(w_back_hbm, w_back_ref)
    greet([sibling])
    mine = pl.multiple_of(core * half, half)
    theirs = pl.multiple_of((1 - core) * half, half)

    def rows_at(i):
        return pl.ds(pl.multiple_of(i * STEP, STEP), STEP)

    def slab_at(n):
        return pl.ds(pl.multiple_of(n * feat, feat), feat)

    def vec(i):
        return vec_refs[i][...].reshape(1, feat)

    zero = jnp.zeros((8, feat), jnp.float32)

    def put(i, value):
        small_ref[i : i + 1, :] = jnp.sum(value, axis=0, keepdims=True)

    small_ref[...] = jnp.zeros_like(small_ref)

    acc[...] = dot(mixed_ref[...], w_out_ref[...])

    def norm_one(i, carry):
        at = rows_at(i)
        v = tok_ref[at, :].astype(jnp.float32) + (acc[at, :] + vec(0))
        v = v - row_mean(v)
        r = lax.rsqrt(row_mean(v * v) + NORM_EPS)
        u = v * r
        unit[at, :] = u
        spread[at, :] = jnp.broadcast_to(r, (STEP, 128))
        hid[at, :] = (u * vec(1) + vec(2)).astype(low)
        return carry

    lax.fori_loop(0, chunks, norm_one, 0)
    load_in.wait()

    group = rows // 6

    def inner_of(n, i):
        return dot(hid[i * group : (i + 1) * group, :], w_in_ref[:, n * feat : (n + 1) * feat])

    inner = [inner_of(0, i) for i in range(6)]
    load_back.wait()
    for n in range(count):
        bias = bias_ref[n * feat : (n + 1) * feat].reshape(1, feat)
        following = []
        for i in range(6):
            if n + 1 < count:
                following.append(inner_of(n + 1, i))
            for j in range(group // TILE):
                at = slice(i * group + j * TILE, i * group + (j + 1) * TILE)
                v = inner[i][j * TILE : (j + 1) * TILE] + bias
                chance, fall = gelu_parts(v)
                active[n, at, :] = (v * chance).astype(low)
                slope[n, at, :] = (chance + (v * 0.3989422804014327) * fall).astype(low)
            at = slice(i * group, (i + 1) * group)
            second = dot(active[n, at, :], w_back_ref[n * feat : (n + 1) * feat, :])
            acc2[at, :] = second if n == 0 else acc2[at, :] + second
        inner = following

    def norm_two(i, sums):
        at = rows_at(i)
        v = (unit[at, :] * vec(1) + vec(2)) + (acc2[at, :] + vec(3))
        v = v - row_mean(v)
        r = lax.rsqrt(row_mean(v * v) + NORM_EPS)
        u = v * r
        out_ref[at, :] = (u * vec(4) + vec(5)).astype(low)
        c = cot_ref[at, :].astype(jnp.float32)
        a = c * vec(4)
        g = r * (a - row_mean(a) - u * row_mean(a * u))
        acc2[at, :] = g
        g_low = g.astype(low)
        gsecond[at, :] = g_low
        return (
            sums[0] + fold8(c * u), sums[1] + fold8(c), sums[2] + fold8(g_low.astype(jnp.float32)),
        )

    sums = lax.fori_loop(0, chunks, norm_two, (zero, zero, zero))
    put(4, sums[0])
    put(5, sums[1])
    put(3, sums[2])

    def exchange(k, n):
        return pltpu.make_async_remote_copy(
            src_ref=slabs.at[k, n],
            dst_ref=got0.at[k, n],
            send_sem=send_sem.at[k * 4 + n],
            recv_sem=recv_sem.at[k * 4 + n],
            device_id=sibling,
            device_id_type=pl.DeviceIdType.MESH,
        )

    def collect(k, n):
        exchange(k, n).wait_recv()
        add_rows(work.at[k, lax.div(n, 2), lax.rem(n, 2)], got0.at[k, n], 128)
        exchange(k, n).wait_send()

    def back_slab(n, carry):
        columns = slab_at(n)
        slabs[1, n] = dot(active[n, :, pl.ds(theirs, half)], gsecond[...], TN).astype(low)
        exchange(1, n).start()
        work[1, lax.div(n, 2), lax.rem(n, 2)] = dot(active[n, :, pl.ds(mine, half)], gsecond[...], TN).astype(low)
        gactive = dot(gsecond[...], w_back_ref[columns, :], NT)
        total = zero
        for i in range(rows // TILE):
            at = slice(i * TILE, (i + 1) * TILE)
            g = (gactive[at] * slope[n, at, :].astype(jnp.float32)).astype(low)
            slope[n, at, :] = g
            total = total + fold8(g.astype(jnp.float32))

        small_ref[pl.ds(6 + n, 1), :] = jnp.sum(total, axis=0, keepdims=True)
        slabs[0, n] = dot(hid[:, pl.ds(theirs, half)], slope[n], TN).astype(low)
        exchange(0, n).start()

        @pl.when(n > 0)
        def _():
            collect(1, n - 1)
            collect(0, n - 1)

        work[0, lax.div(n, 2), lax.rem(n, 2)] = dot(hid[:, pl.ds(mine, half)], slope[n], TN).astype(low)

        acc2[...] += dot(slope[n], w_in_ref[:, columns], NT)
        return carry

    lax.fori_loop(0, count, back_slab, 0)

    def norm_back(i, sums):
        at = rows_at(i)
        g = acc2[at, :]
        u = unit[at, :]
        r = spread[at, 0:1]
        a = g * vec(1)
        d = r * (a - row_mean(a) - u * row_mean(a * u))
        pre_ref[at, :] = d
        d_low = d.astype(low)
        gbranch[at, :] = d_low
        return (
            sums[0] + fold8(g * u), sums[1] + fold8(g), sums[2] + fold8(d_low.astype(jnp.float32)),
        )

    sums = lax.fori_loop(0, chunks, norm_back, (zero, zero, zero))
    put(1, sums[0])
    put(2, sums[1])
    put(0, sums[2])
    gmix_ref[...] = dot(gbranch[...], w_out_ref[...], NT).astype(low)
    gw_out_ref[...] = dot(mixed_ref[...], gbranch[...], TN).astype(low)

    collect(1, count - 1)
    collect(0, count - 1)
    stores = [copies.local(work, work_out)]
    bits = {"x": x, "y": y, "near": near, "far": far}
    rings = Rings(copies, half, plan, bits, device, None)
    for k in range(2):
        for p in range(len(plan)):
            stores.append(
                copies.local(rings.part(work.at[k], rings.fixed(p, 0, True), p), away[p].at[k])
            )
    for store in stores:
        store.wait()


def middle(mixed, tokens, cotangent, vectors, b_in, w_out, w_in, w_back):
    rows, feat = tokens.shape
    half = rows // 2
    low = jnp.bfloat16
    wide = jnp.float32
    vmem = pl.BlockSpec(memory_space=pltpu.VMEM)
    anywhere = pl.BlockSpec(memory_space=pl.ANY)
    full = jax.ShapeDtypeStruct((rows, feat), low)
    return pl.pallas_call(
        functools.partial(middle_kernel, PLAN),
        out_shape=(
            full,
            jax.ShapeDtypeStruct((rows, feat), wide),
            full,
            full,
            jax.ShapeDtypeStruct((16, feat), wide),
            jax.ShapeDtypeStruct((2, 2, 2, half, feat), low),
        )
        + tuple(jax.ShapeDtypeStruct((2,) + shape, low) for shape in step_shapes(half, PLAN, 0, 1)),
        in_specs=[vmem] * 11 + [anywhere] * 2,
        out_specs=(vmem,) * 5 + (anywhere,) * (1 + len(PLAN)),
        scratch_shapes=[
            pltpu.VMEM(w_in.shape, low),
            pltpu.VMEM(w_back.shape, low),
            pltpu.VMEM((rows, feat), wide),
            pltpu.VMEM((rows, 128), wide),
            pltpu.VMEM((rows, feat), low),
            pltpu.VMEM((4, rows, feat), low),
            pltpu.VMEM((4, rows, feat), low),
            pltpu.VMEM((rows, feat), wide),
            pltpu.VMEM((rows, feat), wide),
            pltpu.VMEM((rows, feat), low),
            pltpu.VMEM((rows, feat), low),
            pltpu.VMEM((2, 2, 2, half, feat), low),
            pltpu.VMEM((2, 4, half, feat), low),
            pltpu.VMEM((2, 4, half, feat), low),
            pltpu.SemaphoreType.DMA((8,)),
            pltpu.SemaphoreType.DMA((8,)),
            pltpu.SemaphoreType.DMA((16,)),
        ],
        compiler_params=pltpu.CompilerParams(
            collective_id=1, has_side_effects=True, vmem_limit_bytes=60 * 2**20
        ),
        name="middle",
    )(mixed, tokens, cotangent, *vectors, b_in, w_out, w_in, w_back)


FLIPS = {"x": (1, 0), "y": (0, 2), "near": (2, 0)}


def trade(value, name):
    parts = lax.axis_size("seq")
    flip_b, flip_s = FLIPS[name]
    pairs = [
        (b * parts + s, (b ^ flip_b) * parts + (s ^ flip_s))
        for b in range(lax.axis_size("batch"))
        for s in range(parts)
    ]
    return lax.ppermute(value, ("batch", "seq"), pairs)


def per_device(
    tokens,
    group_bucket,
    lengths,
    random_blocks,
    w_qkv,
    w_out,
    b_out,
    norm1_gain,
    norm1_shift,
    w_in,
    b_in,
    w_back,
    b_back,
    norm2_gain,
    norm2_shift,
    cotangent,
):
    low = jnp.bfloat16
    seq_parts = lax.axis_size("seq")
    tok_rows, feat = tokens.shape
    layout = (group_bucket, lengths, random_blocks)
    queries, kv, flipped_tokens = front(tokens, w_qkv, seq_parts)
    mixed, logs = attend(layout, queries, kv)
    vectors = (b_out, norm1_gain, norm1_shift, b_back, norm2_gain, norm2_shift)
    layer_out, grad_pre1, grad_mixed, grad_w_out, small, work, *away = middle(
        mixed, tokens, cotangent, vectors, b_in, w_out, w_in, w_back
    )
    early = [trade(value, names[0]) for value, (names, _, _) in zip(away, PLAN)]
    dq, dk, dv = attend_back(layout, queries, kv, grad_mixed, logs)
    grads, grad_tokens, sums = finish(
        work,
        early,
        grad_w_out,
        small,
        dq,
        dk,
        dv,
        flipped_tokens,
        w_qkv,
        grad_pre1,
    )
    wide = jnp.float32
    outer = lax.axis_size("batch") // BLOCK8
    if outer > 1:
        groups = [[o * BLOCK8 + i for o in range(outer)] for i in range(BLOCK8)]
        grads = lax.psum(grads.astype(wide), "batch", axis_index_groups=groups)
        sums = lax.psum(sums, "batch", axis_index_groups=groups)
    if outer > 1:
        grads = grads.astype(low)
    full_in, full_back, full_qkv, full_out, layer_out, grad_tokens, grad_b_in, *vectors = widen(
        grads, sums, layer_out, grad_tokens
    )
    return (
        layer_out,
        grad_tokens,
        full_qkv,
        full_out,
        *vectors[0:3],
        full_in,
        grad_b_in,
        full_back,
        *vectors[3:6],
    )


def solution(mesh):
    rows = P(("batch", "seq"), None)
    whole = P()
    placed = (rows, P("batch"), P("batch", None), P("batch", None, None)) + (whole,) * 11 + (rows,)
    return jax.shard_map(
        per_device,
        mesh=mesh,
        in_specs=placed,
        out_specs=(rows, rows) + (whole,) * 11,
        check_vma=False,
    )
```
